32 devices in a mesh: fsdp: 4 (over z), head: 4 (over y, x), tensor: 2 (over core).
Axes of the slice: x: 2, y: 2, z: 4, core: 2. Of those that a mesh axis runs over, the one named last changes fastest.
Arguments:
- tokens: bfloat16 [8192, 2048], P(('fsdp', 'head', 'tensor')), may hold values from -6 to 6
- lengths: int32 [4, 2], P('fsdp'), may hold values from 0 to 2048, as said below
- attention_gain: float32 [2048], replicated, may hold values from 0.5 to 1.5
- query_weight: bfloat16 [2048, 8, 2, 128], P('fsdp', 'head', 'tensor'), may hold values from -0.1875 to 0.1875
- key_weight: bfloat16 [2048, 8, 2, 128], P('fsdp', 'head', 'tensor'), may hold values from -0.1875 to 0.1875
- value_weight: bfloat16 [2048, 8, 256], P('fsdp', 'head', 'tensor'), may hold values from -0.125 to 0.125
- output_weight: bfloat16 [8, 256, 2048], P('head', 'tensor', 'fsdp'), may hold values from -0.125 to 0.125
- lambda_vectors: float32 [8, 4, 128], replicated, may hold values from -0.9 to 0.9
- head_gain: float32 [8, 256], replicated, may hold values from 0.5 to 1.5
- feedforward_gain: float32 [2048], replicated, may hold values from 0.5 to 1.5
- gate_weight: bfloat16 [2048, 5632], P('fsdp', ('head', 'tensor')), may hold values from -0.125 to 0.125
- up_weight: bfloat16 [2048, 5632], P('fsdp', ('head', 'tensor')), may hold values from -0.125 to 0.125
- down_weight: bfloat16 [5632, 2048], P(('head', 'tensor'), 'fsdp'), may hold values from -0.078125 to 0.078125
- cotangent: bfloat16 [8192, 2048], P(('fsdp', 'head', 'tensor')), may hold values from -6 to 6
Outputs:
- block_output: bfloat16 [8192, 2048], P(('fsdp', 'head', 'tensor'))
- tokens_grad: float32 [8192, 2048], P(('fsdp', 'head', 'tensor'))
- attention_gain_grad: float32 [2048], replicated
- query_weight_grad: float32 [2048, 8, 2, 128], P('fsdp', 'head', 'tensor')
- key_weight_grad: float32 [2048, 8, 2, 128], P('fsdp', 'head', 'tensor')
- value_weight_grad: float32 [2048, 8, 256], P('fsdp', 'head', 'tensor')
- output_weight_grad: float32 [8, 256, 2048], P('head', 'tensor', 'fsdp')
- lambda_vectors_grad: float32 [8, 4, 128], replicated
- head_gain_grad: float32 [8, 256], replicated
- feedforward_gain_grad: float32 [2048], replicated
- gate_weight_grad: float32 [2048, 5632], P('fsdp', ('head', 'tensor'))
- up_weight_grad: float32 [2048, 5632], P('fsdp', ('head', 'tensor'))
- down_weight_grad: float32 [5632, 2048], P(('head', 'tensor'), 'fsdp')
The draws below stay inside these ranges and needn't reach their ends.
Inputs may be any that keep to these rules, and one draw needn't show every extreme that they name: Each row of 2048 slots holds one or two sequences packed from its start, given by its two lengths in order (the second 0 where there is one); every sequence has 512 tokens or more, together they take 5 * 256 slots or more of the row, and the slots after them are padding; some row holds a single sequence of 2048 tokens.
All inputs are finite; a program needn't handle non-finite values.
Results may differ from the reference program's by a relative error of at most 0.019.
Values may be sent and summed in bfloat16 or wider, within the bound.
No kernel may reach another device: no remote copies, remote signals or barrier semaphores. Data moves between devices by JAX's collectives and lax.ppermute only.
A program may use at most 320 MiB of HBM per device.

```python
import jax
import jax.numpy as jnp
from jax import lax

D = 2048
H = 8
E = 128
V = 256
FF = 5632
SLOTS = 2048
SEQ_MIN = 512
ROWS = 4
TOKENS = 8192


def draw_lengths(key, part):
    total_key, split_key, choice_key, full_key = jax.random.split(key, 4)
    row_index = jnp.arange(ROWS, dtype=jnp.int32)
    totals = jax.random.randint(total_key, (ROWS,), SLOTS * 5 // 8, SLOTS + 1)
    full_row = jax.random.randint(full_key, (), 0, ROWS)
    totals = jnp.where(row_index == full_row, SLOTS, totals)
    wanted = jax.random.randint(choice_key, (ROWS,), 0, 2)
    upper = jnp.maximum(totals - SEQ_MIN + 1, SEQ_MIN + 1)
    first_try = jax.random.randint(split_key, (ROWS,), SEQ_MIN, upper)
    splitting = (wanted == 1) & (totals >= 2 * SEQ_MIN) & (row_index != full_row)
    first_length = jnp.where(splitting, first_try, totals)
    second_length = jnp.where(splitting, totals - first_try, 0)
    return jnp.stack([first_length, second_length], axis=1).astype(jnp.int32)


def block_scale(own_key, dims, pieces, least, top_value):
    def one(axis_at, blocks):
        steps = jax.random.uniform(jax.random.fold_in(jax.random.fold_in(own_key, 6), axis_at), (blocks,), jnp.float32, least / len(pieces), top_value / len(pieces))
        return jnp.repeat(jnp.exp(steps), dims[axis_at] // blocks).reshape((-1,) + (1,) * (len(dims) - axis_at - 1))

    factor_of = one(*pieces[0])
    for cut in pieces[1:]:
        factor_of = factor_of * one(*cut)
    return factor_of


def noise(key, shape, spread, limit, shards=(), held_as=jnp.bfloat16):
    level = block_scale(key, shape, shards, -0.22, 0.18) if shards else 1.0
    drawn = jax.random.normal(key, shape, jnp.float32) * spread * level
    return jnp.minimum(jnp.maximum(drawn, -limit), limit).astype(held_as)


def setup_inputs(seed: int = 0) -> dict:
    keys = jax.random.split(jax.random.key(seed), 15)
    return {
        "tokens": noise(keys[0], (TOKENS, D), 1.0, 6.0, ((0, 32),)),
        "lengths": draw_lengths(jax.random.fold_in(keys[14], 71), 0),
        "attention_gain": jnp.clip(1.0 + 0.1 * jax.random.normal(keys[2], (D,), jnp.float32), 0.5, 1.5),
        "query_weight": noise(keys[3], (D, H, 2, E), (D // 2) ** -0.5, 0.1875, ((0, 4), (1, 4), (2, 2))),
        "key_weight": noise(keys[4], (D, H, 2, E), (D // 2) ** -0.5, 0.1875, ((0, 4), (1, 4), (2, 2))),
        "value_weight": noise(keys[5], (D, H, V), D ** -0.5, 0.125, ((0, 4), (1, 4), (2, 2))),
        "output_weight": noise(keys[6], (H, V, D), (H * V) ** -0.5, 0.125, ((0, 4), (1, 2), (2, 4))),
        "lambda_vectors": noise(keys[7], (H, 4, E), 0.15, 0.9, (), jnp.float32),
        "head_gain": jnp.clip(1.0 + 0.1 * jax.random.normal(keys[8], (H, V), jnp.float32), 0.5, 1.5),
        "feedforward_gain": jnp.clip(1.0 + 0.1 * jax.random.normal(keys[9], (D,), jnp.float32), 0.5, 1.5),
        "gate_weight": noise(keys[10], (D, FF), D ** -0.5, 0.125, ((0, 4), (1, 8))),
        "up_weight": noise(keys[11], (D, FF), D ** -0.5, 0.125, ((0, 4), (1, 8))),
        "down_weight": noise(keys[12], (FF, D), FF ** -0.5, 0.078125, ((0, 8), (1, 4))),
        "cotangent": noise(keys[13], (TOKENS, D), 1.0, 6.0, ((0, 32),)),
    }


@jax.custom_vjp
def low(v):
    return lax.optimization_barrier(v.astype(jnp.bfloat16)).astype(jnp.float32)

@jax.custom_vjp
def low_back(v):
    return v

def low_keep(v):
    return (low(v), None)

def low_pass(kept, grad):
    return (grad,)

def back_keep(v):
    return (v, None)

def back_low(kept, grad):
    return (low(grad),)
low.defvjp(low_keep, low_pass)
low_back.defvjp(back_keep, back_low)
lambda_base = 0.2

def product(left_side, right_side):
    return jnp.dot(left_side, right_side, precision=lax.Precision.HIGHEST)

def slot_layout(row_lengths):
    slot_index = jnp.arange(SLOTS, dtype=jnp.int32)
    first_end = row_lengths[:, 0:1]
    second_end = first_end + row_lengths[:, 1:2]
    segment = (slot_index[None, :] >= first_end).astype(jnp.int32) + (slot_index[None, :] >= second_end).astype(jnp.int32)
    starts = jnp.where(segment == 0, 0, jnp.where(segment == 1, first_end, second_end)).astype(jnp.int32)
    return (segment, slot_index[None, :] - starts)

def rope_tables(positions, qk_width):
    half_width = qk_width // 2
    frequency = 10000.0 ** (-jnp.arange(half_width, dtype=jnp.float32) / half_width)
    angles = positions.astype(jnp.float32)[:, None] * frequency[None, :]
    return (jnp.cos(angles), jnp.sin(angles))

def rotate(values, cosine_table, sine_table):
    half_width = values.shape[-1] // 2
    first_half = values[..., :half_width]
    second_half = values[..., half_width:]
    cosine_wide = cosine_table[:, None, :]
    sine_wide = sine_table[:, None, :]
    return jnp.concatenate([first_half * cosine_wide - second_half * sine_wide, second_half * cosine_wide + first_half * sine_wide], axis=-1)

def block_row(row_values, row_lengths, weights):
    attention_gain, query_weight, key_weight, value_weight, output_weight, lambda_vectors, head_gain, feedforward_gain, gate_weight, up_weight, down_weight = weights
    heads = query_weight.shape[1]
    qk_width = query_weight.shape[3]
    segment, positions = slot_layout(row_lengths[None, :])
    segment = segment[0]
    positions = positions[0]
    valid = (segment < 2).astype(jnp.float32)[:, None]
    slot_index = jnp.arange(SLOTS, dtype=jnp.int32)
    allowed = (segment[:, None] == segment[None, :]) & (slot_index[None, :] <= slot_index[:, None])
    attention_scale = lax.rsqrt(lax.optimization_barrier(jnp.mean(row_values * row_values, axis=-1, keepdims=True)) + 1e-06)
    normed = low(row_values * attention_scale * attention_gain)
    cosine_table, sine_table = rope_tables(positions, qk_width)
    query_pre = low_back(product(normed, query_weight.reshape(D, -1))).reshape(SLOTS, heads * 2, qk_width)
    queries = low(rotate(query_pre, cosine_table, sine_table) * qk_width ** (-0.5)).reshape(SLOTS, heads, 2, qk_width)
    key_pre = low_back(product(normed, key_weight.reshape(D, -1))).reshape(SLOTS, heads * 2, qk_width)
    keys_all = low(rotate(key_pre, cosine_table, sine_table)).reshape(SLOTS, heads, 2, qk_width)
    values_all = low(low_back(product(normed, value_weight.reshape(D, -1)))).reshape(SLOTS, heads, -1)
    scores = low_back(jnp.einsum('qhme,khme->hmqk', queries, keys_all, precision=lax.Precision.HIGHEST))
    masked = jnp.where(allowed[None, None], scores, -1e+30)
    probability = low(jax.nn.softmax(masked, axis=-1))
    maps_out = low_back(jnp.einsum('hmqk,khv->qhmv', probability, values_all, precision=lax.Precision.HIGHEST))
    first_dot = lax.optimization_barrier(jnp.sum(lambda_vectors[:, 0] * lambda_vectors[:, 1], axis=-1))
    second_dot = lax.optimization_barrier(jnp.sum(lambda_vectors[:, 2] * lambda_vectors[:, 3], axis=-1))
    lambda_value = jnp.exp(first_dot) - jnp.exp(second_dot) + lambda_base
    mixed = maps_out[:, :, 0] - lambda_value[None, :, None] * maps_out[:, :, 1]
    head_scale = lax.rsqrt(lax.optimization_barrier(jnp.mean(mixed * mixed, axis=-1, keepdims=True)) + 1e-05)
    head_out = low(mixed * head_scale * head_gain * (1.0 - lambda_base))
    attention_out = low_back(product(head_out.reshape(SLOTS, -1), output_weight.reshape(-1, D)))
    residual = row_values + attention_out
    ffn_scale = lax.rsqrt(lax.optimization_barrier(jnp.mean(residual * residual, axis=-1, keepdims=True)) + 1e-06)
    ffn_in = low(residual * ffn_scale * feedforward_gain)
    gate_pre = low_back(product(ffn_in, gate_weight))
    upward = low_back(product(ffn_in, up_weight))
    hidden = low(jax.nn.silu(gate_pre) * upward)
    ffn_out = low_back(product(hidden, down_weight))
    return valid * (residual + ffn_out)

def reference(tokens, lengths, attention_gain, query_weight, key_weight, value_weight, output_weight, lambda_vectors, head_gain, feedforward_gain, gate_weight, up_weight, down_weight, cotangent):
    params = tuple((weight.astype(jnp.float32) for weight in (attention_gain, query_weight, key_weight, value_weight, output_weight, lambda_vectors, head_gain, feedforward_gain, gate_weight, up_weight, down_weight)))
    rows_in = tokens.astype(jnp.float32).reshape(ROWS, SLOTS, D)

    def forward(rows_values, weights):

        def run_row(item):
            return jax.checkpoint(block_row)(item[0], item[1], weights)
        return lax.map(run_row, (rows_values, lengths))
    result, pullback = jax.vjp(forward, rows_in, params)
    rows_grad, grads = pullback(cotangent.astype(jnp.float32).reshape(ROWS, SLOTS, D))
    return (result.reshape(TOKENS, D).astype(jnp.bfloat16), rows_grad.reshape(TOKENS, D), grads[0], grads[1], grads[2], grads[3], grads[4], grads[5], grads[6], grads[7], grads[8], grads[9], grads[10])
```

```python
import jax
import jax.numpy as jnp
from jax import lax
from jax.sharding import PartitionSpec as P

lambda_base = 0.2
attention_block = 512
low = jnp.bfloat16


def contract(left_side, right_side, left_dim, right_dim):
    return lax.dot_general(
        left_side,
        right_side,
        (((left_dim,), (right_dim,)), ((), ())),
        preferred_element_type=jnp.float32,
    )


def swap(values, axis, mask):
    size = lax.axis_size(axis)
    return lax.ppermute(values, axis, [(place, place ^ mask) for place in range(size)])


def shift(values, axis, step):
    size = lax.axis_size(axis)
    return lax.ppermute(values, axis, [(place, (place + step) % size) for place in range(size)])


def fsdp_gather(own):
    size = lax.axis_size("fsdp")
    shards = [own] + [None] * (size - 1)
    up, down = own, own
    for step in range(1, size // 2 + 1):
        up = shift(up, "fsdp", 1)
        shards[size - step] = up
        if step <= size - 1 - size // 2:
            down = shift(down, "fsdp", -1)
            shards[step] = down
    return shards


def fsdp_reduce(partial):
    size = lax.axis_size("fsdp")
    up_steps = size // 2
    down_steps = size - 1 - up_steps
    total = partial[0]
    carry = partial[up_steps].astype(low)
    for left in range(up_steps - 1, -1, -1):
        carry = shift(carry, "fsdp", 1).astype(jnp.float32)
        if left:
            carry = (carry + partial[left]).astype(low)
    total = total + carry
    if down_steps:
        carry = partial[size - down_steps].astype(low)
        for left in range(down_steps - 1, -1, -1):
            carry = shift(carry, "fsdp", -1).astype(jnp.float32)
            if left:
                carry = (carry + partial[size - left]).astype(low)
        total = total + carry
    return total


def group_gather(own):
    half = own.shape[0] // 2
    first = swap(own, "head", 1)
    second = swap(own, "head", 2)
    third_low = swap(second[:half], "head", 1)
    third_high = swap(first[half:], "head", 2)
    return jnp.concatenate([own, first, second, third_low, third_high], axis=0)


def group_reduce(partial, rows):
    half = rows // 2
    own, first, second, third = (partial[place * rows : (place + 1) * rows] for place in range(4))
    to_first = swap(third[:half].astype(low), "head", 1)
    to_second = swap(third[half:].astype(low), "head", 2)
    second = jnp.concatenate(
        [second[:half] + to_first.astype(jnp.float32), second[half:]], axis=0
    ).astype(low)
    first = jnp.concatenate(
        [first[:half], first[half:] + to_second.astype(jnp.float32)], axis=0
    ).astype(low)
    from_first = swap(first, "head", 1)
    from_second = swap(second, "head", 2)
    return own + from_first.astype(jnp.float32) + from_second.astype(jnp.float32)


def total_over_all(values):
    for axis in ("tensor", "head", "fsdp"):
        mask = 1
        while mask < lax.axis_size(axis):
            values = values + swap(values, axis, mask)
            mask *= 2
    return values


def rolled(values, start):
    twice = jnp.concatenate([values, values], axis=-1)
    return lax.dynamic_slice_in_dim(twice, start, values.shape[-1], values.ndim - 1)


def slot_layout(lengths, slots):
    first_end = lengths[0, 0]
    second_end = first_end + lengths[0, 1]
    segment = (slots >= first_end).astype(jnp.int32) + (slots >= second_end).astype(jnp.int32)
    start = jnp.where(segment == 0, 0, jnp.where(segment == 1, first_end, second_end))
    return segment, slots - start


def swap_halves(values):
    half = values.shape[1] // 2
    return jnp.concatenate([values[:, half:], values[:, :half]], axis=1)


def body(
    tokens,
    lengths,
    attention_gain,
    query_weight,
    key_weight,
    value_weight,
    output_weight,
    lambda_vectors,
    head_gain,
    feedforward_gain,
    gate_weight,
    up_weight,
    down_weight,
    cotangent,
):
    rows, width = tokens.shape
    fsdp_index = lax.axis_index("fsdp")
    head_index = lax.axis_index("head")
    core = lax.axis_index("tensor")
    shard = query_weight.shape[0]
    qk_width = query_weight.shape[3]
    value_half = value_weight.shape[2]
    value_width = 2 * value_half
    slots = rows * 8
    scale = qk_width ** (-0.5)
    column_start = fsdp_index * shard

    own_slots = (
        (jnp.arange(4, dtype=jnp.int32) ^ head_index)[:, None] * (2 * rows)
        + core * rows
        + jnp.arange(rows, dtype=jnp.int32)[None, :]
    ).reshape(-1)
    segment_own, position_own = slot_layout(lengths, own_slots)
    valid = (segment_own[:rows] < 2).astype(jnp.float32)[:, None]
    half_width = qk_width // 2
    frequency = 10000.0 ** (-jnp.arange(half_width, dtype=jnp.float32) / half_width)
    angles = position_own.astype(jnp.float32)[:, None] * frequency[None, :]
    cosine = jnp.cos(angles)
    sine = jnp.sin(angles)
    cosine = jnp.concatenate([cosine, cosine], axis=1)
    sine = jnp.concatenate([-sine, sine], axis=1)

    own_head = head_index * 2 + core
    vectors = lax.dynamic_slice_in_dim(lambda_vectors, own_head, 1, 0)[0]
    first_exp = jnp.exp(jnp.sum(vectors[0] * vectors[1]))
    second_exp = jnp.exp(jnp.sum(vectors[2] * vectors[3]))
    lambda_value = first_exp - second_exp + lambda_base
    own_coefficient = jnp.where(core == 0, 1.0, -lambda_value)
    other_coefficient = jnp.where(core == 0, -lambda_value, 1.0)
    gain_own = rolled(
        lax.dynamic_slice_in_dim(head_gain, own_head, 1, 0), core * value_half
    ) * (1.0 - lambda_base)

    tokens_wide = rolled(tokens, column_start).astype(jnp.float32)
    attention_gain = rolled(attention_gain, column_start)
    feedforward_gain = rolled(feedforward_gain, column_start)
    attention_scale = lax.rsqrt(jnp.mean(tokens_wide * tokens_wide, axis=-1, keepdims=True) + 1e-06)
    normed = group_gather((tokens_wide * attention_scale * attention_gain).astype(low))

    def by_head(weight, axis):
        return jnp.where(core == 0, weight, jnp.flip(weight, axis))

    mine = [
        by_head(weight, 1).reshape(shard, 2, -1)
        for weight in (query_weight, key_weight, value_weight)
    ]
    qkv_local = jnp.concatenate(
        [part[:, place] for place in range(2) for part in mine], axis=1
    )
    qkv_own = fsdp_gather(qkv_local)
    qkv_other = [swap(part, "tensor", 1) for part in qkv_own]
    third = 3 * qk_width

    def qkv_columns(own, other):
        pieces = [
            source[:, start + place * qk_width : start + (place + 1) * qk_width]
            for sources in (((own, 0), (other, third)), ((other, 0), (own, third)))
            for place in range(3)
            for source, start in sources
        ]
        return jnp.concatenate(pieces, axis=1)

    qkv_all = jnp.concatenate(
        [qkv_columns(own, other) for own, other in zip(qkv_own, qkv_other)], axis=0
    )

    output_local = by_head(output_weight, 0).reshape(2 * value_half, -1)
    output_own = fsdp_gather(output_local)
    output_other = [swap(part, "tensor", 1) for part in output_own]
    output_own = jnp.concatenate(output_own, axis=1)
    output_other = jnp.concatenate(output_other, axis=1)
    output_all = jnp.concatenate(
        [
            output_own[:value_half],
            output_other[value_half:],
            output_other[:value_half],
            output_own[value_half:],
        ],
        axis=0,
    )

    def hidden_rows(local):
        own = fsdp_gather(local)
        other = [swap(part, "tensor", 1) for part in own]
        return jnp.concatenate(
            [jnp.concatenate(own, axis=1), jnp.concatenate(other, axis=1)], axis=0
        )

    gate_all = hidden_rows(jnp.transpose(gate_weight))
    up_all = hidden_rows(jnp.transpose(up_weight))
    down_all = hidden_rows(down_weight)
    units = down_weight.shape[0]

    qkv = contract(normed, qkv_all, 1, 0)

    def rotate(part):
        return part * cosine + swap_halves(part) * sine

    def rotate_back(part):
        return part * cosine - swap_halves(part) * sine

    def finish(block):
        columns = [
            block[:, place * qk_width : (place + 1) * qk_width] for place in range(6)
        ]
        return jnp.concatenate(
            [
                rotate(columns[0]) * scale,
                rotate(columns[1]) * scale,
                rotate(columns[2]),
                rotate(columns[3]),
                columns[4],
                columns[5],
            ],
            axis=1,
        ).astype(low)

    head_columns = 2 * third
    qkv_kept = finish(qkv[:, :head_columns])
    qkv_received = swap(finish(qkv[:, head_columns:]), "tensor", 1)

    block_order = jnp.arange(8, dtype=jnp.int32)
    place_of = ((block_order & 1) ^ core) * 4 + ((block_order >> 1) ^ head_index)

    def in_order(kept, received):
        both = jnp.concatenate([kept, received], axis=0).reshape(8, rows, -1)
        return jnp.take(both, place_of, axis=0).reshape(slots, -1)

    slot_of_place = jnp.zeros((8,), jnp.int32).at[place_of].set(block_order)

    def by_place(ordered):
        both = jnp.take(ordered.reshape(8, rows, -1), slot_of_place, axis=0)
        return both[:4].reshape(slots // 2, -1), both[4:].reshape(slots // 2, -1)

    qkv_head = in_order(qkv_kept, qkv_received)
    queries = jnp.stack([qkv_head[:, :qk_width], qkv_head[:, qk_width : 2 * qk_width]])
    keys = jnp.stack(
        [qkv_head[:, 2 * qk_width : 3 * qk_width], qkv_head[:, 3 * qk_width : 4 * qk_width]]
    )
    values = qkv_head[:, 4 * qk_width :]
    segment, _ = slot_layout(lengths, jnp.arange(slots, dtype=jnp.int32))

    def allowed(start, stop):
        query_slot = jnp.arange(start, stop, dtype=jnp.int32)
        key_slot = jnp.arange(stop, dtype=jnp.int32)
        return (segment[start:stop, None] == segment[None, :stop]) & (
            key_slot[None, :] <= query_slot[:, None]
        )

    out_pieces, total_pieces = [], []
    for start in range(0, slots, attention_block):
        stop = start + attention_block
        scores = jnp.einsum(
            "mqe,mke->mqk",
            queries[:, start:stop],
            keys[:, :stop],
            preferred_element_type=jnp.float32,
        )
        scores = jnp.where(allowed(start, stop)[None], scores, -1e30)
        row_max = jnp.max(scores, axis=-1, keepdims=True)
        expanded = jnp.exp(scores - row_max)
        row_total = jnp.sum(expanded, axis=-1, keepdims=True)
        probability = (expanded / row_total).astype(low)
        out_pieces.append(
            jnp.einsum(
                "mqk,kv->mqv", probability, values[:stop], preferred_element_type=jnp.float32
            )
        )
        total_pieces.append(row_max + jnp.log(row_total))
    maps_out = jnp.concatenate(out_pieces, axis=1)
    log_total = jnp.concatenate(total_pieces, axis=1)
    mixed = maps_out[0] * own_coefficient + maps_out[1] * other_coefficient
    head_scale = lax.rsqrt(jnp.mean(mixed * mixed, axis=-1, keepdims=True) + 1e-05)
    head_out_kept, head_out_sent = by_place((mixed * head_scale * gain_own).astype(low))
    head_out = jnp.concatenate([head_out_kept, swap(head_out_sent, "tensor", 1)], axis=1)

    residual = tokens_wide + group_reduce(contract(head_out, output_all, 1, 0), rows)
    ffn_scale = lax.rsqrt(jnp.mean(residual * residual, axis=-1, keepdims=True) + 1e-06)
    ffn_in = group_gather((residual * ffn_scale * feedforward_gain).astype(low))
    ffn_out_grad = valid * rolled(cotangent, column_start).astype(jnp.float32)
    ffn_out_grad_all = group_gather(ffn_out_grad.astype(low))
    gate_pre = contract(gate_all, ffn_in, 1, 1)
    upward = contract(up_all, ffn_in, 1, 1)
    sigmoid_gate = jax.nn.sigmoid(gate_pre)
    silu_gate = gate_pre * sigmoid_gate
    hidden = (silu_gate * upward).astype(low)
    ffn_here = group_reduce(contract(hidden, down_all, 0, 0), rows)
    block_output = (valid * (residual + ffn_here)).astype(low)

    def shared(partial_all):
        own, other = partial_all[: partial_all.shape[0] // 2], partial_all[partial_all.shape[0] // 2 :]
        total = own + swap(other.astype(low), "tensor", 1).astype(jnp.float32)
        return fsdp_reduce(
            [total[:, start : start + shard] for start in range(0, width, shard)]
        )

    hidden_grad = contract(down_all, ffn_out_grad_all, 1, 1)
    down_grad = shared(contract(hidden, ffn_out_grad_all, 1, 0))
    gate_grad = (
        hidden_grad * upward * sigmoid_gate * (1.0 + gate_pre * (1.0 - sigmoid_gate))
    ).astype(low)
    up_grad = (hidden_grad * silu_gate).astype(low)
    ffn_in_grad = group_reduce(
        contract(gate_grad, gate_all, 0, 0) + contract(up_grad, up_all, 0, 0), rows
    )
    gate_weight_grad = jnp.transpose(shared(contract(gate_grad, ffn_in, 1, 0)))
    up_weight_grad = jnp.transpose(shared(contract(up_grad, ffn_in, 1, 0)))
    feedforward_gain_grad = jnp.sum(ffn_in_grad * residual * ffn_scale, axis=0)
    ffn_gained = ffn_in_grad * feedforward_gain
    residual_grad = (
        ffn_out_grad
        + ffn_scale * ffn_gained
        - residual * ffn_scale**3 * jnp.mean(ffn_gained * residual, axis=-1, keepdims=True)
    )

    attention_out_grad = group_gather(residual_grad.astype(low))
    head_out_grad_all = contract(attention_out_grad, output_all, 1, 1)
    head_out_grad = in_order(
        head_out_grad_all[:, :value_width].astype(low),
        swap(head_out_grad_all[:, value_width:].astype(low), "tensor", 1),
    ).astype(jnp.float32)
    output_grad = contract(head_out, attention_out_grad, 0, 0)
    output_grad = shared(
        jnp.concatenate(
            [
                output_grad[:value_half],
                output_grad[3 * value_half :],
                output_grad[2 * value_half : 3 * value_half],
                output_grad[value_half : 2 * value_half],
            ],
            axis=0,
        )
    )
    head_gain_part = jnp.sum(head_out_grad * mixed * head_scale, axis=0, keepdims=True) * (
        1.0 - lambda_base
    )
    weighted = head_out_grad * gain_own
    mixed_grad = head_scale * weighted - mixed * head_scale**3 * jnp.mean(
        weighted * mixed, axis=-1, keepdims=True
    )
    second_map = jnp.where(core == 1, maps_out[0], maps_out[1])
    lambda_grad = -jnp.sum(mixed_grad * second_map)
    vector_grads = lambda_grad * jnp.stack(
        [
            first_exp * vectors[1],
            first_exp * vectors[0],
            -second_exp * vectors[3],
            -second_exp * vectors[2],
        ]
    )
    map_grad = jnp.stack([mixed_grad * own_coefficient, mixed_grad * other_coefficient]).astype(low)
    query_pieces = []
    key_grad = jnp.zeros((2, slots, qk_width), jnp.float32)
    value_grad = jnp.zeros((slots, value_width), jnp.float32)
    for start in range(0, slots, attention_block):
        stop = start + attention_block
        scores = jnp.einsum(
            "mqe,mke->mqk",
            queries[:, start:stop],
            keys[:, :stop],
            preferred_element_type=jnp.float32,
        )
        scores = jnp.where(allowed(start, stop)[None], scores, -1e30)
        probability = jnp.exp(scores - log_total[:, start:stop])
        prob_grad = jnp.einsum(
            "mqv,kv->mqk",
            map_grad[:, start:stop],
            values[:stop],
            preferred_element_type=jnp.float32,
        )
        value_grad = value_grad.at[:stop].add(
            jnp.einsum(
                "mqk,mqv->kv",
                probability.astype(low),
                map_grad[:, start:stop],
                preferred_element_type=jnp.float32,
            )
        )
        delta_sum = jnp.sum(probability * prob_grad, axis=-1, keepdims=True)
        score_grad = (probability * (prob_grad - delta_sum)).astype(low)
        query_pieces.append(
            jnp.einsum("mqk,mke->mqe", score_grad, keys[:, :stop], preferred_element_type=jnp.float32)
        )
        key_grad = key_grad.at[:, :stop].add(
            jnp.einsum(
                "mqk,mqe->mke",
                score_grad,
                queries[:, start:stop],
                preferred_element_type=jnp.float32,
            )
        )
    query_grad = jnp.concatenate(query_pieces, axis=1)
    segment_all, position_all = slot_layout(lengths, jnp.arange(slots, dtype=jnp.int32))
    angles = position_all.astype(jnp.float32)[:, None] * frequency[None, :]
    cosine = jnp.concatenate([jnp.cos(angles)] * 2, axis=1)
    sine = jnp.concatenate([-jnp.sin(angles), jnp.sin(angles)], axis=1)
    qkv_grad = jnp.concatenate(
        [
            rotate_back(query_grad[0] * scale),
            rotate_back(query_grad[1] * scale),
            rotate_back(key_grad[0]),
            rotate_back(key_grad[1]),
            value_grad,
        ],
        axis=1,
    ).astype(low)
    qkv_grad_kept, qkv_grad_sent = by_place(qkv_grad)
    qkv_grad = jnp.concatenate([qkv_grad_kept, swap(qkv_grad_sent, "tensor", 1)], axis=1)

    normed_partial = contract(qkv_grad, qkv_all, 1, 1)
    attention_gain_part = jnp.sum(normed_partial * normed.astype(jnp.float32), axis=0)
    back = width - column_start
    attention_gain_grad = total_over_all(rolled(attention_gain_part / attention_gain, back))
    normed_grad = group_reduce(normed_partial, rows)
    qkv_weight_grad = contract(normed, qkv_grad, 0, 0)
    columns = [
        qkv_weight_grad[:, place * qk_width : (place + 1) * qk_width] for place in range(12)
    ]
    own_terms = jnp.concatenate([columns[k] for k in (0, 2, 4, 7, 9, 11)], axis=1)
    other_terms = jnp.concatenate([columns[k] for k in (6, 8, 10, 1, 3, 5)], axis=1)
    own_terms = own_terms + swap(other_terms.astype(low), "tensor", 1).astype(jnp.float32)
    qkv_weight_grad = fsdp_reduce(
        [own_terms[start : start + shard] for start in range(0, width, shard)]
    ).reshape(shard, 2, 3, qk_width)
    qkv_weight_grad = by_head(qkv_weight_grad, 1)
    output_grad = by_head(output_grad.reshape(2, value_half, -1), 0)

    attention_gained = normed_grad * attention_gain
    tokens_grad = (
        residual_grad
        + attention_scale * attention_gained
        - tokens_wide
        * attention_scale**3
        * jnp.mean(attention_gained * tokens_wide, axis=-1, keepdims=True)
    )

    lambda_full = lax.dynamic_update_slice(
        jnp.zeros(lambda_vectors.shape, jnp.float32), vector_grads[None], (own_head, 0, 0)
    )
    gain_full = lax.dynamic_update_slice(
        jnp.zeros(head_gain.shape, jnp.float32),
        rolled(head_gain_part, core * value_half),
        (own_head, 0),
    )
    small = total_over_all(
        jnp.concatenate(
            [
                rolled(feedforward_gain_grad, back),
                lambda_full.reshape(-1),
                gain_full.reshape(-1),
            ]
        )
    )
    feedforward_gain_grad = small[:width]
    lambda_grads = small[width : width + lambda_full.size].reshape(lambda_full.shape)
    gain_grads = small[width + lambda_full.size :].reshape(gain_full.shape)
    return (
        rolled(block_output, back),
        rolled(tokens_grad, back),
        attention_gain_grad,
        qkv_weight_grad[:, :, 0].reshape(query_weight.shape),
        qkv_weight_grad[:, :, 1].reshape(key_weight.shape),
        qkv_weight_grad[:, :, 2].reshape(value_weight.shape),
        output_grad.reshape(output_weight.shape),
        lambda_grads,
        gain_grads,
        feedforward_gain_grad,
        gate_weight_grad,
        up_weight_grad,
        down_grad,
    )


def solution(mesh):
    placed = (
        P(("fsdp", "head", "tensor"), None),
        P("fsdp", None),
        P(),
        P("fsdp", "head", "tensor", None),
        P("fsdp", "head", "tensor", None),
        P("fsdp", "head", "tensor"),
        P("head", "tensor", "fsdp"),
        P(),
        P(),
        P(),
        P("fsdp", ("head", "tensor")),
        P("fsdp", ("head", "tensor")),
        P(("head", "tensor"), "fsdp"),
        P(("fsdp", "head", "tensor"), None),
    )
    return jax.shard_map(
        body,
        mesh=mesh,
        in_specs=placed,
        out_specs=(
            P(("fsdp", "head", "tensor"), None),
            P(("fsdp", "head", "tensor"), None),
            P(),
            P("fsdp", "head", "tensor", None),
            P("fsdp", "head", "tensor", None),
            P("fsdp", "head", "tensor"),
            P("head", "tensor", "fsdp"),
            P(),
            P(),
            P(),
            P("fsdp", ("head", "tensor")),
            P("fsdp", ("head", "tensor")),
            P(("head", "tensor"), "fsdp"),
        ),
        check_vma=False,
    )
```

```python
import functools

import jax
import jax.numpy as jnp
from jax import lax
from jax.experimental import pallas as pl
from jax.experimental.pallas import tpu as pltpu
from jax.sharding import PartitionSpec as P

lambda_base = 0.2
tile = 512
low = jnp.bfloat16


def contract(left_side, right_side, left_dim, right_dim):
    return lax.dot_general(
        left_side,
        right_side,
        (((left_dim,), (right_dim,)), ((), ())),
        preferred_element_type=jnp.float32,
    )


def after(values, *others):
    return lax.optimization_barrier((values, *others))[0]


def swap(values, axis, mask):
    size = lax.axis_size(axis)
    return lax.ppermute(values, axis, [(place, place ^ mask) for place in range(size)])


def shift(values, axis, step):
    size = lax.axis_size(axis)
    return lax.ppermute(values, axis, [(place, (place + step) % size) for place in range(size)])


class Line:
    def __init__(self):
        self.arrived = []

    def send(self, values, step):
        if len(self.arrived) > 1:
            values = after(values, self.arrived[-2])
        values = shift(values, "fsdp", step)
        self.arrived.append(values)
        return values

    def gather(self, own):
        size = lax.axis_size("fsdp")
        shards = [own] + [None] * (size - 1)
        up, down = own, own
        for step in range(1, size // 2 + 1):
            up = self.send(up, 1)
            shards[size - step] = up
            if step <= size - 1 - size // 2:
                down = self.send(down, -1)
                shards[step] = down
        return shards

    def reduce(self, partial):
        size = lax.axis_size("fsdp")
        up_steps = size // 2
        down_steps = size - 1 - up_steps
        up = down = None
        for step in range(up_steps):
            term = partial[up_steps - step]
            up = self.send(term if up is None else add_low(term, up), 1)
            if step < down_steps:
                term = partial[size - down_steps + step]
                down = self.send(term if down is None else add_low(term, down), -1)
        total = partial[0].astype(jnp.float32) + up.astype(jnp.float32)
        return total if down is None else total + down.astype(jnp.float32)


def add_low(left_side, right_side):
    return (left_side.astype(jnp.float32) + right_side.astype(jnp.float32)).astype(low)


def group_gather(own):
    half = own.shape[0] // 2
    first = swap(own, "head", 1)
    second = swap(own, "head", 2)
    third_low = swap(second[:half], "head", 1)
    third_high = swap(first[half:], "head", 2)
    return jnp.concatenate([own, first, second, third_low, third_high], axis=0)


def group_reduce(nearer, third):
    rows = third.shape[0]
    half = rows // 2
    own, first, second = (nearer[place * rows : (place + 1) * rows] for place in range(3))
    to_first = swap(third[:half].astype(low), "head", 1)
    to_second = swap(third[half:].astype(low), "head", 2)
    second = jnp.concatenate(
        [add_low(second[:half], to_first), second[half:].astype(low)], axis=0
    )
    first = jnp.concatenate(
        [first[:half].astype(low), add_low(first[half:], to_second)], axis=0
    )
    from_first = swap(first, "head", 1)
    from_second = swap(second, "head", 2)
    return (
        own.astype(jnp.float32) + from_first.astype(jnp.float32) + from_second.astype(jnp.float32)
    )


def total_over_all(values):
    for axis in ("tensor", "head", "fsdp"):
        mask = 1
        while mask < lax.axis_size(axis):
            values = values + swap(values, axis, mask)
            mask *= 2
    return values


def rolled(values, start):
    twice = jnp.concatenate([values, values], axis=-1)
    return lax.dynamic_slice_in_dim(twice, start, values.shape[-1], values.ndim - 1)


def slot_layout(lengths, slots):
    first_end = lengths[0, 0]
    second_end = first_end + lengths[0, 1]
    segment = (slots >= first_end).astype(jnp.int32) + (slots >= second_end).astype(jnp.int32)
    start = jnp.where(segment == 0, 0, jnp.where(segment == 1, first_end, second_end))
    return segment, slots - start


def swap_halves(values):
    half = values.shape[1] // 2
    return jnp.concatenate([values[:, half:], values[:, :half]], axis=1)


def place_of(block, head_index, core):
    return ((block & 1) ^ core) * 4 + ((block >> 1) ^ head_index)


def row_starts(slots, first_end, second_end):
    return jnp.where(slots >= second_end, second_end, jnp.where(slots >= first_end, first_end, 0))


def attention_forward_kernel(
    ints, floats, kept, received, gain, head_out, ordered, outs, log_totals
):
    head_index, core, first_end, second_end = (ints[place] for place in range(4))
    rows = kept.shape[0] // 4
    slots = 8 * rows
    width = gain.shape[1]
    e = width // 2
    for part, other in ((kept, 0), (received, 1)):
        for j in range(4):
            block = (head_index ^ j) * 2 + (core ^ other)
            at = pl.ds(pl.multiple_of(block * rows, rows), rows)
            for m in range(2):
                for kind in range(3):
                    to, source = (2 * kind + m) * e, (3 * m + kind) * e
                    ordered[at, to : to + e] = part[
                        j * rows : (j + 1) * rows, source : source + e
                    ]
    for start in range(0, slots, tile):
        stop = start + tile
        row = start + lax.broadcasted_iota(jnp.int32, (tile, 1), 0)
        begin = row_starts(row, first_end, second_end)
        value = ordered[:stop, 4 * e :]
        results = []
        for m in range(2):
            scores = contract(
                ordered[start:stop, m * e : (m + 1) * e],
                ordered[:stop, (2 + m) * e : (3 + m) * e],
                1,
                1,
            )
            column = lax.broadcasted_iota(jnp.int32, (tile, stop), 1)
            scores = jnp.where((column >= begin) & (column <= row), scores, -1e30)
            row_max = jnp.max(scores, axis=1, keepdims=True)
            expanded = jnp.exp(scores - row_max)
            row_total = jnp.sum(expanded, axis=1, keepdims=True)
            result = contract(expanded.astype(low), value, 1, 0) / row_total
            outs[m, start:stop, :] = result
            results.append(result)
            wide = jnp.broadcast_to(row_max + jnp.log(row_total), (tile, 128))
            log_totals[m : m + 1, start:stop] = jnp.transpose(wide)[:1]
        mixed = results[0] * floats[0] + results[1] * floats[1]
        scale = lax.rsqrt(jnp.mean(mixed * mixed, axis=1, keepdims=True) + 1e-05)
        normed = (mixed * scale * gain[...]).astype(low)
        for piece in range(tile // rows):
            place = place_of(start // rows + piece, head_index, core)
            head_out[pl.ds(pl.multiple_of(place * rows, rows), rows), :] = normed[
                piece * rows : (piece + 1) * rows
            ]


def attention_forward(ints, floats, kept, received, gain):
    rows = kept.shape[0] // 4
    slots = 8 * rows
    width = gain.shape[1]
    vmem = pl.BlockSpec(memory_space=pltpu.VMEM)
    smem = pl.BlockSpec(memory_space=pltpu.SMEM)
    return pl.pallas_call(
        attention_forward_kernel,
        in_specs=[smem, smem, vmem, vmem, vmem],
        out_specs=[vmem] * 4,
        out_shape=[
            jax.ShapeDtypeStruct((slots, width), low),
            jax.ShapeDtypeStruct((slots, 3 * width), low),
            jax.ShapeDtypeStruct((2, slots, width), jnp.float32),
            jax.ShapeDtypeStruct((2, slots), jnp.float32),
        ],
        compiler_params=pltpu.CompilerParams(vmem_limit_bytes=40 * 2**20),
        cost_estimate=pl.CostEstimate(
            flops=20 * 10**9, bytes_accessed=16 * 2**20, transcendentals=6 * 10**6
        ),
        name="attention_forward",
    )(ints, floats, kept, received, gain)


def attention_backward_kernel(
    ints,
    floats,
    ordered,
    grads_kept,
    grads_received,
    outs,
    log_totals,
    gain,
    cosine,
    sine,
    qkv_grad,
    gain_grad,
    lambda_grad,
    map_grads,
    deltas,
    query_grads,
    key_grads,
    value_grads,
):
    head_index, core, first_end, second_end = (ints[place] for place in range(4))
    rows = grads_kept.shape[0] // 4
    slots = 8 * rows
    width = gain.shape[1]
    e = width // 2
    gain_total = jnp.zeros((1, width), jnp.float32)
    lambda_total = jnp.zeros((1, width), jnp.float32)
    for part, other in ((grads_kept, 0), (grads_received, 1)):
        for j in range(4):
            block = (head_index ^ j) * 2 + (core ^ other)
            at = pl.ds(pl.multiple_of(block * rows, rows), rows)
            grad = part[j * rows : (j + 1) * rows, :].astype(jnp.float32)
            first, second = outs[0, at, :], outs[1, at, :]
            mixed = first * floats[0] + second * floats[1]
            scale = lax.rsqrt(jnp.mean(mixed * mixed, axis=1, keepdims=True) + 1e-05)
            gain_total += jnp.sum(grad * (mixed * scale), axis=0, keepdims=True)
            weighted = grad * gain[...]
            inner = jnp.mean(weighted * mixed, axis=1, keepdims=True)
            mixed_grad = scale * weighted - mixed * (scale * scale * scale * inner)
            lambda_total += jnp.sum(
                mixed_grad * jnp.where(core == 1, first, second), axis=0, keepdims=True
            )
            for m, out in ((0, first), (1, second)):
                map_grad = (mixed_grad * floats[m]).astype(low)
                map_grads[m, at, :] = map_grad
                delta = jnp.sum(map_grad.astype(jnp.float32) * out, axis=1, keepdims=True)
                deltas[m, :, at] = jnp.transpose(jnp.broadcast_to(delta, (rows, 128)))[:8]
    gain_grad[...] = gain_total * (1.0 - lambda_base)
    lambda_grad[...] = lambda_total
    query_grads[...] = jnp.zeros_like(query_grads)

    def pair(key_start, query_start, diagonal):
        at_keys = pl.ds(key_start, tile)
        at_queries = pl.ds(query_start, tile)
        column = query_start + lax.broadcasted_iota(jnp.int32, (1, tile), 1)
        begin = row_starts(column, first_end, second_end)
        row = key_start + lax.broadcasted_iota(jnp.int32, (tile, tile), 0)
        allowed = row >= begin
        if diagonal:
            allowed = allowed & (row <= column)
        value = ordered[at_keys, 4 * e :]
        for m in range(2):
            query = ordered[at_queries, m * e : (m + 1) * e]
            key = ordered[at_keys, (2 + m) * e : (3 + m) * e]
            map_grad = map_grads[m, at_queries, :]
            scores = contract(key, query, 1, 1)
            probability = jnp.where(
                allowed, jnp.exp(scores - log_totals[m : m + 1, at_queries]), 0.0
            )
            prob_grad = contract(value, map_grad, 1, 1)
            score_grad = (probability * (prob_grad - deltas[m, 0:1, at_queries])).astype(low)
            value_term = contract(probability.astype(low), map_grad, 1, 0)
            key_term = contract(score_grad, query, 1, 0)
            query_grads[m, at_queries, :] += contract(score_grad, key, 0, 0)
            if diagonal:
                key_grads[m, at_keys, :] = key_term
                if m == 0:
                    value_grads[at_keys, :] = value_term
                else:
                    value_grads[at_keys, :] += value_term
            else:
                key_grads[m, at_keys, :] += key_term
                value_grads[at_keys, :] += value_term

    for key_start in range(0, slots, tile):
        pair(key_start, key_start, True)

        def step(at, carry, key_start=key_start):
            pair(key_start, pl.multiple_of(at * tile, tile), False)
            return carry

        lax.fori_loop(key_start // tile + 1, slots // tile, step, 0)

    def turn_back(values, at):
        return values * cosine[at, :] - pltpu.roll(values, e // 2, 1) * sine[at, :]

    for block in range(8):
        at = slice(block * rows, (block + 1) * rows)
        to = pl.ds(pl.multiple_of(place_of(block, head_index, core) * rows, rows), rows)
        for m in range(2):
            first = 3 * m * e
            qkv_grad[to, first : first + e] = (
                turn_back(query_grads[m, at, :], at) * e ** (-0.5)
            ).astype(low)
            qkv_grad[to, first + e : first + 2 * e] = turn_back(key_grads[m, at, :], at).astype(
                low
            )
            qkv_grad[to, first + 2 * e : first + 3 * e] = value_grads[
                at, m * e : (m + 1) * e
            ].astype(low)


def attention_backward(
    ints, floats, ordered, grads_kept, grads_received, outs, log_totals, gain, cosine, sine
):
    slots, width = outs.shape[1:]
    vmem = pl.BlockSpec(memory_space=pltpu.VMEM)
    smem = pl.BlockSpec(memory_space=pltpu.SMEM)
    return pl.pallas_call(
        attention_backward_kernel,
        in_specs=[smem, smem] + [vmem] * 8,
        out_specs=[vmem] * 3,
        out_shape=[
            jax.ShapeDtypeStruct((slots, 3 * width), low),
            jax.ShapeDtypeStruct((1, width), jnp.float32),
            jax.ShapeDtypeStruct((1, width), jnp.float32),
        ],
        scratch_shapes=[
            pltpu.VMEM((2, slots, width), low),
            pltpu.VMEM((2, 8, slots), jnp.float32),
            pltpu.VMEM((2, slots, width // 2), jnp.float32),
            pltpu.VMEM((2, slots, width // 2), jnp.float32),
            pltpu.VMEM((slots, width), jnp.float32),
        ],
        compiler_params=pltpu.CompilerParams(vmem_limit_bytes=48 * 2**20),
        cost_estimate=pl.CostEstimate(
            flops=40 * 10**9, bytes_accessed=24 * 2**20, transcendentals=6 * 10**6
        ),
        name="attention_backward",
    )(ints, floats, ordered, grads_kept, grads_received, outs, log_totals, gain, cosine, sine)


def gate_kernel(inputs, gate, up, hidden, gate_factor, up_factor):
    gate_pre = contract(gate[...], inputs[...], 1, 1)
    upward = contract(up[...], inputs[...], 1, 1)
    sigmoid = 1.0 / (1.0 + jnp.exp(-gate_pre))
    silu = gate_pre * sigmoid
    hidden[...] = (silu * upward).astype(low)
    gate_factor[...] = (upward * (sigmoid * (1.0 + gate_pre * (1.0 - sigmoid)))).astype(low)
    up_factor[...] = silu.astype(low)


def gate_units(inputs, gate, up):
    slots, width = inputs.shape
    units = gate.shape[0]
    block = slots // 4
    whole = pl.BlockSpec((units, width), lambda i: (0, 0))
    across = pl.BlockSpec((units, block), lambda i: (0, i))
    return pl.pallas_call(
        gate_kernel,
        grid=(4,),
        in_specs=[pl.BlockSpec((block, width), lambda i: (i, 0)), whole, whole],
        out_specs=[across] * 3,
        out_shape=[jax.ShapeDtypeStruct((units, slots), low)] * 3,
        compiler_params=pltpu.CompilerParams(vmem_limit_bytes=40 * 2**20),
        cost_estimate=pl.CostEstimate(
            flops=4 * slots * width * units,
            bytes_accessed=16 * 2**20,
            transcendentals=units * slots,
        ),
        name="gate_units",
    )(inputs, gate, up)


def gate_grad_kernel(grads, down, gate_factor, up_factor, gate_grad, up_grad):
    hidden_grad = contract(down[...], grads[...], 1, 1)
    gate_grad[...] = (hidden_grad * gate_factor[...].astype(jnp.float32)).astype(low)
    up_grad[...] = (hidden_grad * up_factor[...].astype(jnp.float32)).astype(low)


def gate_grads(grads, down, gate_factor, up_factor):
    slots, width = grads.shape
    units = down.shape[0]
    block = slots // 4
    across = pl.BlockSpec((units, block), lambda i: (0, i))
    return pl.pallas_call(
        gate_grad_kernel,
        grid=(4,),
        in_specs=[
            pl.BlockSpec((block, width), lambda i: (i, 0)),
            pl.BlockSpec((units, width), lambda i: (0, 0)),
            across,
            across,
        ],
        out_specs=[across] * 2,
        out_shape=[jax.ShapeDtypeStruct((units, slots), low)] * 2,
        compiler_params=pltpu.CompilerParams(vmem_limit_bytes=40 * 2**20),
        cost_estimate=pl.CostEstimate(
            flops=2 * slots * width * units, bytes_accessed=16 * 2**20, transcendentals=0
        ),
        name="gate_grads",
    )(grads, down, gate_factor, up_factor)


def sum_kernel(terms, *refs):
    out = refs[-1]
    total = contract(refs[0][...], refs[terms][...], 0, 0)
    for place in range(1, terms):
        total += contract(refs[place][...], refs[terms + place][...], 0, 0)
    out[...] = total.astype(out.dtype)


def sum_over_units(factors, weights, first, count, rows):
    units, width = weights[0].shape
    terms = len(factors)
    return pl.pallas_call(
        functools.partial(sum_kernel, terms),
        grid=(count,),
        in_specs=[pl.BlockSpec((units, rows), lambda i: (0, first + i))] * terms
        + [pl.BlockSpec((units, width), lambda i: (0, 0))] * terms,
        out_specs=pl.BlockSpec((rows, width), lambda i: (i, 0)),
        out_shape=jax.ShapeDtypeStruct((count * rows, width), low),
        compiler_params=pltpu.CompilerParams(vmem_limit_bytes=48 * 2**20),
        cost_estimate=pl.CostEstimate(
            flops=2 * count * rows * width * units * terms,
            bytes_accessed=terms * 4 * 2**20,
            transcendentals=0,
        ),
        name="sum_over_units",
    )(*factors, *weights)


def body(
    tokens,
    lengths,
    attention_gain,
    query_weight,
    key_weight,
    value_weight,
    output_weight,
    lambda_vectors,
    head_gain,
    feedforward_gain,
    gate_weight,
    up_weight,
    down_weight,
    cotangent,
):
    rows, width = tokens.shape
    fsdp_index = lax.axis_index("fsdp")
    head_index = lax.axis_index("head")
    core = lax.axis_index("tensor")
    shard = query_weight.shape[0]
    qk_width = query_weight.shape[3]
    value_half = value_weight.shape[2]
    slots = rows * 8
    half_slots = slots // 2
    scale = qk_width ** (-0.5)
    column_start = fsdp_index * shard
    back = width - column_start

    def in_order(mine, other):
        return jnp.where(core == 0, mine, other), jnp.where(core == 0, other, mine)

    tokens_wide = rolled(tokens, column_start).astype(jnp.float32)
    attention_gain = rolled(attention_gain, column_start)
    feedforward_gain = rolled(feedforward_gain, column_start)
    attention_scale = lax.rsqrt(jnp.mean(tokens_wide * tokens_wide, axis=-1, keepdims=True) + 1e-06)
    normed = group_gather((tokens_wide * attention_scale * attention_gain).astype(low))

    third = 3 * qk_width
    heads = [
        jnp.concatenate(
            [
                weight[:, place].reshape(shard, -1)
                for weight in (query_weight, key_weight, value_weight)
            ],
            axis=1,
        )
        for place in range(2)
    ]
    line = Line()
    qkv_own = jnp.concatenate(line.gather(jnp.concatenate(in_order(*heads), axis=1)), axis=0)
    qkv_other = swap(qkv_own, "tensor", 1)
    output_own = jnp.concatenate(
        line.gather(jnp.concatenate(in_order(output_weight[0], output_weight[1]), axis=0)), axis=1
    )
    output_all = jnp.concatenate([output_own, swap(output_own, "tensor", 1)], axis=0)

    def both_cores(local):
        own = jnp.concatenate(line.gather(local), axis=1)
        return own, swap(own, "tensor", 1)

    gate_own, gate_other = both_cores(jnp.transpose(gate_weight))
    up_own, up_other = both_cores(jnp.transpose(up_weight))
    down_own, down_other = both_cores(down_weight)

    own_slots = (
        (jnp.arange(4, dtype=jnp.int32) ^ head_index)[:, None] * (2 * rows)
        + core * rows
        + jnp.arange(rows, dtype=jnp.int32)[None, :]
    ).reshape(-1)
    segment_own, position_own = slot_layout(lengths, own_slots)
    valid = (segment_own[:rows] < 2).astype(jnp.float32)[:, None]
    half_width = qk_width // 2
    frequency = 10000.0 ** (-jnp.arange(half_width, dtype=jnp.float32) / half_width)

    def turn_tables(positions):
        angles = positions.astype(jnp.float32)[:, None] * frequency[None, :]
        cosine, sine = jnp.cos(angles), jnp.sin(angles)
        return jnp.concatenate([cosine, cosine], axis=1), jnp.concatenate([-sine, sine], axis=1)

    cosine, sine = turn_tables(position_own)
    cosine_all, sine_all = turn_tables(
        slot_layout(lengths, jnp.arange(slots, dtype=jnp.int32))[1]
    )
    own_head = head_index * 2 + core
    vectors = lax.dynamic_slice_in_dim(lambda_vectors, own_head, 1, 0)[0]
    first_exp = jnp.exp(jnp.sum(vectors[0] * vectors[1]))
    second_exp = jnp.exp(jnp.sum(vectors[2] * vectors[3]))
    lambda_value = first_exp - second_exp + lambda_base
    floats = jnp.stack(in_order(1.0, -lambda_value))
    ints = jnp.stack([head_index, core, lengths[0, 0], lengths[0, 0] + lengths[0, 1]])
    gain_own = rolled(
        lax.dynamic_slice_in_dim(head_gain, own_head, 1, 0), core * value_half
    ) * (1.0 - lambda_base)

    from_own = contract(normed, qkv_own, 1, 0)
    from_other = contract(normed, qkv_other, 1, 0)

    def rotate(part):
        return part * cosine + swap_halves(part) * sine

    def finish(block):
        return [
            rotate(block[:, :qk_width]) * scale,
            rotate(block[:, qk_width : 2 * qk_width]),
            block[:, 2 * qk_width :],
        ]

    qkv_kept = jnp.concatenate(
        finish(from_own[:, :third]) + finish(from_other[:, third:]), axis=1
    ).astype(low)
    qkv_sent = jnp.concatenate(
        finish(from_other[:, :third]) + finish(from_own[:, third:]), axis=1
    ).astype(low)
    head_out_both, ordered, outs, log_totals = attention_forward(
        ints, floats, qkv_kept, swap(qkv_sent, "tensor", 1), gain_own
    )
    kept, received = head_out_both[:half_slots], swap(head_out_both[half_slots:], "tensor", 1)
    head_out = jnp.concatenate(
        [
            kept[:, :value_half],
            received[:, value_half:],
            received[:, :value_half],
            kept[:, value_half:],
        ],
        axis=1,
    )

    ffn_out_grad = valid * rolled(cotangent, column_start).astype(jnp.float32)
    ffn_out_grad_all = group_gather(after(ffn_out_grad.astype(low), normed))
    third_out = contract(head_out[3 * rows :], output_all, 1, 0).astype(low)
    nearer_out = contract(after(head_out, third_out)[: 3 * rows], output_all, 1, 0)
    residual = tokens_wide + group_reduce(nearer_out, after(third_out, ffn_out_grad_all))
    ffn_scale = lax.rsqrt(jnp.mean(residual * residual, axis=-1, keepdims=True) + 1e-06)
    ffn_in = group_gather((residual * ffn_scale * feedforward_gain).astype(low))
    hidden_own, gate_factor_own, up_factor_own = gate_units(ffn_in, gate_own, up_own)
    hidden_other, gate_factor_other, up_factor_other = gate_units(ffn_in, gate_other, up_other)

    def weight_grad(own_side, other_side, right_side, left_dim):
        other = contract(other_side, right_side, left_dim, 0).astype(low)
        other = swap(other, "tensor", 1)
        total = add_low(contract(own_side, right_side, left_dim, 0), other)
        return [total[:, start : start + shard] for start in range(0, width, shard)]

    down_terms = weight_grad(hidden_own, hidden_other, ffn_out_grad_all, 1)
    down_grad = line.reduce(down_terms)
    gate_grad_own, up_grad_own = gate_grads(
        ffn_out_grad_all, down_own, gate_factor_own, up_factor_own
    )
    gate_grad_other, up_grad_other = gate_grads(
        ffn_out_grad_all, down_other, gate_factor_other, up_factor_other
    )
    factors = [gate_grad_own, up_grad_own, gate_grad_other, up_grad_other]
    weights = [gate_own, up_own, gate_other, up_other]
    third_grad = sum_over_units(factors, weights, 3, 1, rows)
    nearer_grad = sum_over_units([after(factors[0], third_grad)] + factors[1:], weights, 0, 3, rows)
    ffn_in_grad = group_reduce(nearer_grad, third_grad)
    gate_weight_grad = jnp.transpose(
        line.reduce(weight_grad(after(gate_grad_own, nearer_grad), gate_grad_other, ffn_in, 1))
    )
    up_weight_grad = jnp.transpose(
        line.reduce(weight_grad(after(up_grad_own, nearer_grad), up_grad_other, ffn_in, 1))
    )
    feedforward_gain_part = jnp.sum(ffn_in_grad * residual * ffn_scale, axis=0)
    ffn_gained = ffn_in_grad * feedforward_gain
    residual_grad = (
        ffn_out_grad
        + ffn_scale * ffn_gained
        - residual * ffn_scale**3 * jnp.mean(ffn_gained * residual, axis=-1, keepdims=True)
    )

    attention_out_grad = group_gather(residual_grad.astype(low))
    head_out_grad = contract(attention_out_grad, output_all, 1, 1).astype(low)
    pieces = [
        head_out_grad[:, place * value_half : (place + 1) * value_half] for place in range(4)
    ]
    qkv_grad_both, head_gain_part, lambda_part = attention_backward(
        ints,
        floats,
        ordered,
        jnp.concatenate([pieces[0], pieces[3]], axis=1),
        swap(jnp.concatenate([pieces[2], pieces[1]], axis=1), "tensor", 1),
        outs,
        log_totals,
        gain_own,
        cosine_all,
        sine_all,
    )
    output_terms = contract(head_out, attention_out_grad, 0, 0)
    output_other_part = swap(output_terms[2 * value_half :].astype(low), "tensor", 1)
    output_terms = add_low(output_terms[: 2 * value_half], output_other_part)
    output_grad = line.reduce(
        [output_terms[:, start : start + shard] for start in range(0, width, shard)]
    )

    ffn_out = sum_over_units(
        [after(hidden_own, attention_out_grad), hidden_other], [down_own, down_other], 0, 4, rows
    )
    ffn_here = group_reduce(ffn_out[: 3 * rows], ffn_out[3 * rows :])
    block_output = (valid * (residual + ffn_here)).astype(low)

    kept, received = qkv_grad_both[:half_slots], swap(qkv_grad_both[half_slots:], "tensor", 1)
    grad_own = jnp.concatenate([kept[:, :third], received[:, third:]], axis=1)
    grad_other = jnp.concatenate([received[:, :third], kept[:, third:]], axis=1)
    other_terms = swap(contract(normed, grad_other, 0, 0).astype(low), "tensor", 1)
    own_terms = add_low(contract(normed, grad_own, 0, 0), other_terms)
    qkv_weight_grad = line.reduce(
        [own_terms[start : start + shard] for start in range(0, width, shard)]
    )
    qkv_weight_grad = jnp.stack(
        in_order(qkv_weight_grad[:, :third], qkv_weight_grad[:, third:]), axis=1
    )
    output_grad = jnp.stack(in_order(output_grad[:value_half], output_grad[value_half:]))
    normed_terms = contract(
        jnp.concatenate([grad_own, grad_other], axis=1),
        jnp.concatenate([qkv_own, qkv_other], axis=1),
        1,
        1,
    )
    normed_grad = group_reduce(normed_terms[: 3 * rows], after(normed_terms[3 * rows :], ffn_here))
    attention_gain_part = jnp.sum(normed_terms * normed.astype(jnp.float32), axis=0)
    attention_gained = normed_grad * attention_gain
    tokens_grad = (
        residual_grad
        + attention_scale * attention_gained
        - tokens_wide
        * attention_scale**3
        * jnp.mean(attention_gained * tokens_wide, axis=-1, keepdims=True)
    )

    lambda_grad = -jnp.sum(lambda_part)
    vector_grads = lambda_grad * jnp.stack(
        [
            first_exp * vectors[1],
            first_exp * vectors[0],
            -second_exp * vectors[3],
            -second_exp * vectors[2],
        ]
    )
    lambda_full = lax.dynamic_update_slice(
        jnp.zeros(lambda_vectors.shape, jnp.float32), vector_grads[None], (own_head, 0, 0)
    )
    gain_full = lax.dynamic_update_slice(
        jnp.zeros(head_gain.shape, jnp.float32),
        rolled(head_gain_part, core * value_half),
        (own_head, 0),
    )
    small = total_over_all(
        jnp.concatenate(
            [
                rolled(attention_gain_part / attention_gain, back),
                rolled(feedforward_gain_part, back),
                lambda_full.reshape(-1),
                gain_full.reshape(-1),
            ]
        )
    )
    lambda_end = 2 * width + lambda_full.size
    return (
        rolled(block_output, back),
        rolled(tokens_grad, back),
        small[:width],
        qkv_weight_grad[:, :, :qk_width].reshape(query_weight.shape),
        qkv_weight_grad[:, :, qk_width : 2 * qk_width].reshape(key_weight.shape),
        qkv_weight_grad[:, :, 2 * qk_width :].reshape(value_weight.shape),
        output_grad.reshape(output_weight.shape),
        small[2 * width : lambda_end].reshape(lambda_full.shape),
        small[lambda_end:].reshape(gain_full.shape),
        small[width : 2 * width],
        gate_weight_grad,
        up_weight_grad,
        down_grad,
    )


def solution(mesh):
    placed = (
        P(("fsdp", "head", "tensor"), None),
        P("fsdp", None),
        P(),
        P("fsdp", "head", "tensor", None),
        P("fsdp", "head", "tensor", None),
        P("fsdp", "head", "tensor"),
        P("head", "tensor", "fsdp"),
        P(),
        P(),
        P(),
        P("fsdp", ("head", "tensor")),
        P("fsdp", ("head", "tensor")),
        P(("head", "tensor"), "fsdp"),
        P(("fsdp", "head", "tensor"), None),
    )
    return jax.shard_map(
        body,
        mesh=mesh,
        in_specs=placed,
        out_specs=(
            P(("fsdp", "head", "tensor"), None),
            P(("fsdp", "head", "tensor"), None),
            P(),
            P("fsdp", "head", "tensor", None),
            P("fsdp", "head", "tensor", None),
            P("fsdp", "head", "tensor"),
            P("head", "tensor", "fsdp"),
            P(),
            P(),
            P(),
            P("fsdp", ("head", "tensor")),
            P("fsdp", ("head", "tensor")),
            P(("head", "tensor"), "fsdp"),
        ),
        check_vma=False,
    )
```

```python
import functools

import jax
import jax.numpy as jnp
from jax import lax
from jax.experimental import pallas as pl
from jax.experimental.pallas import tpu as pltpu
from jax.sharding import PartitionSpec as P

lambda_base = 0.2
tile = 512
cost_share = 0.4
low = jnp.bfloat16


def contract(left_side, right_side, left_dim, right_dim):
    return lax.dot_general(
        left_side,
        right_side,
        (((left_dim,), (right_dim,)), ((), ())),
        preferred_element_type=jnp.float32,
    )


def after(values, *others):
    if not others:
        return values
    return lax.optimization_barrier((values, *others))[0]


def swap(values, axis, mask):
    size = lax.axis_size(axis)
    return lax.ppermute(values, axis, [(place, place ^ mask) for place in range(size)])


def fsdp_gather(own, axis, *others):
    return lax.all_gather(after(own, *others), "fsdp", axis=axis, tiled=True)


def fsdp_reduce(partial, axis):
    return lax.psum_scatter(partial, "fsdp", scatter_dimension=axis, tiled=True)


def shift(values, step):
    size = lax.axis_size("fsdp")
    return lax.ppermute(values, "fsdp", [(place, (place + step) % size) for place in range(size)])


def line_gather(own):
    size = lax.axis_size("fsdp")
    return [own] + [shift(own, -step) for step in range(1, size)]


def place_kernel(index, *refs):
    shards, out = refs[:-1], refs[-1]
    size, width = len(shards), shards[0].shape[1]
    for place, shard in enumerate(shards):
        to = lax.rem(index[0] + place, size) * width
        out[:, pl.ds(pl.multiple_of(to, width), width)] = shard[...]


def placed(shards):
    size = len(shards)
    rows, width = shards[0].shape
    vmem = pl.BlockSpec(memory_space=pltpu.VMEM)
    return pl.pallas_call(
        place_kernel,
        in_specs=[pl.BlockSpec(memory_space=pltpu.SMEM)] + [vmem] * size,
        out_specs=vmem,
        out_shape=jax.ShapeDtypeStruct((rows, size * width), low),
        cost_estimate=estimate(10**8),
        name="placed",
    )(lax.axis_index("fsdp")[None], *shards)


def add_low(left_side, right_side):
    return (left_side.astype(jnp.float32) + right_side.astype(jnp.float32)).astype(low)


def near_rows(own):
    return swap(own, "head", 1), swap(own, "head", 2)


def group_rows(own, near):
    half = own.shape[0] // 2
    first, second = near
    third_low = swap(second[:half], "head", 1)
    third_high = swap(first[half:], "head", 2)
    return jnp.concatenate([own, first, second, third_low, third_high], axis=0)


def join_kernel(start, near, to_first, to_second, first, second):
    rows = first.shape[0]
    half = rows // 2
    middle = start + rows
    first[:half] = near[start : start + half]
    first[half:] = add_low(near[start + half : middle], to_second[...])
    second[:half] = add_low(near[middle : middle + half], to_first[...])
    second[half:] = near[middle + half : middle + rows]


def group_reduce(near, start, third, own_part):
    rows, width = third.shape
    half = rows // 2
    to_first = swap(third[:half], "head", 1)
    to_second = swap(third[half:], "head", 2)
    own = own_part(to_first, to_second)
    vmem = pl.BlockSpec(memory_space=pltpu.VMEM)
    first, second = pl.pallas_call(
        functools.partial(join_kernel, start),
        in_specs=[vmem] * 3,
        out_specs=[vmem] * 2,
        out_shape=[jax.ShapeDtypeStruct((rows, width), low)] * 2,
        compiler_params=pltpu.CompilerParams(vmem_limit_bytes=24 * 2**20),
        cost_estimate=estimate(10**9),
        name="join",
    )(near, to_first, to_second)
    from_first = swap(first, "head", 1)
    from_second = swap(second, "head", 2)
    return (own, from_first, from_second), (first, second)


def summed(parts):
    return sum(part.astype(jnp.float32) for part in parts)


def total_over_all(values):
    for axis in ("tensor", "fsdp", "head"):
        mask = 1
        while mask < lax.axis_size(axis):
            values = values + swap(values, axis, mask)
            mask *= 2
    return values


def rolled(values, start):
    twice = jnp.concatenate([values, values], axis=-1)
    return lax.dynamic_slice_in_dim(twice, start, values.shape[-1], values.ndim - 1)


def slot_layout(lengths, slots):
    first_end = lengths[0, 0]
    second_end = first_end + lengths[0, 1]
    segment = (slots >= first_end).astype(jnp.int32) + (slots >= second_end).astype(jnp.int32)
    start = jnp.where(segment == 0, 0, jnp.where(segment == 1, first_end, second_end))
    return segment, slots - start


def estimate(flops):
    return pl.CostEstimate(
        flops=int(flops * cost_share), bytes_accessed=2**20, transcendentals=0
    )


def store_block(block, ints, values, kept, sent, columns):
    rows = values.shape[0]
    at = pl.ds(pl.multiple_of(((block >> 1) ^ ints[0]) * rows, rows), rows)

    @pl.when(ints[1] == (block & 1))
    def _():
        kept[at, columns] = values

    @pl.when(ints[1] != (block & 1))
    def _():
        sent[at, columns] = values


def row_starts(slots, first_end, second_end):
    return jnp.where(slots >= second_end, second_end, jnp.where(slots >= first_end, first_end, 0))


def attention_forward_kernel(
    ints,
    floats,
    kept_first,
    kept_second,
    received_first,
    received_second,
    gain,
    head_out_kept,
    head_out_sent,
    ordered,
    outs,
    log_totals,
):
    head_index, core, first_end, second_end = (ints[place] for place in range(4))
    rows = kept_first.shape[0] // 4
    slots = 8 * rows
    width = gain.shape[1]
    e = width // 2
    for parts, other in (
        ((kept_first, kept_second), 0),
        ((received_first, received_second), 1),
    ):
        for j in range(4):
            block = (head_index ^ j) * 2 + (core ^ other)
            at = pl.ds(pl.multiple_of(block * rows, rows), rows)
            for m in range(2):
                for kind in range(3):
                    to = (2 * kind + m) * e
                    ordered[at, to : to + e] = parts[m][
                        j * rows : (j + 1) * rows, kind * e : (kind + 1) * e
                    ]
    for start in range(0, slots, tile):
        stop = start + tile
        row = start + lax.broadcasted_iota(jnp.int32, (tile, 1), 0)
        begin = row_starts(row, first_end, second_end)
        value = ordered[:stop, 4 * e :]
        results = []
        for m in range(2):
            scores = contract(
                ordered[start:stop, m * e : (m + 1) * e],
                ordered[:stop, (2 + m) * e : (3 + m) * e],
                1,
                1,
            )
            column = lax.broadcasted_iota(jnp.int32, (tile, stop), 1)
            scores = jnp.where((column >= begin) & (column <= row), scores, -1e30)
            row_max = jnp.max(scores, axis=1, keepdims=True)
            expanded = jnp.exp(scores - row_max)
            row_total = jnp.sum(expanded, axis=1, keepdims=True)
            result = contract(expanded.astype(low), value, 1, 0) / row_total
            outs[m, start:stop, :] = result
            results.append(result)
            wide = jnp.broadcast_to(row_max + jnp.log(row_total), (tile, 128))
            log_totals[m : m + 1, start:stop] = jnp.transpose(wide)[:1]
        mixed = results[0] * floats[0] + results[1] * floats[1]
        scale = lax.rsqrt(jnp.mean(mixed * mixed, axis=1, keepdims=True) + 1e-05)
        normed = (mixed * scale * gain[...]).astype(low)
        for piece in range(tile // rows):
            store_block(
                start // rows + piece,
                ints,
                normed[piece * rows : (piece + 1) * rows],
                head_out_kept,
                head_out_sent,
                slice(None),
            )


def attention_forward(ints, floats, kept, received, gain):
    rows = kept[0].shape[0] // 4
    slots = 8 * rows
    width = gain.shape[1]
    vmem = pl.BlockSpec(memory_space=pltpu.VMEM)
    smem = pl.BlockSpec(memory_space=pltpu.SMEM)
    return pl.pallas_call(
        attention_forward_kernel,
        in_specs=[smem, smem] + [vmem] * 5,
        out_specs=[vmem] * 5,
        out_shape=[
            jax.ShapeDtypeStruct((slots // 2, width), low),
            jax.ShapeDtypeStruct((slots // 2, width), low),
            jax.ShapeDtypeStruct((slots, 3 * width), low),
            jax.ShapeDtypeStruct((2, slots, width), jnp.float32),
            jax.ShapeDtypeStruct((2, slots), jnp.float32),
        ],
        compiler_params=pltpu.CompilerParams(vmem_limit_bytes=40 * 2**20),
        cost_estimate=estimate(5 * 10**9),
        name="attention_forward",
    )(ints, floats, *kept, *received, gain)


def attention_backward_kernel(
    ints,
    floats,
    ordered,
    grads_kept,
    grads_received,
    outs,
    log_totals,
    gain,
    cosine,
    sine,
    kept_first,
    kept_second,
    sent_first,
    sent_second,
    gain_grad,
    lambda_grad,
    map_grads,
    deltas,
    query_grads,
    key_grads,
    value_grads,
):
    head_index, core, first_end, second_end = (ints[place] for place in range(4))
    rows = grads_kept.shape[0] // 4
    slots = 8 * rows
    width = gain.shape[1]
    e = width // 2
    gain_total = jnp.zeros((1, width), jnp.float32)
    lambda_total = jnp.zeros((1, width), jnp.float32)
    for part, other in ((grads_kept, 0), (grads_received, 1)):
        for j in range(4):
            block = (head_index ^ j) * 2 + (core ^ other)
            at = pl.ds(pl.multiple_of(block * rows, rows), rows)
            grad = part[j * rows : (j + 1) * rows, :].astype(jnp.float32)
            first, second = outs[0, at, :], outs[1, at, :]
            mixed = first * floats[0] + second * floats[1]
            scale = lax.rsqrt(jnp.mean(mixed * mixed, axis=1, keepdims=True) + 1e-05)
            gain_total += jnp.sum(grad * (mixed * scale), axis=0, keepdims=True)
            weighted = grad * gain[...]
            inner = jnp.mean(weighted * mixed, axis=1, keepdims=True)
            mixed_grad = scale * weighted - mixed * (scale * scale * scale * inner)
            lambda_total += jnp.sum(
                mixed_grad * jnp.where(core == 1, first, second), axis=0, keepdims=True
            )
            for m, out in ((0, first), (1, second)):
                map_grad = (mixed_grad * floats[m]).astype(low)
                map_grads[m, at, :] = map_grad
                delta = jnp.sum(map_grad.astype(jnp.float32) * out, axis=1, keepdims=True)
                deltas[m, :, at] = jnp.transpose(jnp.broadcast_to(delta, (rows, 128)))[:8]
    gain_grad[...] = gain_total * (1.0 - lambda_base)
    lambda_grad[...] = lambda_total
    query_grads[...] = jnp.zeros_like(query_grads)

    def pair(key_start, query_start, diagonal):
        at_keys = pl.ds(key_start, tile)
        at_queries = pl.ds(query_start, tile)
        column = query_start + lax.broadcasted_iota(jnp.int32, (1, tile), 1)
        begin = row_starts(column, first_end, second_end)
        row = key_start + lax.broadcasted_iota(jnp.int32, (tile, tile), 0)
        allowed = row >= begin
        if diagonal:
            allowed = allowed & (row <= column)
        value = ordered[at_keys, 4 * e :]
        for m in range(2):
            query = ordered[at_queries, m * e : (m + 1) * e]
            key = ordered[at_keys, (2 + m) * e : (3 + m) * e]
            map_grad = map_grads[m, at_queries, :]
            scores = contract(key, query, 1, 1)
            probability = jnp.where(
                allowed, jnp.exp(scores - log_totals[m : m + 1, at_queries]), 0.0
            )
            prob_grad = contract(value, map_grad, 1, 1)
            score_grad = (probability * (prob_grad - deltas[m, 0:1, at_queries])).astype(low)
            value_term = contract(probability.astype(low), map_grad, 1, 0)
            key_term = contract(score_grad, query, 1, 0)
            query_grads[m, at_queries, :] += contract(score_grad, key, 0, 0)
            if diagonal:
                key_grads[m, at_keys, :] = key_term
                if m == 0:
                    value_grads[at_keys, :] = value_term
                else:
                    value_grads[at_keys, :] += value_term
            else:
                key_grads[m, at_keys, :] += key_term
                value_grads[at_keys, :] += value_term

    for key_start in range(0, slots, tile):
        pair(key_start, key_start, True)

        def step(at, carry, key_start=key_start):
            pair(key_start, pl.multiple_of(at * tile, tile), False)
            return carry

        lax.fori_loop(key_start // tile + 1, slots // tile, step, 0)

    def turn_back(values, at):
        return values * cosine[at, :] - pltpu.roll(values, e // 2, 1) * sine[at, :]

    for block in range(8):
        at = slice(block * rows, (block + 1) * rows)
        for m, kept, sent in ((0, kept_first, sent_first), (1, kept_second, sent_second)):
            query = (turn_back(query_grads[m, at, :], at) * e ** (-0.5)).astype(low)
            key = turn_back(key_grads[m, at, :], at).astype(low)
            value = value_grads[at, m * e : (m + 1) * e].astype(low)
            store_block(
                block, ints, jnp.concatenate([query, key, value], axis=1), kept, sent, slice(None)
            )


def attention_backward(
    ints, floats, ordered, grads_kept, grads_received, outs, log_totals, gain, cosine, sine
):
    slots, width = outs.shape[1:]
    vmem = pl.BlockSpec(memory_space=pltpu.VMEM)
    smem = pl.BlockSpec(memory_space=pltpu.SMEM)
    return pl.pallas_call(
        attention_backward_kernel,
        in_specs=[smem, smem] + [vmem] * 8,
        out_specs=[vmem] * 6,
        out_shape=[jax.ShapeDtypeStruct((slots // 2, 3 * width // 2), low)] * 4
        + [jax.ShapeDtypeStruct((1, width), jnp.float32)] * 2,
        scratch_shapes=[
            pltpu.VMEM((2, slots, width), low),
            pltpu.VMEM((2, 8, slots), jnp.float32),
            pltpu.VMEM((2, slots, width // 2), jnp.float32),
            pltpu.VMEM((2, slots, width // 2), jnp.float32),
            pltpu.VMEM((slots, width), jnp.float32),
        ],
        compiler_params=pltpu.CompilerParams(vmem_limit_bytes=48 * 2**20),
        cost_estimate=estimate(20 * 10**9),
        name="attention_backward",
    )(ints, floats, ordered, grads_kept, grads_received, outs, log_totals, gain, cosine, sine)


def norm_back_kernel(one, two, three, values, gain, added, out, out_low, gain_grad):
    wide = values[...].astype(jnp.float32)
    grad = (
        one[...].astype(jnp.float32) + two[...].astype(jnp.float32) + three[...].astype(jnp.float32)
    )
    scale = lax.rsqrt(jnp.mean(wide * wide, axis=1, keepdims=True) + 1e-06)
    gained = grad * gain[...]
    inner = jnp.mean(gained * wide, axis=1, keepdims=True)
    result = added[...] + scale * gained - wide * (scale * scale * scale * inner)
    out[...] = result
    out_low[...] = result.astype(low)

    @pl.when(pl.program_id(0) == 0)
    def _():
        gain_grad[...] = jnp.zeros_like(gain_grad)

    gain_grad[...] += jnp.sum(grad * (wide * scale), axis=0, keepdims=True)


def norm_back(parts, values, gain, added):
    rows, width = values.shape
    block = rows // 4
    down = pl.BlockSpec((block, width), lambda i: (i, 0))
    once = pl.BlockSpec((1, width), lambda i: (0, 0))
    return pl.pallas_call(
        norm_back_kernel,
        grid=(4,),
        in_specs=[down] * 4 + [once, down],
        out_specs=[down, down, once],
        out_shape=[
            jax.ShapeDtypeStruct((rows, width), jnp.float32),
            jax.ShapeDtypeStruct((rows, width), low),
            jax.ShapeDtypeStruct((1, width), jnp.float32),
        ],
        compiler_params=pltpu.CompilerParams(vmem_limit_bytes=24 * 2**20),
        cost_estimate=estimate(10**9),
        name="norm_back",
    )(*parts, values, gain[None], added)


def project_kernel(inputs, weight, cosine, sine, first, second):
    e = cosine.shape[1]
    product = contract(inputs[...], weight[...], 1, 0)

    def turned(start):
        part = product[:, start : start + e]
        return part * cosine[...] + pltpu.roll(part, e // 2, 1) * sine[...]

    for out, start in ((first, 0), (second, 3 * e)):
        out[:, :e] = (turned(start) * e ** (-0.5)).astype(low)
        out[:, e : 2 * e] = turned(start + e).astype(low)
        out[:, 2 * e :] = product[:, start + 2 * e : start + 3 * e].astype(low)


def project(inputs, weight, cosine, sine):
    slots, width = inputs.shape
    columns = weight.shape[1]
    block = slots // 4
    down = lambda size: pl.BlockSpec((block, size), lambda i: (i, 0))
    return pl.pallas_call(
        project_kernel,
        grid=(4,),
        in_specs=[
            down(width),
            pl.BlockSpec((width, columns), lambda i: (0, 0)),
            down(cosine.shape[1]),
            down(cosine.shape[1]),
        ],
        out_specs=[down(columns // 2)] * 2,
        out_shape=[jax.ShapeDtypeStruct((slots, columns // 2), low)] * 2,
        compiler_params=pltpu.CompilerParams(vmem_limit_bytes=32 * 2**20),
        cost_estimate=estimate(2 * slots * width * columns),
        name="project",
    )(inputs, weight, cosine, sine)


def project_back_kernel(one, two, three, four, own, other, normed, out, gain):
    half = one.shape[1]
    total = contract(one[...], own[:, :half], 1, 1)
    total += contract(two[...], own[:, half:], 1, 1)
    total += contract(three[...], other[:, :half], 1, 1)
    total += contract(four[...], other[:, half:], 1, 1)
    out[...] = total.astype(low)
    part = jnp.sum(total * normed[...].astype(jnp.float32), axis=0, keepdims=True)

    @pl.when(pl.program_id(0) == 0)
    def _():
        gain[...] = jnp.zeros_like(gain)

    gain[...] += part


def project_back(parts, own, other, normed, first, count, rows):
    width, columns = own.shape
    down = lambda size: pl.BlockSpec((rows, size), lambda i: (first + i, 0))
    whole = pl.BlockSpec((width, columns), lambda i: (0, 0))
    return pl.pallas_call(
        project_back_kernel,
        grid=(count,),
        in_specs=[down(columns // 2)] * 4 + [whole, whole, down(width)],
        out_specs=[
            pl.BlockSpec((rows, width), lambda i: (i, 0)),
            pl.BlockSpec((1, width), lambda i: (0, 0)),
        ],
        out_shape=[
            jax.ShapeDtypeStruct((count * rows, width), low),
            jax.ShapeDtypeStruct((1, width), jnp.float32),
        ],
        compiler_params=pltpu.CompilerParams(vmem_limit_bytes=40 * 2**20),
        cost_estimate=estimate(4 * count * rows * width * columns),
        name="project_back",
    )(*parts, own, other, normed)


def gate_kernel(inputs, gate, up, hidden, gate_factor, up_factor):
    gate_pre = contract(gate[...], inputs[...], 1, 1)
    upward = contract(up[...], inputs[...], 1, 1)
    sigmoid = 1.0 / (1.0 + jnp.exp(-gate_pre))
    silu = gate_pre * sigmoid
    hidden[...] = (silu * upward).astype(low)
    gate_factor[...] = (upward * (sigmoid * (1.0 + gate_pre * (1.0 - sigmoid)))).astype(low)
    up_factor[...] = silu.astype(low)


def gate_units(inputs, gate, up):
    slots, width = inputs.shape
    units = gate.shape[0]
    block = slots // 4
    whole = pl.BlockSpec((units, width), lambda i: (0, 0))
    across = pl.BlockSpec((units, block), lambda i: (0, i))
    return pl.pallas_call(
        gate_kernel,
        grid=(4,),
        in_specs=[pl.BlockSpec((block, width), lambda i: (i, 0)), whole, whole],
        out_specs=[across] * 3,
        out_shape=[jax.ShapeDtypeStruct((units, slots), low)] * 3,
        compiler_params=pltpu.CompilerParams(vmem_limit_bytes=40 * 2**20),
        cost_estimate=estimate(4 * slots * width * units),
        name="gate_units",
    )(inputs, gate, up)


def gate_grad_kernel(grads, down, gate_factor, up_factor, gate_grad, up_grad):
    hidden_grad = contract(down[...], grads[...], 1, 1)
    gate_grad[...] = (hidden_grad * gate_factor[...].astype(jnp.float32)).astype(low)
    up_grad[...] = (hidden_grad * up_factor[...].astype(jnp.float32)).astype(low)


def gate_grads(grads, down, gate_factor, up_factor):
    slots, width = grads.shape
    units = down.shape[0]
    block = slots // 4
    across = pl.BlockSpec((units, block), lambda i: (0, i))
    return pl.pallas_call(
        gate_grad_kernel,
        grid=(4,),
        in_specs=[
            pl.BlockSpec((block, width), lambda i: (i, 0)),
            pl.BlockSpec((units, width), lambda i: (0, 0)),
            across,
            across,
        ],
        out_specs=[across] * 2,
        out_shape=[jax.ShapeDtypeStruct((units, slots), low)] * 2,
        compiler_params=pltpu.CompilerParams(vmem_limit_bytes=40 * 2**20),
        cost_estimate=estimate(2 * slots * width * units),
        name="gate_grads",
    )(grads, down, gate_factor, up_factor)


def sum_kernel(terms, *refs):
    out = refs[-1]
    total = contract(refs[0][...], refs[terms][...], 0, 0)
    for place in range(1, terms):
        total += contract(refs[place][...], refs[terms + place][...], 0, 0)
    out[...] = total.astype(out.dtype)


def sum_over_units(factors, weights, first, count, rows):
    units, width = weights[0].shape
    terms = len(factors)
    return pl.pallas_call(
        functools.partial(sum_kernel, terms),
        grid=(count,),
        in_specs=[pl.BlockSpec((units, rows), lambda i: (0, first + i))] * terms
        + [pl.BlockSpec((units, width), lambda i: (0, 0))] * terms,
        out_specs=pl.BlockSpec((rows, width), lambda i: (i, 0)),
        out_shape=jax.ShapeDtypeStruct((count * rows, width), low),
        compiler_params=pltpu.CompilerParams(vmem_limit_bytes=48 * 2**20),
        cost_estimate=estimate(2 * count * rows * width * units * terms),
        name="sum_over_units",
    )(*factors, *weights)


def body(
    tokens,
    lengths,
    attention_gain,
    query_weight,
    key_weight,
    value_weight,
    output_weight,
    lambda_vectors,
    head_gain,
    feedforward_gain,
    gate_weight,
    up_weight,
    down_weight,
    cotangent,
):
    rows, width = tokens.shape
    head_index = lax.axis_index("head")
    core = lax.axis_index("tensor")
    shard = query_weight.shape[0]
    qk_width = query_weight.shape[3]
    value_half = value_weight.shape[2]
    slots = rows * 8

    def in_order(mine, other):
        return jnp.where(core == 0, mine, other), jnp.where(core == 0, other, mine)

    own_slots = (
        (jnp.arange(4, dtype=jnp.int32) ^ head_index)[:, None] * (2 * rows)
        + core * rows
        + jnp.arange(rows, dtype=jnp.int32)[None, :]
    ).reshape(-1)
    segment_own, position_own = slot_layout(lengths, own_slots)
    valid = (segment_own[:rows] < 2).astype(jnp.float32)[:, None]
    half_width = qk_width // 2
    frequency = 10000.0 ** (-jnp.arange(half_width, dtype=jnp.float32) / half_width)

    def turn_tables(positions):
        angles = positions.astype(jnp.float32)[:, None] * frequency[None, :]
        cosine, sine = jnp.cos(angles), jnp.sin(angles)
        return jnp.concatenate([cosine, cosine], axis=1), jnp.concatenate([-sine, sine], axis=1)

    cosine, sine = turn_tables(position_own)
    cosine_all, sine_all = turn_tables(
        slot_layout(lengths, jnp.arange(slots, dtype=jnp.int32))[1]
    )
    own_head = head_index * 2 + core
    vectors = lax.dynamic_slice_in_dim(lambda_vectors, own_head, 1, 0)[0]
    first_exp = jnp.exp(jnp.sum(vectors[0] * vectors[1]))
    second_exp = jnp.exp(jnp.sum(vectors[2] * vectors[3]))
    lambda_value = first_exp - second_exp + lambda_base
    floats = jnp.stack(in_order(1.0, -lambda_value))
    ints = jnp.stack([head_index, core, lengths[0, 0], lengths[0, 0] + lengths[0, 1]])
    gain_own = rolled(
        lax.dynamic_slice_in_dim(head_gain, own_head, 1, 0), core * value_half
    ) * (1.0 - lambda_base)

    tokens_wide = tokens.astype(jnp.float32)
    attention_scale = lax.rsqrt(jnp.mean(tokens_wide * tokens_wide, axis=-1, keepdims=True) + 1e-06)
    normed_own = (tokens_wide * attention_scale * attention_gain).astype(low)
    output_local = jnp.concatenate(in_order(output_weight[0], output_weight[1]), axis=0)
    output_shards = line_gather(output_local)
    ffn_out_grad = valid * cotangent.astype(jnp.float32)
    ffn_out_grad_own = ffn_out_grad.astype(low)
    normed_near = [
        after(
            near,
            *(cosine, sine, cosine_all, sine_all),
            *(ffn_out_grad_own, ints, floats, gain_own, *output_shards),
        )
        for near in near_rows(normed_own)
    ]
    normed = group_rows(normed_own, normed_near)

    third = 3 * qk_width
    heads = [
        jnp.concatenate(
            [
                weight[:, place].reshape(shard, -1)
                for weight in (query_weight, key_weight, value_weight)
            ],
            axis=1,
        )
        for place in range(2)
    ]
    qkv_own = after(fsdp_gather(jnp.concatenate(in_order(*heads), axis=1), 0), normed)
    qkv_other = swap(qkv_own, "tensor", 1)
    gate_own = fsdp_gather(jnp.transpose(gate_weight), 1)
    up_own = fsdp_gather(jnp.transpose(up_weight), 1, normed)

    ffn_out_grad_own = after(ffn_out_grad_own, normed)
    ffn_out_grad_near = near_rows(ffn_out_grad_own)
    output_own = placed(output_shards)
    kept_first, sent_second = project(after(normed, output_own), qkv_own, cosine, sine)
    sent_first, kept_second = project(after(normed, kept_first), qkv_other, cosine, sine)
    ffn_out_grad_near = [after(near, sent_first) for near in ffn_out_grad_near]
    output_all = jnp.concatenate(
        [output_own, swap(after(output_own, sent_first), "tensor", 1)], axis=0
    )
    kept, sent, ordered, outs, log_totals = attention_forward(
        ints,
        floats,
        (after(kept_first, *ffn_out_grad_near), kept_second),
        (swap(sent_first, "tensor", 1), swap(sent_second, "tensor", 1)),
        gain_own,
    )
    received = swap(sent, "tensor", 1)
    head_out = jnp.concatenate(
        [
            kept[:, :value_half],
            received[:, value_half:],
            received[:, :value_half],
            kept[:, value_half:],
        ],
        axis=1,
    )

    ffn_out_grad_all = group_rows(ffn_out_grad_own, ffn_out_grad_near)
    third_out = contract(head_out[3 * rows :], output_all, 1, 0).astype(low)
    third_out = after(third_out, ffn_out_grad_all)
    down_own = fsdp_gather(down_weight, 1, third_out)
    nearer_out = contract(after(head_out, third_out)[: 3 * rows], output_all, 1, 0).astype(low)
    attention_out, _ = group_reduce(
        nearer_out,
        rows,
        third_out,
        lambda *arrived: nearer_out[:rows],
    )
    residual = tokens_wide + summed([after(part, gate_own) for part in attention_out])
    ffn_scale = lax.rsqrt(jnp.mean(residual * residual, axis=-1, keepdims=True) + 1e-06)
    ffn_in_own = (residual * ffn_scale * feedforward_gain).astype(low)
    ffn_in_near = near_rows(ffn_in_own)
    ffn_in = group_rows(ffn_in_own, ffn_in_near)
    gate_own, up_own = after(gate_own, ffn_in), after(up_own, ffn_in)
    gate_other, up_other = swap(gate_own, "tensor", 1), swap(up_own, "tensor", 1)
    hidden_own, gate_factor_own, up_factor_own = gate_units(ffn_in, gate_own, up_own)
    hidden_other, gate_factor_other, up_factor_other = gate_units(
        after(ffn_in, hidden_own), gate_other, up_other
    )

    down_own = after(down_own, hidden_other)
    down_other = swap(down_own, "tensor", 1)

    def weight_grad(own_side, other_side, right_side, *events):
        other = contract(other_side, right_side, 1, 0).astype(low)
        own = contract(after(own_side, other, *events), right_side, 1, 0)
        total = add_low(own, swap(other, "tensor", 1))
        return total, fsdp_reduce(total, 1)

    down_terms, down_grad = weight_grad(hidden_own, hidden_other, ffn_out_grad_all)
    gate_grad_own, up_grad_own = gate_grads(
        after(ffn_out_grad_all, down_terms), down_own, gate_factor_own, up_factor_own
    )
    gate_grad_other, up_grad_other = gate_grads(
        ffn_out_grad_all, down_other, gate_factor_other, up_factor_other
    )
    factors = [gate_grad_own, up_grad_own, gate_grad_other, up_grad_other]
    weights = [gate_own, up_own, gate_other, up_other]
    third_grad = sum_over_units(factors, weights, 3, 1, rows)
    gate_other_part = contract(after(gate_grad_other, third_grad), ffn_in, 1, 0).astype(low)
    near_grad = sum_over_units(
        [after(factors[0], gate_other_part)] + factors[1:], weights, 1, 2, rows
    )
    gate_terms = add_low(
        contract(after(gate_grad_own, near_grad), ffn_in, 1, 0),
        swap(gate_other_part, "tensor", 1),
    )
    gate_weight_grad = fsdp_reduce(gate_terms, 1)
    own_grads = []

    def own_grad(*arrived):
        own_grads.append(
            sum_over_units(
                [after(factors[0], gate_terms, down_grad, *arrived)] + factors[1:],
                weights,
                0,
                1,
                rows,
            )
        )
        return own_grads[0]

    ffn_in_sum, near_sent = group_reduce(near_grad, 0, third_grad, own_grad)
    up_terms, up_weight_grad = weight_grad(
        after(up_grad_own, own_grads[0]), after(up_grad_other, own_grads[0], *near_sent), ffn_in
    )
    residual_grad, residual_grad_low, feedforward_gain_part = norm_back(
        [after(part, up_terms) for part in ffn_in_sum],
        residual,
        feedforward_gain,
        ffn_out_grad,
    )
    feedforward_gain_part = feedforward_gain_part[0]

    ffn_out = sum_over_units(
        [after(hidden_own, residual_grad_low), hidden_other], [down_own, down_other], 0, 4, rows
    )
    residual_grad_near = [
        after(near, ffn_out, gate_weight_grad) for near in near_rows(residual_grad_low)
    ]
    attention_out_grad = group_rows(residual_grad_low, residual_grad_near)
    output_terms = contract(head_out, attention_out_grad, 0, 0).astype(low)
    head_out_grad = contract(after(attention_out_grad, output_terms), output_all, 1, 1).astype(low)
    pieces = [
        head_out_grad[:, place * value_half : (place + 1) * value_half] for place in range(4)
    ]
    ffn_arrived = []

    def ffn_own(*arrived):
        ffn_arrived.extend(arrived)
        return ffn_out[:rows]

    ffn_here, _ = group_reduce(
        ffn_out,
        rows,
        after(ffn_out[3 * rows :], attention_out_grad),
        ffn_own,
    )
    output_sum = add_low(
        output_terms[: 2 * value_half], swap(output_terms[2 * value_half :], "tensor", 1)
    )
    output_grad = fsdp_reduce(output_sum, 1)
    kept_first, kept_second, sent_first, sent_second, head_gain_part, lambda_part = (
        attention_backward(
            ints,
            floats,
            ordered,
            after(jnp.concatenate([pieces[0], pieces[3]], axis=1), output_sum, up_weight_grad),
            swap(jnp.concatenate([pieces[2], pieces[1]], axis=1), "tensor", 1),
            outs,
            log_totals,
            gain_own,
            cosine_all,
            sine_all,
        )
    )

    received_first = swap(after(sent_first, *ffn_arrived, output_grad), "tensor", 1)
    received_second = swap(sent_second, "tensor", 1)
    others_second = contract(normed, kept_second, 0, 0).astype(low)
    others_first = contract(after(normed, others_second), received_first, 0, 0).astype(low)
    parts = (kept_first, received_second, received_first, kept_second)
    own_first = add_low(
        contract(after(normed, others_first), kept_first, 0, 0), swap(others_first, "tensor", 1)
    )
    own_second = add_low(
        contract(after(normed, others_first), received_second, 0, 0),
        swap(others_second, "tensor", 1),
    )
    third_terms, third_gain = project_back(
        (after(kept_first, own_first, own_second, output_grad),) + parts[1:],
        qkv_own,
        qkv_other,
        normed,
        3,
        1,
        rows,
    )
    qkv_weight_grad = in_order(
        fsdp_reduce(own_first, 0).astype(jnp.float32),
        fsdp_reduce(own_second, 0).astype(jnp.float32),
    )
    output_grad = output_grad.astype(jnp.float32)
    output_grad = jnp.stack(in_order(output_grad[:value_half], output_grad[value_half:]))
    nearer_terms, nearer_gain = project_back(
        (after(kept_first, third_terms, own_first, own_second),) + parts[1:],
        qkv_own,
        qkv_other,
        normed,
        0,
        3,
        rows,
    )
    normed_grad, _ = group_reduce(
        nearer_terms,
        rows,
        after(third_terms, *ffn_here),
        lambda *arrived: nearer_terms[:rows],
    )
    attention_gain_part = (third_gain + nearer_gain)[0]
    ffn_here = [after(part, nearer_gain) for part in ffn_here]
    block_output = (valid * (residual + summed(ffn_here))).astype(low)
    tokens_grad, _, _ = norm_back(normed_grad, tokens, attention_gain, residual_grad)

    lambda_grad = -jnp.sum(lambda_part)
    vector_grads = lambda_grad * jnp.stack(
        [
            first_exp * vectors[1],
            first_exp * vectors[0],
            -second_exp * vectors[3],
            -second_exp * vectors[2],
        ]
    )
    lambda_full = lax.dynamic_update_slice(
        jnp.zeros(lambda_vectors.shape, jnp.float32), vector_grads[None], (own_head, 0, 0)
    )
    gain_full = lax.dynamic_update_slice(
        jnp.zeros(head_gain.shape, jnp.float32),
        rolled(head_gain_part, core * value_half),
        (own_head, 0),
    )
    small = total_over_all(
        jnp.concatenate(
            [
                attention_gain_part / attention_gain,
                feedforward_gain_part,
                lambda_full.reshape(-1),
                gain_full.reshape(-1),
            ]
        )
    )
    lambda_end = 2 * width + lambda_full.size
    return (
        block_output,
        tokens_grad,
        small[:width],
        *(
            jnp.stack(
                [part[:, kind * qk_width : (kind + 1) * qk_width] for part in qkv_weight_grad],
                axis=1,
            ).reshape(weight.shape)
            for kind, weight in enumerate((query_weight, key_weight, value_weight))
        ),
        output_grad.reshape(output_weight.shape),
        small[2 * width : lambda_end].reshape(lambda_full.shape),
        small[lambda_end:].reshape(gain_full.shape),
        small[width : 2 * width],
        jnp.transpose(gate_weight_grad).astype(jnp.float32),
        jnp.transpose(up_weight_grad).astype(jnp.float32),
        down_grad.astype(jnp.float32),
    )


def solution(mesh):
    placed = (
        P(("fsdp", "head", "tensor"), None),
        P("fsdp", None),
        P(),
        P("fsdp", "head", "tensor", None),
        P("fsdp", "head", "tensor", None),
        P("fsdp", "head", "tensor"),
        P("head", "tensor", "fsdp"),
        P(),
        P(),
        P(),
        P("fsdp", ("head", "tensor")),
        P("fsdp", ("head", "tensor")),
        P(("head", "tensor"), "fsdp"),
        P(("fsdp", "head", "tensor"), None),
    )
    return jax.shard_map(
        body,
        mesh=mesh,
        in_specs=placed,
        out_specs=(
            P(("fsdp", "head", "tensor"), None),
            P(("fsdp", "head", "tensor"), None),
            P(),
            P("fsdp", "head", "tensor", None),
            P("fsdp", "head", "tensor", None),
            P("fsdp", "head", "tensor"),
            P("head", "tensor", "fsdp"),
            P(),
            P(),
            P(),
            P("fsdp", ("head", "tensor")),
            P("fsdp", ("head", "tensor")),
            P(("head", "tensor"), "fsdp"),
        ),
        check_vma=False,
    )
```

```python
import functools

import jax
import jax.numpy as jnp
from jax import lax
from jax.experimental import pallas as pl
from jax.experimental.pallas import tpu as pltpu
from jax.sharding import PartitionSpec as P

lambda_base = 0.2
tile = 512
cost_share = 0.02
low = jnp.bfloat16


def contract(left_side, right_side, left_dim, right_dim):
    return lax.dot_general(
        left_side,
        right_side,
        (((left_dim,), (right_dim,)), ((), ())),
        preferred_element_type=jnp.float32,
    )


def after(values, *others):
    if not others:
        return values
    return lax.optimization_barrier((values, *others))[0]


def swap(values, axis, mask):
    size = lax.axis_size(axis)
    return lax.ppermute(values, axis, [(place, place ^ mask) for place in range(size)])


def fsdp_gather(own, axis, *others):
    return lax.all_gather(after(own, *others), "fsdp", axis=axis, tiled=True)


def fsdp_reduce(partial, axis):
    return lax.psum_scatter(partial, "fsdp", scatter_dimension=axis, tiled=True)


def shift(values, step):
    size = lax.axis_size("fsdp")
    return lax.ppermute(values, "fsdp", [(place, (place + step) % size) for place in range(size)])


def line_gather(own):
    size = lax.axis_size("fsdp")
    return [own] + [shift(own, -step) for step in range(1, size)]


def place_kernel(index, *refs):
    shards, out = refs[:-1], refs[-1]
    size, width = len(shards), shards[0].shape[1]
    for place, shard in enumerate(shards):
        to = lax.rem(index[0] + place, size) * width
        out[:, pl.ds(pl.multiple_of(to, width), width)] = shard[...]


def placed(shards):
    size = len(shards)
    rows, width = shards[0].shape
    vmem = pl.BlockSpec(memory_space=pltpu.VMEM)
    return pl.pallas_call(
        place_kernel,
        in_specs=[pl.BlockSpec(memory_space=pltpu.SMEM)] + [vmem] * size,
        out_specs=vmem,
        out_shape=jax.ShapeDtypeStruct((rows, size * width), low),
        cost_estimate=estimate(10**8),
        name="placed",
    )(lax.axis_index("fsdp")[None], *shards)


def add_low(left_side, right_side):
    return (left_side.astype(jnp.float32) + right_side.astype(jnp.float32)).astype(low)


def near_rows(own):
    return swap(own, "head", 1), swap(own, "head", 2)


def group_rows(own, near, *events):
    half = own.shape[0] // 2
    first, second = near
    third_low = swap(second[:half], "head", 1)
    third_high = swap(first[half:], "head", 2)
    far = [after(part, *events) for part in (third_low, third_high)]
    return jnp.concatenate([after(own, *events), first, second, *far], axis=0)


def join_kernel(start, near, to_first, to_second, first, second):
    rows = first.shape[0]
    half = rows // 2
    middle = start + rows
    first[:half] = near[start : start + half]
    first[half:] = add_low(near[start + half : middle], to_second[...])
    second[:half] = add_low(near[middle : middle + half], to_first[...])
    second[half:] = near[middle + half : middle + rows]


def group_reduce(near, start, halves, own_part, hold=()):
    half, width = halves[0].shape
    rows = 2 * half
    to_first = swap(halves[0], "head", 1)
    to_second = swap(halves[1], "head", 2)
    own = own_part(to_first, to_second)
    vmem = pl.BlockSpec(memory_space=pltpu.VMEM)
    first, second = pl.pallas_call(
        functools.partial(join_kernel, start),
        in_specs=[vmem] * 3,
        out_specs=[vmem] * 2,
        out_shape=[jax.ShapeDtypeStruct((rows, width), low)] * 2,
        compiler_params=pltpu.CompilerParams(vmem_limit_bytes=24 * 2**20),
        cost_estimate=estimate(10**9),
        name="join",
    )(after(near, *hold), to_first, to_second)
    from_first = swap(first, "head", 1)
    from_second = swap(second, "head", 2)
    return (own, from_first, from_second), (first, second)


def summed(parts):
    return sum(part.astype(jnp.float32) for part in parts)


def total_over_all(values):
    for axis in ("tensor", "fsdp", "head"):
        mask = 1
        while mask < lax.axis_size(axis):
            values = values + swap(values, axis, mask)
            mask *= 2
    return values


def rolled(values, start):
    twice = jnp.concatenate([values, values], axis=-1)
    return lax.dynamic_slice_in_dim(twice, start, values.shape[-1], values.ndim - 1)


def slot_layout(lengths, slots):
    first_end = lengths[0, 0]
    second_end = first_end + lengths[0, 1]
    segment = (slots >= first_end).astype(jnp.int32) + (slots >= second_end).astype(jnp.int32)
    start = jnp.where(segment == 0, 0, jnp.where(segment == 1, first_end, second_end))
    return segment, slots - start


def store_parts(values, outs):
    size = values.shape[0] // len(outs)
    for place, out in enumerate(outs):
        out[...] = values[place * size : (place + 1) * size].astype(out.dtype)


def estimate(flops):
    return pl.CostEstimate(
        flops=int(flops * cost_share), bytes_accessed=2**20, transcendentals=0
    )


def store_block(block, ints, values, kept, sent, columns):
    rows = values.shape[0]
    at = pl.ds(pl.multiple_of(((block >> 1) ^ ints[0]) * rows, rows), rows)

    @pl.when(ints[1] == (block & 1))
    def _():
        kept[at, columns] = values

    @pl.when(ints[1] != (block & 1))
    def _():
        sent[at, columns] = values


def row_starts(slots, first_end, second_end):
    return jnp.where(slots >= second_end, second_end, jnp.where(slots >= first_end, first_end, 0))


def attention_forward_kernel(
    ints,
    floats,
    kept_first,
    kept_second,
    received_first,
    received_second,
    gain,
    head_out_kept,
    head_out_sent,
    ordered,
    outs,
    log_totals,
):
    head_index, core, first_end, second_end = (ints[place] for place in range(4))
    rows = kept_first.shape[0] // 4
    slots = 8 * rows
    width = gain.shape[1]
    e = width // 2
    for parts, other in (
        ((kept_first, kept_second), 0),
        ((received_first, received_second), 1),
    ):
        for j in range(4):
            block = (head_index ^ j) * 2 + (core ^ other)
            at = pl.ds(pl.multiple_of(block * rows, rows), rows)
            for m in range(2):
                for kind in range(3):
                    to = (2 * kind + m) * e
                    ordered[at, to : to + e] = parts[m][
                        j * rows : (j + 1) * rows, kind * e : (kind + 1) * e
                    ]
    for start in range(0, slots, tile):
        stop = start + tile
        row = start + lax.broadcasted_iota(jnp.int32, (tile, 1), 0)
        begin = row_starts(row, first_end, second_end)
        value = ordered[:stop, 4 * e :]
        results = []
        for m in range(2):
            scores = contract(
                ordered[start:stop, m * e : (m + 1) * e],
                ordered[:stop, (2 + m) * e : (3 + m) * e],
                1,
                1,
            )
            column = lax.broadcasted_iota(jnp.int32, (tile, stop), 1)
            scores = jnp.where((column >= begin) & (column <= row), scores, -1e30)
            row_max = jnp.max(scores, axis=1, keepdims=True)
            expanded = jnp.exp(scores - row_max)
            row_total = jnp.sum(expanded, axis=1, keepdims=True)
            result = contract(expanded.astype(low), value, 1, 0) / row_total
            outs[m, start:stop, :] = result
            results.append(result)
            wide = jnp.broadcast_to(row_max + jnp.log(row_total), (tile, 128))
            log_totals[m : m + 1, start:stop] = jnp.transpose(wide)[:1]
        mixed = results[0] * floats[0] + results[1] * floats[1]
        scale = lax.rsqrt(jnp.mean(mixed * mixed, axis=1, keepdims=True) + 1e-05)
        normed = (mixed * scale * gain[...]).astype(low)
        for piece in range(tile // rows):
            store_block(
                start // rows + piece,
                ints,
                normed[piece * rows : (piece + 1) * rows],
                head_out_kept,
                head_out_sent,
                slice(None),
            )


def attention_forward(ints, floats, kept, received, gain):
    rows = kept[0].shape[0] // 4
    slots = 8 * rows
    width = gain.shape[1]
    vmem = pl.BlockSpec(memory_space=pltpu.VMEM)
    smem = pl.BlockSpec(memory_space=pltpu.SMEM)
    return pl.pallas_call(
        attention_forward_kernel,
        in_specs=[smem, smem] + [vmem] * 5,
        out_specs=[vmem] * 5,
        out_shape=[
            jax.ShapeDtypeStruct((slots // 2, width), low),
            jax.ShapeDtypeStruct((slots // 2, width), low),
            jax.ShapeDtypeStruct((slots, 3 * width), low),
            jax.ShapeDtypeStruct((2, slots, width), jnp.float32),
            jax.ShapeDtypeStruct((2, slots), jnp.float32),
        ],
        compiler_params=pltpu.CompilerParams(vmem_limit_bytes=40 * 2**20),
        cost_estimate=estimate(5 * 10**9),
        name="attention_forward",
    )(ints, floats, *kept, *received, gain)


def attention_backward_kernel(
    ints,
    floats,
    ordered,
    grads_kept,
    grads_received,
    outs,
    log_totals,
    gain,
    cosine,
    sine,
    kept_first,
    kept_second,
    sent_first,
    sent_second,
    gain_grad,
    lambda_grad,
    map_grads,
    deltas,
    query_grads,
    key_grads,
    value_grads,
):
    head_index, core, first_end, second_end = (ints[place] for place in range(4))
    rows = grads_kept.shape[0] // 4
    slots = 8 * rows
    width = gain.shape[1]
    e = width // 2
    gain_total = jnp.zeros((1, width), jnp.float32)
    lambda_total = jnp.zeros((1, width), jnp.float32)
    for part, other in ((grads_kept, 0), (grads_received, 1)):
        for j in range(4):
            block = (head_index ^ j) * 2 + (core ^ other)
            at = pl.ds(pl.multiple_of(block * rows, rows), rows)
            grad = part[j * rows : (j + 1) * rows, :].astype(jnp.float32)
            first, second = outs[0, at, :], outs[1, at, :]
            mixed = first * floats[0] + second * floats[1]
            scale = lax.rsqrt(jnp.mean(mixed * mixed, axis=1, keepdims=True) + 1e-05)
            gain_total += jnp.sum(grad * (mixed * scale), axis=0, keepdims=True)
            weighted = grad * gain[...]
            inner = jnp.mean(weighted * mixed, axis=1, keepdims=True)
            mixed_grad = scale * weighted - mixed * (scale * scale * scale * inner)
            lambda_total += jnp.sum(
                mixed_grad * jnp.where(core == 1, first, second), axis=0, keepdims=True
            )
            for m, out in ((0, first), (1, second)):
                map_grad = (mixed_grad * floats[m]).astype(low)
                map_grads[m, at, :] = map_grad
                delta = jnp.sum(map_grad.astype(jnp.float32) * out, axis=1, keepdims=True)
                deltas[m, :, at] = jnp.transpose(jnp.broadcast_to(delta, (rows, 128)))[:8]
    gain_grad[...] = gain_total * (1.0 - lambda_base)
    lambda_grad[...] = lambda_total
    query_grads[...] = jnp.zeros_like(query_grads)

    def pair(key_start, query_start, diagonal):
        at_keys = pl.ds(key_start, tile)
        at_queries = pl.ds(query_start, tile)
        column = query_start + lax.broadcasted_iota(jnp.int32, (1, tile), 1)
        begin = row_starts(column, first_end, second_end)
        row = key_start + lax.broadcasted_iota(jnp.int32, (tile, tile), 0)
        allowed = row >= begin
        if diagonal:
            allowed = allowed & (row <= column)
        value = ordered[at_keys, 4 * e :]
        for m in range(2):
            query = ordered[at_queries, m * e : (m + 1) * e]
            key = ordered[at_keys, (2 + m) * e : (3 + m) * e]
            map_grad = map_grads[m, at_queries, :]
            scores = contract(key, query, 1, 1)
            probability = jnp.where(
                allowed, jnp.exp(scores - log_totals[m : m + 1, at_queries]), 0.0
            )
            prob_grad = contract(value, map_grad, 1, 1)
            score_grad = (probability * (prob_grad - deltas[m, 0:1, at_queries])).astype(low)
            value_term = contract(probability.astype(low), map_grad, 1, 0)
            key_term = contract(score_grad, query, 1, 0)
            query_grads[m, at_queries, :] += contract(score_grad, key, 0, 0)
            if diagonal:
                key_grads[m, at_keys, :] = key_term
                if m == 0:
                    value_grads[at_keys, :] = value_term
                else:
                    value_grads[at_keys, :] += value_term
            else:
                key_grads[m, at_keys, :] += key_term
                value_grads[at_keys, :] += value_term

    for key_start in range(0, slots, tile):
        pair(key_start, key_start, True)

        def step(at, carry, key_start=key_start):
            pair(key_start, pl.multiple_of(at * tile, tile), False)
            return carry

        lax.fori_loop(key_start // tile + 1, slots // tile, step, 0)

    def turn_back(values, at):
        return values * cosine[at, :] - pltpu.roll(values, e // 2, 1) * sine[at, :]

    for block in range(8):
        at = slice(block * rows, (block + 1) * rows)
        for m, kept, sent in ((0, kept_first, sent_first), (1, kept_second, sent_second)):
            query = (turn_back(query_grads[m, at, :], at) * e ** (-0.5)).astype(low)
            key = turn_back(key_grads[m, at, :], at).astype(low)
            value = value_grads[at, m * e : (m + 1) * e].astype(low)
            store_block(
                block, ints, jnp.concatenate([query, key, value], axis=1), kept, sent, slice(None)
            )


def attention_backward(
    ints, floats, ordered, grads_kept, grads_received, outs, log_totals, gain, cosine, sine
):
    slots, width = outs.shape[1:]
    vmem = pl.BlockSpec(memory_space=pltpu.VMEM)
    smem = pl.BlockSpec(memory_space=pltpu.SMEM)
    return pl.pallas_call(
        attention_backward_kernel,
        in_specs=[smem, smem] + [vmem] * 8,
        out_specs=[vmem] * 6,
        out_shape=[jax.ShapeDtypeStruct((slots // 2, 3 * width // 2), low)] * 4
        + [jax.ShapeDtypeStruct((1, width), jnp.float32)] * 2,
        scratch_shapes=[
            pltpu.VMEM((2, slots, width), low),
            pltpu.VMEM((2, 8, slots), jnp.float32),
            pltpu.VMEM((2, slots, width // 2), jnp.float32),
            pltpu.VMEM((2, slots, width // 2), jnp.float32),
            pltpu.VMEM((slots, width), jnp.float32),
        ],
        compiler_params=pltpu.CompilerParams(vmem_limit_bytes=48 * 2**20),
        cost_estimate=estimate(20 * 10**9),
        name="attention_backward",
    )(ints, floats, ordered, grads_kept, grads_received, outs, log_totals, gain, cosine, sine)


def norm_back_kernel(one, two, three, values, gain, added, out, out_low, gain_grad):
    wide = values[...].astype(jnp.float32)
    grad = (
        one[...].astype(jnp.float32) + two[...].astype(jnp.float32) + three[...].astype(jnp.float32)
    )
    scale = lax.rsqrt(jnp.mean(wide * wide, axis=1, keepdims=True) + 1e-06)
    gained = grad * gain[...]
    inner = jnp.mean(gained * wide, axis=1, keepdims=True)
    result = added[...] + scale * gained - wide * (scale * scale * scale * inner)
    out[...] = result
    out_low[...] = result.astype(low)

    @pl.when(pl.program_id(0) == 0)
    def _():
        gain_grad[...] = jnp.zeros_like(gain_grad)

    gain_grad[...] += jnp.sum(grad * (wide * scale), axis=0, keepdims=True)


def norm_back(parts, values, gain, added):
    rows, width = values.shape
    block = rows // 4
    down = pl.BlockSpec((block, width), lambda i: (i, 0))
    once = pl.BlockSpec((1, width), lambda i: (0, 0))
    return pl.pallas_call(
        norm_back_kernel,
        grid=(4,),
        in_specs=[down] * 4 + [once, down],
        out_specs=[down, down, once],
        out_shape=[
            jax.ShapeDtypeStruct((rows, width), jnp.float32),
            jax.ShapeDtypeStruct((rows, width), low),
            jax.ShapeDtypeStruct((1, width), jnp.float32),
        ],
        compiler_params=pltpu.CompilerParams(vmem_limit_bytes=24 * 2**20),
        cost_estimate=estimate(10**9),
        name="norm_back",
    )(*parts, values, gain[None], added)


def project_kernel(inputs, weight, cosine, sine, first, second):
    e = cosine.shape[1]
    product = contract(inputs[...], weight[...], 1, 0)

    def turned(start):
        part = product[:, start : start + e]
        return part * cosine[...] + pltpu.roll(part, e // 2, 1) * sine[...]

    for out, start in ((first, 0), (second, 3 * e)):
        out[:, :e] = (turned(start) * e ** (-0.5)).astype(low)
        out[:, e : 2 * e] = turned(start + e).astype(low)
        out[:, 2 * e :] = product[:, start + 2 * e : start + 3 * e].astype(low)


def project(inputs, weight, cosine, sine):
    slots, width = inputs.shape
    columns = weight.shape[1]
    block = slots // 4
    down = lambda size: pl.BlockSpec((block, size), lambda i: (i, 0))
    return pl.pallas_call(
        project_kernel,
        grid=(4,),
        in_specs=[
            down(width),
            pl.BlockSpec((width, columns), lambda i: (0, 0)),
            down(cosine.shape[1]),
            down(cosine.shape[1]),
        ],
        out_specs=[down(columns // 2)] * 2,
        out_shape=[jax.ShapeDtypeStruct((slots, columns // 2), low)] * 2,
        compiler_params=pltpu.CompilerParams(vmem_limit_bytes=32 * 2**20),
        cost_estimate=estimate(2 * slots * width * columns),
        name="project",
    )(inputs, weight, cosine, sine)


def project_back_kernel(one, two, three, four, own, other, normed, gain, *outs):
    half = one.shape[1]
    total = contract(one[...], own[:, :half], 1, 1)
    total += contract(two[...], own[:, half:], 1, 1)
    total += contract(three[...], other[:, :half], 1, 1)
    total += contract(four[...], other[:, half:], 1, 1)
    store_parts(total, outs)
    part = jnp.sum(total * normed[...].astype(jnp.float32), axis=0, keepdims=True)

    @pl.when(pl.program_id(0) == 0)
    def _():
        gain[...] = jnp.zeros_like(gain)

    gain[...] += part


def project_back(grads, own, other, normed, first, count, rows, parts=1):
    width, columns = own.shape
    down = lambda size: pl.BlockSpec((rows, size), lambda i: (first + i, 0))
    whole = pl.BlockSpec((width, columns), lambda i: (0, 0))
    return pl.pallas_call(
        project_back_kernel,
        grid=(count,),
        in_specs=[down(columns // 2)] * 4 + [whole, whole, down(width)],
        out_specs=[pl.BlockSpec((1, width), lambda i: (0, 0))]
        + [pl.BlockSpec((rows // parts, width), lambda i: (i, 0))] * parts,
        out_shape=[jax.ShapeDtypeStruct((1, width), jnp.float32)]
        + [jax.ShapeDtypeStruct((count * rows // parts, width), low)] * parts,
        compiler_params=pltpu.CompilerParams(vmem_limit_bytes=40 * 2**20),
        cost_estimate=estimate(4 * count * rows * width * columns),
        name="project_back",
    )(*grads, own, other, normed)


def gate_kernel(inputs, gate, up, hidden, gate_factor, up_factor):
    gate_pre = contract(gate[...], inputs[...], 1, 1)
    upward = contract(up[...], inputs[...], 1, 1)
    sigmoid = 1.0 / (1.0 + jnp.exp(-gate_pre))
    silu = gate_pre * sigmoid
    hidden[...] = (silu * upward).astype(low)
    gate_factor[...] = (upward * (sigmoid * (1.0 + gate_pre * (1.0 - sigmoid)))).astype(low)
    up_factor[...] = silu.astype(low)


def gate_units(inputs, gate, up):
    slots, width = inputs.shape
    units = gate.shape[0]
    block = slots // 4
    whole = pl.BlockSpec((units, width), lambda i: (0, 0))
    across = pl.BlockSpec((units, block), lambda i: (0, i))
    return pl.pallas_call(
        gate_kernel,
        grid=(4,),
        in_specs=[pl.BlockSpec((block, width), lambda i: (i, 0)), whole, whole],
        out_specs=[across] * 3,
        out_shape=[jax.ShapeDtypeStruct((units, slots), low)] * 3,
        compiler_params=pltpu.CompilerParams(vmem_limit_bytes=40 * 2**20),
        cost_estimate=estimate(4 * slots * width * units),
        name="gate_units",
    )(inputs, gate, up)


def gate_grad_kernel(grads, down, gate_factor, up_factor, gate_grad, up_grad):
    hidden_grad = contract(down[...], grads[...], 1, 1)
    gate_grad[...] = (hidden_grad * gate_factor[...].astype(jnp.float32)).astype(low)
    up_grad[...] = (hidden_grad * up_factor[...].astype(jnp.float32)).astype(low)


def gate_grads(grads, down, gate_factor, up_factor):
    slots, width = grads.shape
    units = down.shape[0]
    block = slots // 4
    across = pl.BlockSpec((units, block), lambda i: (0, i))
    return pl.pallas_call(
        gate_grad_kernel,
        grid=(4,),
        in_specs=[
            pl.BlockSpec((block, width), lambda i: (i, 0)),
            pl.BlockSpec((units, width), lambda i: (0, 0)),
            across,
            across,
        ],
        out_specs=[across] * 2,
        out_shape=[jax.ShapeDtypeStruct((units, slots), low)] * 2,
        compiler_params=pltpu.CompilerParams(vmem_limit_bytes=40 * 2**20),
        cost_estimate=estimate(2 * slots * width * units),
        name="gate_grads",
    )(grads, down, gate_factor, up_factor)


def sum_kernel(terms, *refs):
    total = contract(refs[0][...], refs[terms][...], 0, 0)
    for place in range(1, terms):
        total += contract(refs[place][...], refs[terms + place][...], 0, 0)
    store_parts(total, refs[2 * terms :])


def sum_over_units(factors, weights, first, count, rows, parts=1):
    units, width = weights[0].shape
    terms = len(factors)
    return pl.pallas_call(
        functools.partial(sum_kernel, terms),
        grid=(count,),
        in_specs=[pl.BlockSpec((units, rows), lambda i: (0, first + i))] * terms
        + [pl.BlockSpec((units, width), lambda i: (0, 0))] * terms,
        out_specs=[pl.BlockSpec((rows // parts, width), lambda i: (i, 0))] * parts,
        out_shape=[jax.ShapeDtypeStruct((count * rows // parts, width), low)] * parts,
        compiler_params=pltpu.CompilerParams(vmem_limit_bytes=48 * 2**20),
        cost_estimate=estimate(2 * count * rows * width * units * terms),
        name="sum_over_units",
    )(*factors, *weights)


def body(
    tokens,
    lengths,
    attention_gain,
    query_weight,
    key_weight,
    value_weight,
    output_weight,
    lambda_vectors,
    head_gain,
    feedforward_gain,
    gate_weight,
    up_weight,
    down_weight,
    cotangent,
):
    rows, width = tokens.shape
    head_index = lax.axis_index("head")
    core = lax.axis_index("tensor")
    shard = query_weight.shape[0]
    qk_width = query_weight.shape[3]
    value_half = value_weight.shape[2]
    slots = rows * 8

    def in_order(mine, other):
        return jnp.where(core == 0, mine, other), jnp.where(core == 0, other, mine)

    own_slots = (
        (jnp.arange(4, dtype=jnp.int32) ^ head_index)[:, None] * (2 * rows)
        + core * rows
        + jnp.arange(rows, dtype=jnp.int32)[None, :]
    ).reshape(-1)
    segment_own, position_own = slot_layout(lengths, own_slots)
    valid = (segment_own[:rows] < 2).astype(jnp.float32)[:, None]
    half_width = qk_width // 2
    frequency = 10000.0 ** (-jnp.arange(half_width, dtype=jnp.float32) / half_width)

    def turn_tables(positions):
        angles = positions.astype(jnp.float32)[:, None] * frequency[None, :]
        cosine, sine = jnp.cos(angles), jnp.sin(angles)
        return jnp.concatenate([cosine, cosine], axis=1), jnp.concatenate([-sine, sine], axis=1)

    cosine, sine = turn_tables(position_own)
    cosine_all, sine_all = turn_tables(
        slot_layout(lengths, jnp.arange(slots, dtype=jnp.int32))[1]
    )
    own_head = head_index * 2 + core
    vectors = lax.dynamic_slice_in_dim(lambda_vectors, own_head, 1, 0)[0]
    first_exp = jnp.exp(jnp.sum(vectors[0] * vectors[1]))
    second_exp = jnp.exp(jnp.sum(vectors[2] * vectors[3]))
    lambda_value = first_exp - second_exp + lambda_base
    floats = jnp.stack(in_order(1.0, -lambda_value))
    ints = jnp.stack([head_index, core, lengths[0, 0], lengths[0, 0] + lengths[0, 1]])
    gain_own = rolled(
        lax.dynamic_slice_in_dim(head_gain, own_head, 1, 0), core * value_half
    ) * (1.0 - lambda_base)

    third = 3 * qk_width
    heads = [
        jnp.concatenate(
            [
                weight[:, place].reshape(shard, -1)
                for weight in (query_weight, key_weight, value_weight)
            ],
            axis=1,
        )
        for place in range(2)
    ]
    qkv_local = jnp.concatenate(in_order(*heads), axis=1)

    output_local = jnp.concatenate(in_order(output_weight[0], output_weight[1]), axis=0)

    tokens_wide = after(tokens, output_local).astype(jnp.float32)
    attention_scale = lax.rsqrt(jnp.mean(tokens_wide * tokens_wide, axis=-1, keepdims=True) + 1e-06)
    normed_own = (tokens_wide * attention_scale * attention_gain).astype(low)
    output_own = placed(line_gather(output_local))
    ffn_out_grad = valid * cotangent.astype(jnp.float32)
    ffn_out_grad_own = ffn_out_grad.astype(low)
    normed_near = [
        after(
            near,
            *(cosine, sine, cosine_all, sine_all),
            *(ffn_out_grad_own, ints, floats, gain_own, output_own),
        )
        for near in near_rows(normed_own)
    ]
    normed = group_rows(normed_own, normed_near)

    qkv_own = after(fsdp_gather(qkv_local, 0), normed)
    qkv_other = swap(qkv_own, "tensor", 1)
    gate_own = fsdp_gather(jnp.transpose(gate_weight), 1)
    up_own = fsdp_gather(jnp.transpose(up_weight), 1, normed)

    ffn_out_grad_own = after(ffn_out_grad_own, normed)
    ffn_out_grad_near = near_rows(ffn_out_grad_own)
    kept_first, sent_second = project(normed, qkv_own, cosine, sine)
    sent_first, kept_second = project(after(normed, kept_first), qkv_other, cosine, sine)
    ffn_out_grad_near = [after(near, sent_first) for near in ffn_out_grad_near]
    output_other = swap(after(output_own, sent_first), "tensor", 1)
    output_kept = jnp.concatenate([output_own[:value_half], output_other[value_half:]], axis=0)
    output_sent = jnp.concatenate([output_other[:value_half], output_own[value_half:]], axis=0)
    output_all = jnp.concatenate([output_kept, output_sent], axis=0)
    kept, sent, ordered, outs, log_totals = attention_forward(
        ints,
        floats,
        (after(kept_first, *ffn_out_grad_near), kept_second),
        (swap(sent_first, "tensor", 1), swap(sent_second, "tensor", 1)),
        gain_own,
    )
    head_out = jnp.concatenate([kept, swap(sent, "tensor", 1)], axis=1)

    third_out = [
        contract(head_out[start : start + rows // 2], output_all, 1, 0).astype(low)
        for start in (3 * rows, 7 * rows // 2)
    ]
    down_own = fsdp_gather(down_weight, 1, *third_out)
    nearer_out = contract(after(head_out, *third_out)[: 3 * rows], output_all, 1, 0).astype(low)
    attention_out, _ = group_reduce(
        nearer_out,
        rows,
        third_out,
        lambda *arrived: nearer_out[:rows],
    )
    residual = tokens_wide + summed([after(part, gate_own) for part in attention_out])
    ffn_scale = lax.rsqrt(jnp.mean(residual * residual, axis=-1, keepdims=True) + 1e-06)
    ffn_in_own = (residual * ffn_scale * feedforward_gain).astype(low)
    ffn_in_near = near_rows(ffn_in_own)
    ffn_in = group_rows(ffn_in_own, ffn_in_near)
    gate_own, up_own = after(gate_own, ffn_in), after(up_own, ffn_in)
    gate_other, up_other = swap(gate_own, "tensor", 1), swap(up_own, "tensor", 1)
    hidden_own, gate_factor_own, up_factor_own = gate_units(ffn_in, gate_own, up_own)
    hidden_other, gate_factor_other, up_factor_other = gate_units(
        after(ffn_in, hidden_own), gate_other, up_other
    )

    down_own = after(down_own, hidden_other)
    down_other = swap(down_own, "tensor", 1)

    ffn_out_grad_all = group_rows(ffn_out_grad_own, ffn_out_grad_near, hidden_own)

    def weight_grad(own_side, other_side, right_side, *events):
        other = contract(other_side, right_side, 1, 0).astype(low)
        own = contract(after(own_side, other, *events), right_side, 1, 0)
        total = add_low(own, swap(other, "tensor", 1))
        return total, fsdp_reduce(total, 1)

    down_terms, down_grad = weight_grad(hidden_own, hidden_other, ffn_out_grad_all)
    gate_grad_own, up_grad_own = gate_grads(
        after(ffn_out_grad_all, down_terms), down_own, gate_factor_own, up_factor_own
    )
    gate_grad_other, up_grad_other = gate_grads(
        ffn_out_grad_all, down_other, gate_factor_other, up_factor_other
    )
    factors = [gate_grad_own, up_grad_own, gate_grad_other, up_grad_other]
    weights = [gate_own, up_own, gate_other, up_other]
    third_grad = sum_over_units(factors, weights, 3, 1, rows, 2)
    gate_other_part = contract(after(gate_grad_other, *third_grad), ffn_in, 1, 0).astype(low)
    (near_grad,) = sum_over_units(
        [after(factors[0], gate_other_part)] + factors[1:], weights, 1, 2, rows
    )
    own_grads, gate_sums = [], []

    def own_grad(*arrived):
        gate_terms = add_low(
            contract(after(gate_grad_own, near_grad, *arrived), ffn_in, 1, 0),
            swap(gate_other_part, "tensor", 1),
        )
        gate_sums.append(fsdp_reduce(gate_terms, 1))
        own_grads.extend(
            sum_over_units(
                [after(factors[0], gate_terms, down_grad, *arrived)] + factors[1:],
                weights,
                0,
                1,
                rows,
            )
        )
        return own_grads[0]

    ffn_in_sum, near_sent = group_reduce(near_grad, 0, third_grad, own_grad)
    gate_weight_grad = gate_sums[0]
    up_terms, up_weight_grad = weight_grad(
        after(up_grad_own, own_grads[0]), after(up_grad_other, own_grads[0], *near_sent), ffn_in
    )
    residual_grad, residual_grad_low, feedforward_gain_part = norm_back(
        [after(part, up_terms) for part in ffn_in_sum],
        residual,
        feedforward_gain,
        ffn_out_grad,
    )
    feedforward_gain_part = feedforward_gain_part[0]

    (ffn_out,) = sum_over_units(
        [after(hidden_own, residual_grad_low), hidden_other], [down_own, down_other], 0, 4, rows
    )
    residual_grad_near = [
        after(near, ffn_out, gate_weight_grad) for near in near_rows(residual_grad_low)
    ]
    attention_out_grad = group_rows(residual_grad_low, residual_grad_near)
    head_grad_sent = contract(attention_out_grad, output_sent, 1, 1).astype(low)
    head_grad_kept = contract(after(attention_out_grad, head_grad_sent), output_kept, 1, 1)
    output_terms = contract(head_out, after(attention_out_grad, head_grad_sent), 0, 0).astype(low)
    output_terms = [
        output_terms[place * value_half : (place + 1) * value_half] for place in range(4)
    ]
    output_sum = add_low(
        jnp.concatenate([output_terms[0], output_terms[3]], axis=0),
        swap(jnp.concatenate([output_terms[2], output_terms[1]], axis=0), "tensor", 1),
    )
    output_grad = fsdp_reduce(output_sum, 1)
    kept_first, kept_second, sent_first, sent_second, head_gain_part, lambda_part = (
        attention_backward(
            ints,
            floats,
            ordered,
            after(head_grad_kept.astype(low), output_sum, up_weight_grad),
            swap(head_grad_sent, "tensor", 1),
            outs,
            log_totals,
            gain_own,
            cosine_all,
            sine_all,
        )
    )

    ffn_arrived = []

    def ffn_own(*arrived):
        ffn_arrived.extend(arrived)
        return ffn_out[:rows]

    ffn_here, ffn_sent = group_reduce(
        ffn_out,
        rows,
        [
            after(ffn_out[start : start + rows // 2], attention_out_grad)
            for start in (3 * rows, 7 * rows // 2)
        ],
        ffn_own,
        (kept_first,),
    )

    received_first = swap(after(sent_first, *ffn_arrived, output_grad), "tensor", 1)
    received_second = swap(sent_second, "tensor", 1)
    others_second = contract(normed, kept_second, 0, 0).astype(low)
    others_first = contract(
        after(normed, others_second, *ffn_sent), received_first, 0, 0
    ).astype(low)
    parts = (kept_first, received_second, received_first, kept_second)
    own_first = add_low(
        contract(after(normed, others_first), kept_first, 0, 0), swap(others_first, "tensor", 1)
    )
    own_second = add_low(
        contract(after(normed, others_first), received_second, 0, 0),
        swap(others_second, "tensor", 1),
    )
    third_gain, *third_terms = project_back(
        (after(kept_first, own_first, own_second, output_grad),) + parts[1:],
        qkv_own,
        qkv_other,
        normed,
        3,
        1,
        rows,
        2,
    )
    qkv_weight_grad = in_order(
        fsdp_reduce(own_first, 0).astype(jnp.float32),
        fsdp_reduce(own_second, 0).astype(jnp.float32),
    )
    output_grad = output_grad.astype(jnp.float32)
    output_grad = jnp.stack(in_order(output_grad[:value_half], output_grad[value_half:]))
    nearer_gain, nearer_terms = project_back(
        (after(kept_first, third_gain),) + parts[1:],
        qkv_own,
        qkv_other,
        normed,
        0,
        3,
        rows,
    )
    normed_grad, _ = group_reduce(
        nearer_terms,
        rows,
        [after(terms, *ffn_here) for terms in third_terms],
        lambda *arrived: nearer_terms[:rows],
    )
    attention_gain_part = (third_gain + nearer_gain)[0]
    ffn_here = [after(part, nearer_gain) for part in ffn_here]
    block_output = (valid * (residual + summed(ffn_here))).astype(low)
    tokens_grad, _, _ = norm_back(normed_grad, tokens, attention_gain, residual_grad)

    lambda_grad = -jnp.sum(lambda_part)
    vector_grads = lambda_grad * jnp.stack(
        [
            first_exp * vectors[1],
            first_exp * vectors[0],
            -second_exp * vectors[3],
            -second_exp * vectors[2],
        ]
    )
    lambda_full = lax.dynamic_update_slice(
        jnp.zeros(lambda_vectors.shape, jnp.float32), vector_grads[None], (own_head, 0, 0)
    )
    gain_full = lax.dynamic_update_slice(
        jnp.zeros(head_gain.shape, jnp.float32),
        rolled(head_gain_part, core * value_half),
        (own_head, 0),
    )
    small = total_over_all(
        jnp.concatenate(
            [
                attention_gain_part / attention_gain,
                feedforward_gain_part,
                lambda_full.reshape(-1),
                gain_full.reshape(-1),
            ]
        )
    )
    lambda_end = 2 * width + lambda_full.size
    return (
        block_output,
        tokens_grad,
        small[:width],
        *(
            jnp.stack(
                [part[:, kind * qk_width : (kind + 1) * qk_width] for part in qkv_weight_grad],
                axis=1,
            ).reshape(weight.shape)
            for kind, weight in enumerate((query_weight, key_weight, value_weight))
        ),
        output_grad.reshape(output_weight.shape),
        small[2 * width : lambda_end].reshape(lambda_full.shape),
        small[lambda_end:].reshape(gain_full.shape),
        small[width : 2 * width],
        jnp.transpose(gate_weight_grad).astype(jnp.float32),
        jnp.transpose(up_weight_grad).astype(jnp.float32),
        down_grad.astype(jnp.float32),
    )


def solution(mesh):
    placed = (
        P(("fsdp", "head", "tensor"), None),
        P("fsdp", None),
        P(),
        P("fsdp", "head", "tensor", None),
        P("fsdp", "head", "tensor", None),
        P("fsdp", "head", "tensor"),
        P("head", "tensor", "fsdp"),
        P(),
        P(),
        P(),
        P("fsdp", ("head", "tensor")),
        P("fsdp", ("head", "tensor")),
        P(("head", "tensor"), "fsdp"),
        P(("fsdp", "head", "tensor"), None),
    )
    return jax.shard_map(
        body,
        mesh=mesh,
        in_specs=placed,
        out_specs=(
            P(("fsdp", "head", "tensor"), None),
            P(("fsdp", "head", "tensor"), None),
            P(),
            P("fsdp", "head", "tensor", None),
            P("fsdp", "head", "tensor", None),
            P("fsdp", "head", "tensor"),
            P("head", "tensor", "fsdp"),
            P(),
            P(),
            P(),
            P("fsdp", ("head", "tensor")),
            P("fsdp", ("head", "tensor")),
            P(("head", "tensor"), "fsdp"),
        ),
        check_vma=False,
    )
```

```python
import functools

import jax
import jax.numpy as jnp
from jax import lax
from jax.experimental import pallas as pl
from jax.experimental.pallas import tpu as pltpu
from jax.sharding import PartitionSpec as P

lambda_base = 0.2
tile = 512
cost_share = 0.02
low = jnp.bfloat16


def contract(left_side, right_side, left_dim, right_dim):
    return lax.dot_general(
        left_side,
        right_side,
        (((left_dim,), (right_dim,)), ((), ())),
        preferred_element_type=jnp.float32,
    )


def after(values, *others):
    if not others:
        return values
    return lax.optimization_barrier((values, *others))[0]


def swap(values, axis, mask):
    size = lax.axis_size(axis)
    return lax.ppermute(values, axis, [(place, place ^ mask) for place in range(size)])


def fsdp_gather(own, axis, *others):
    return lax.all_gather(after(own, *others), "fsdp", axis=axis, tiled=True)


def fsdp_reduce(partial, axis):
    return lax.psum_scatter(partial, "fsdp", scatter_dimension=axis, tiled=True)


def shift(values, step):
    size = lax.axis_size("fsdp")
    return lax.ppermute(values, "fsdp", [(place, (place + step) % size) for place in range(size)])


def line_gather(own):
    size = lax.axis_size("fsdp")
    return [own] + [shift(own, -step) for step in range(1, size)]


def place_kernel(index, *refs):
    shards, out = refs[:-1], refs[-1]
    size, width = len(shards), shards[0].shape[1]
    for place, shard in enumerate(shards):
        to = lax.rem(index[0] + place, size) * width
        out[:, pl.ds(pl.multiple_of(to, width), width)] = shard[...]


def placed(shards):
    size = len(shards)
    rows, width = shards[0].shape
    vmem = pl.BlockSpec(memory_space=pltpu.VMEM)
    return pl.pallas_call(
        place_kernel,
        in_specs=[pl.BlockSpec(memory_space=pltpu.SMEM)] + [vmem] * size,
        out_specs=vmem,
        out_shape=jax.ShapeDtypeStruct((rows, size * width), low),
        cost_estimate=estimate(10**8),
        name="placed",
    )(lax.axis_index("fsdp")[None], *shards)


def add_low(left_side, right_side):
    return (left_side.astype(jnp.float32) + right_side.astype(jnp.float32)).astype(low)


def near_rows(own):
    return swap(own, "head", 1), swap(own, "head", 2)


def group_rows(own, near, *events):
    half = own.shape[0] // 2
    first, second = near
    third_low = swap(second[:half], "head", 1)
    third_high = swap(first[half:], "head", 2)
    far = [after(part, *events) for part in (third_low, third_high)]
    return jnp.concatenate([after(own, *events), first, second, *far], axis=0)


def join_kernel(start, near, to_first, to_second, first, second):
    rows = first.shape[0]
    half = rows // 2
    middle = start + rows
    first[:half] = near[start : start + half]
    first[half:] = add_low(near[start + half : middle], to_second[...])
    second[:half] = add_low(near[middle : middle + half], to_first[...])
    second[half:] = near[middle + half : middle + rows]


def group_reduce(near, start, halves, own_part, hold=()):
    half, width = halves[0].shape
    rows = 2 * half
    to_first = swap(halves[0], "head", 1)
    to_second = swap(halves[1], "head", 2)
    own = own_part(to_first, to_second)
    vmem = pl.BlockSpec(memory_space=pltpu.VMEM)
    first, second = pl.pallas_call(
        functools.partial(join_kernel, start),
        in_specs=[vmem] * 3,
        out_specs=[vmem] * 2,
        out_shape=[jax.ShapeDtypeStruct((rows, width), low)] * 2,
        compiler_params=pltpu.CompilerParams(vmem_limit_bytes=10 * 2**20),
        cost_estimate=estimate(10**9),
        name="join",
    )(after(near, *hold), to_first, to_second)
    from_first = swap(first, "head", 1)
    from_second = swap(second, "head", 2)
    return (own, from_first, from_second), (first, second)


def summed(parts):
    return sum(part.astype(jnp.float32) for part in parts)


def total_over_all(values):
    for axis in ("tensor", "fsdp", "head"):
        mask = 1
        while mask < lax.axis_size(axis):
            values = values + swap(values, axis, mask)
            mask *= 2
    return values


def rolled(values, start):
    twice = jnp.concatenate([values, values], axis=-1)
    return lax.dynamic_slice_in_dim(twice, start, values.shape[-1], values.ndim - 1)


def slot_layout(lengths, slots):
    first_end = lengths[0, 0]
    second_end = first_end + lengths[0, 1]
    segment = (slots >= first_end).astype(jnp.int32) + (slots >= second_end).astype(jnp.int32)
    start = jnp.where(segment == 0, 0, jnp.where(segment == 1, first_end, second_end))
    return segment, slots - start


def store_parts(values, outs):
    size = values.shape[0] // len(outs)
    for place, out in enumerate(outs):
        out[...] = values[place * size : (place + 1) * size].astype(out.dtype)


def kept_block(shape):
    return pl.BlockSpec(shape, lambda i: (0,) * len(shape), pipeline_mode=pl.Buffered(1))


def estimate(flops):
    return pl.CostEstimate(
        flops=int(flops * cost_share), bytes_accessed=2**20, transcendentals=0
    )


def store_block(block, ints, values, kept, sent, columns):
    rows = values.shape[0]
    at = pl.ds(pl.multiple_of(((block >> 1) ^ ints[0]) * rows, rows), rows)

    @pl.when(ints[1] == (block & 1))
    def _():
        kept[at, columns] = values

    @pl.when(ints[1] != (block & 1))
    def _():
        sent[at, columns] = values


def row_starts(slots, first_end, second_end):
    return jnp.where(slots >= second_end, second_end, jnp.where(slots >= first_end, first_end, 0))


def attention_forward_kernel(
    ints,
    floats,
    kept_first,
    kept_second,
    received_first,
    received_second,
    gain,
    head_out_kept,
    head_out_sent,
    ordered,
    outs,
    log_totals,
):
    head_index, core, first_end, second_end = (ints[place] for place in range(4))
    rows = kept_first.shape[0] // 4
    slots = 8 * rows
    width = gain.shape[1]
    e = width // 2
    for parts, other in (
        ((kept_first, kept_second), 0),
        ((received_first, received_second), 1),
    ):
        for j in range(4):
            block = (head_index ^ j) * 2 + (core ^ other)
            at = pl.ds(pl.multiple_of(block * rows, rows), rows)
            for m in range(2):
                for kind in range(3):
                    to = (2 * kind + m) * e
                    ordered[at, to : to + e] = parts[m][
                        j * rows : (j + 1) * rows, kind * e : (kind + 1) * e
                    ]
    for start in range(0, slots, tile):
        stop = start + tile
        row = start + lax.broadcasted_iota(jnp.int32, (tile, 1), 0)
        begin = row_starts(row, first_end, second_end)
        value = ordered[:stop, 4 * e :]
        results = []
        for m in range(2):
            scores = contract(
                ordered[start:stop, m * e : (m + 1) * e],
                ordered[:stop, (2 + m) * e : (3 + m) * e],
                1,
                1,
            )
            column = lax.broadcasted_iota(jnp.int32, (tile, stop), 1)
            scores = jnp.where((column >= begin) & (column <= row), scores, -1e30)
            row_max = jnp.max(scores, axis=1, keepdims=True)
            expanded = jnp.exp(scores - row_max)
            row_total = jnp.sum(expanded, axis=1, keepdims=True)
            result = contract(expanded.astype(low), value, 1, 0) / row_total
            outs[m, start:stop, :] = result
            results.append(result)
            wide = jnp.broadcast_to(row_max + jnp.log(row_total), (tile, 128))
            log_totals[m : m + 1, start:stop] = jnp.transpose(wide)[:1]
        mixed = results[0] * floats[0] + results[1] * floats[1]
        scale = lax.rsqrt(jnp.mean(mixed * mixed, axis=1, keepdims=True) + 1e-05)
        normed = (mixed * scale * gain[...]).astype(low)
        for piece in range(tile // rows):
            store_block(
                start // rows + piece,
                ints,
                normed[piece * rows : (piece + 1) * rows],
                head_out_kept,
                head_out_sent,
                slice(None),
            )


def attention_forward(ints, floats, kept, received, gain):
    rows = kept[0].shape[0] // 4
    slots = 8 * rows
    width = gain.shape[1]
    vmem = pl.BlockSpec(memory_space=pltpu.VMEM)
    smem = pl.BlockSpec(memory_space=pltpu.SMEM)
    return pl.pallas_call(
        attention_forward_kernel,
        in_specs=[smem, smem] + [vmem] * 5,
        out_specs=[vmem] * 5,
        out_shape=[
            jax.ShapeDtypeStruct((slots // 2, width), low),
            jax.ShapeDtypeStruct((slots // 2, width), low),
            jax.ShapeDtypeStruct((slots, 3 * width), low),
            jax.ShapeDtypeStruct((2, slots, width), jnp.float32),
            jax.ShapeDtypeStruct((2, slots), jnp.float32),
        ],
        compiler_params=pltpu.CompilerParams(vmem_limit_bytes=32 * 2**20),
        cost_estimate=estimate(5 * 10**9),
        name="attention_forward",
    )(ints, floats, *kept, *received, gain)


def attention_backward_kernel(
    ints,
    floats,
    ordered,
    grads_kept,
    grads_received,
    outs,
    log_totals,
    gain,
    cosine,
    sine,
    kept_first,
    kept_second,
    sent_first,
    sent_second,
    gain_grad,
    lambda_grad,
    map_grads,
    deltas,
    query_grads,
    key_grads,
    value_grads,
):
    head_index, core, first_end, second_end = (ints[place] for place in range(4))
    rows = grads_kept.shape[0] // 4
    slots = 8 * rows
    width = gain.shape[1]
    e = width // 2
    gain_total = jnp.zeros((1, width), jnp.float32)
    lambda_total = jnp.zeros((1, width), jnp.float32)
    for part, other in ((grads_kept, 0), (grads_received, 1)):
        for j in range(4):
            block = (head_index ^ j) * 2 + (core ^ other)
            at = pl.ds(pl.multiple_of(block * rows, rows), rows)
            grad = part[j * rows : (j + 1) * rows, :].astype(jnp.float32)
            first, second = outs[0, at, :], outs[1, at, :]
            mixed = first * floats[0] + second * floats[1]
            scale = lax.rsqrt(jnp.mean(mixed * mixed, axis=1, keepdims=True) + 1e-05)
            gain_total += jnp.sum(grad * (mixed * scale), axis=0, keepdims=True)
            weighted = grad * gain[...]
            inner = jnp.mean(weighted * mixed, axis=1, keepdims=True)
            mixed_grad = scale * weighted - mixed * (scale * scale * scale * inner)
            lambda_total += jnp.sum(
                mixed_grad * jnp.where(core == 1, first, second), axis=0, keepdims=True
            )
            for m, out in ((0, first), (1, second)):
                map_grad = (mixed_grad * floats[m]).astype(low)
                map_grads[m, at, :] = map_grad
                delta = jnp.sum(map_grad.astype(jnp.float32) * out, axis=1, keepdims=True)
                deltas[m, :, at] = jnp.transpose(jnp.broadcast_to(delta, (rows, 128)))[:8]
    gain_grad[...] = gain_total * (1.0 - lambda_base)
    lambda_grad[...] = lambda_total
    query_grads[...] = jnp.zeros_like(query_grads)

    def pair(key_start, query_start, diagonal):
        at_keys = pl.ds(key_start, tile)
        at_queries = pl.ds(query_start, tile)
        column = query_start + lax.broadcasted_iota(jnp.int32, (1, tile), 1)
        begin = row_starts(column, first_end, second_end)
        row = key_start + lax.broadcasted_iota(jnp.int32, (tile, tile), 0)
        allowed = row >= begin
        if diagonal:
            allowed = allowed & (row <= column)
        value = ordered[at_keys, 4 * e :]
        for m in range(2):
            query = ordered[at_queries, m * e : (m + 1) * e]
            key = ordered[at_keys, (2 + m) * e : (3 + m) * e]
            map_grad = map_grads[m, at_queries, :]
            scores = contract(key, query, 1, 1)
            probability = jnp.where(
                allowed, jnp.exp(scores - log_totals[m : m + 1, at_queries]), 0.0
            )
            prob_grad = contract(value, map_grad, 1, 1)
            score_grad = (probability * (prob_grad - deltas[m, 0:1, at_queries])).astype(low)
            value_term = contract(probability.astype(low), map_grad, 1, 0)
            key_term = contract(score_grad, query, 1, 0)
            query_grads[m, at_queries, :] += contract(score_grad, key, 0, 0)
            if diagonal:
                key_grads[m, at_keys, :] = key_term
                if m == 0:
                    value_grads[at_keys, :] = value_term
                else:
                    value_grads[at_keys, :] += value_term
            else:
                key_grads[m, at_keys, :] += key_term
                value_grads[at_keys, :] += value_term

    for key_start in range(0, slots, tile):
        pair(key_start, key_start, True)

        def step(at, carry, key_start=key_start):
            pair(key_start, pl.multiple_of(at * tile, tile), False)
            return carry

        lax.fori_loop(key_start // tile + 1, slots // tile, step, 0)

    def turn_back(values, at):
        return values * cosine[at, :] - pltpu.roll(values, e // 2, 1) * sine[at, :]

    for block in range(8):
        at = slice(block * rows, (block + 1) * rows)
        for m, kept, sent in ((0, kept_first, sent_first), (1, kept_second, sent_second)):
            query = (turn_back(query_grads[m, at, :], at) * e ** (-0.5)).astype(low)
            key = turn_back(key_grads[m, at, :], at).astype(low)
            value = value_grads[at, m * e : (m + 1) * e].astype(low)
            store_block(
                block, ints, jnp.concatenate([query, key, value], axis=1), kept, sent, slice(None)
            )


def attention_backward(
    ints, floats, ordered, grads_kept, grads_received, outs, log_totals, gain, cosine, sine
):
    slots, width = outs.shape[1:]
    vmem = pl.BlockSpec(memory_space=pltpu.VMEM)
    smem = pl.BlockSpec(memory_space=pltpu.SMEM)
    return pl.pallas_call(
        attention_backward_kernel,
        in_specs=[smem, smem] + [vmem] * 8,
        out_specs=[vmem] * 6,
        out_shape=[jax.ShapeDtypeStruct((slots // 2, 3 * width // 2), low)] * 4
        + [jax.ShapeDtypeStruct((1, width), jnp.float32)] * 2,
        scratch_shapes=[
            pltpu.VMEM((2, slots, width), low),
            pltpu.VMEM((2, 8, slots), jnp.float32),
            pltpu.VMEM((2, slots, width // 2), jnp.float32),
            pltpu.VMEM((2, slots, width // 2), jnp.float32),
            pltpu.VMEM((slots, width), jnp.float32),
        ],
        compiler_params=pltpu.CompilerParams(vmem_limit_bytes=40 * 2**20),
        cost_estimate=estimate(20 * 10**9),
        name="attention_backward",
    )(ints, floats, ordered, grads_kept, grads_received, outs, log_totals, gain, cosine, sine)


def norm_back_kernel(one, two, three, values, gain, added, out, out_low, gain_grad):
    wide = values[...].astype(jnp.float32)
    grad = (
        one[...].astype(jnp.float32) + two[...].astype(jnp.float32) + three[...].astype(jnp.float32)
    )
    scale = lax.rsqrt(jnp.mean(wide * wide, axis=1, keepdims=True) + 1e-06)
    gained = grad * gain[...]
    inner = jnp.mean(gained * wide, axis=1, keepdims=True)
    result = added[...] + scale * gained - wide * (scale * scale * scale * inner)
    out[...] = result
    out_low[...] = result.astype(low)

    @pl.when(pl.program_id(0) == 0)
    def _():
        gain_grad[...] = jnp.zeros_like(gain_grad)

    gain_grad[...] += jnp.sum(grad * (wide * scale), axis=0, keepdims=True)


def norm_back(parts, values, gain, added):
    rows, width = values.shape
    block = rows // 4
    down = pl.BlockSpec((block, width), lambda i: (i, 0))
    once = pl.BlockSpec((1, width), lambda i: (0, 0))
    return pl.pallas_call(
        norm_back_kernel,
        grid=(4,),
        in_specs=[down] * 4 + [once, down],
        out_specs=[down, down, once],
        out_shape=[
            jax.ShapeDtypeStruct((rows, width), jnp.float32),
            jax.ShapeDtypeStruct((rows, width), low),
            jax.ShapeDtypeStruct((1, width), jnp.float32),
        ],
        compiler_params=pltpu.CompilerParams(vmem_limit_bytes=12 * 2**20),
        cost_estimate=estimate(10**9),
        name="norm_back",
    )(*parts, values, gain[None], added)


def project_kernel(inputs, weight, cosine, sine, first, second):
    e = cosine.shape[1]
    product = contract(inputs[...], weight[...], 1, 0)

    def turned(start):
        part = product[:, start : start + e]
        return part * cosine[...] + pltpu.roll(part, e // 2, 1) * sine[...]

    for out, start in ((first, 0), (second, 3 * e)):
        out[:, :e] = (turned(start) * e ** (-0.5)).astype(low)
        out[:, e : 2 * e] = turned(start + e).astype(low)
        out[:, 2 * e :] = product[:, start + 2 * e : start + 3 * e].astype(low)


def project(inputs, weight, cosine, sine):
    slots, width = inputs.shape
    columns = weight.shape[1]
    block = slots // 4
    down = lambda size: pl.BlockSpec((block, size), lambda i: (i, 0))
    return pl.pallas_call(
        project_kernel,
        grid=(4,),
        in_specs=[
            down(width),
            kept_block((width, columns)),
            down(cosine.shape[1]),
            down(cosine.shape[1]),
        ],
        out_specs=[down(columns // 2)] * 2,
        out_shape=[jax.ShapeDtypeStruct((slots, columns // 2), low)] * 2,
        compiler_params=pltpu.CompilerParams(vmem_limit_bytes=14 * 2**20),
        cost_estimate=estimate(2 * slots * width * columns),
        name="project",
    )(inputs, weight, cosine, sine)


def project_back_kernel(one, two, three, four, own, other, normed, gain, *outs):
    half = one.shape[1]
    total = contract(one[...], own[:, :half], 1, 1)
    total += contract(two[...], own[:, half:], 1, 1)
    total += contract(three[...], other[:, :half], 1, 1)
    total += contract(four[...], other[:, half:], 1, 1)
    store_parts(total, outs)
    part = jnp.sum(total * normed[...].astype(jnp.float32), axis=0, keepdims=True)

    @pl.when(pl.program_id(0) == 0)
    def _():
        gain[...] = jnp.zeros_like(gain)

    gain[...] += part


def project_back(grads, own, other, normed, first, count, rows, parts=1):
    width, columns = own.shape
    down = lambda size: pl.BlockSpec((rows, size), lambda i: (first + i, 0))
    whole = kept_block((width, columns))
    return pl.pallas_call(
        project_back_kernel,
        grid=(count,),
        in_specs=[down(columns // 2)] * 4 + [whole, whole, down(width)],
        out_specs=[pl.BlockSpec((1, width), lambda i: (0, 0))]
        + [pl.BlockSpec((rows // parts, width), lambda i: (i, 0))] * parts,
        out_shape=[jax.ShapeDtypeStruct((1, width), jnp.float32)]
        + [jax.ShapeDtypeStruct((count * rows // parts, width), low)] * parts,
        compiler_params=pltpu.CompilerParams(vmem_limit_bytes=22 * 2**20),
        cost_estimate=estimate(4 * count * rows * width * columns),
        name="project_back",
    )(*grads, own, other, normed)


def gate_kernel(inputs, gate, up, hidden, gate_factor, up_factor):
    gate_pre = contract(gate[...], inputs[...], 1, 1)
    upward = contract(up[...], inputs[...], 1, 1)
    sigmoid = 1.0 / (1.0 + jnp.exp(-gate_pre))
    silu = gate_pre * sigmoid
    hidden[...] = (silu * upward).astype(low)
    gate_factor[...] = (upward * (sigmoid * (1.0 + gate_pre * (1.0 - sigmoid)))).astype(low)
    up_factor[...] = silu.astype(low)


def gate_units(inputs, gate, up):
    slots, width = inputs.shape
    units = gate.shape[0]
    block = slots // 4
    whole = kept_block((units, width))
    across = pl.BlockSpec((units, block), lambda i: (0, i))
    return pl.pallas_call(
        gate_kernel,
        grid=(4,),
        in_specs=[pl.BlockSpec((block, width), lambda i: (i, 0)), whole, whole],
        out_specs=[across] * 3,
        out_shape=[jax.ShapeDtypeStruct((units, slots), low)] * 3,
        compiler_params=pltpu.CompilerParams(vmem_limit_bytes=22 * 2**20),
        cost_estimate=estimate(4 * slots * width * units),
        name="gate_units",
    )(inputs, gate, up)


def gate_grad_kernel(grads, down, gate_factor, up_factor, gate_grad, up_grad):
    hidden_grad = contract(down[...], grads[...], 1, 1)
    gate_grad[...] = (hidden_grad * gate_factor[...].astype(jnp.float32)).astype(low)
    up_grad[...] = (hidden_grad * up_factor[...].astype(jnp.float32)).astype(low)


def gate_grads(grads, down, gate_factor, up_factor):
    slots, width = grads.shape
    units = down.shape[0]
    block = slots // 4
    across = pl.BlockSpec((units, block), lambda i: (0, i))
    return pl.pallas_call(
        gate_grad_kernel,
        grid=(4,),
        in_specs=[
            pl.BlockSpec((block, width), lambda i: (i, 0)),
            kept_block((units, width)),
            across,
            across,
        ],
        out_specs=[across] * 2,
        out_shape=[jax.ShapeDtypeStruct((units, slots), low)] * 2,
        compiler_params=pltpu.CompilerParams(vmem_limit_bytes=16 * 2**20),
        cost_estimate=estimate(2 * slots * width * units),
        name="gate_grads",
    )(grads, down, gate_factor, up_factor)


def sum_kernel(terms, *refs):
    total = contract(refs[0][...], refs[terms][...], 0, 0)
    for place in range(1, terms):
        total += contract(refs[place][...], refs[terms + place][...], 0, 0)
    store_parts(total, refs[2 * terms :])


def sum_over_units(factors, weights, first, count, rows, parts=1):
    units, width = weights[0].shape
    terms = len(factors)
    return pl.pallas_call(
        functools.partial(sum_kernel, terms),
        grid=(count,),
        in_specs=[pl.BlockSpec((units, rows), lambda i: (0, first + i))] * terms
        + [kept_block((units, width))] * terms,
        out_specs=[pl.BlockSpec((rows // parts, width), lambda i: (i, 0))] * parts,
        out_shape=[jax.ShapeDtypeStruct((count * rows // parts, width), low)] * parts,
        compiler_params=pltpu.CompilerParams(vmem_limit_bytes=26 * 2**20),
        cost_estimate=estimate(2 * count * rows * width * units * terms),
        name="sum_over_units",
    )(*factors, *weights)


def body(
    tokens,
    lengths,
    attention_gain,
    query_weight,
    key_weight,
    value_weight,
    output_weight,
    lambda_vectors,
    head_gain,
    feedforward_gain,
    gate_weight,
    up_weight,
    down_weight,
    cotangent,
):
    rows, width = tokens.shape
    head_index = lax.axis_index("head")
    core = lax.axis_index("tensor")
    shard = query_weight.shape[0]
    qk_width = query_weight.shape[3]
    value_half = value_weight.shape[2]
    slots = rows * 8

    def in_order(mine, other):
        return jnp.where(core == 0, mine, other), jnp.where(core == 0, other, mine)

    own_slots = (
        (jnp.arange(4, dtype=jnp.int32) ^ head_index)[:, None] * (2 * rows)
        + core * rows
        + jnp.arange(rows, dtype=jnp.int32)[None, :]
    ).reshape(-1)
    segment_own, position_own = slot_layout(lengths, own_slots)
    valid = (segment_own[:rows] < 2).astype(jnp.float32)[:, None]
    half_width = qk_width // 2
    frequency = 10000.0 ** (-jnp.arange(half_width, dtype=jnp.float32) / half_width)

    def turn_tables(positions):
        angles = positions.astype(jnp.float32)[:, None] * frequency[None, :]
        cosine, sine = jnp.cos(angles), jnp.sin(angles)
        return jnp.concatenate([cosine, cosine], axis=1), jnp.concatenate([-sine, sine], axis=1)

    cosine, sine = turn_tables(position_own)
    cosine_all, sine_all = turn_tables(
        slot_layout(lengths, jnp.arange(slots, dtype=jnp.int32))[1]
    )
    own_head = head_index * 2 + core
    vectors = lax.dynamic_slice_in_dim(lambda_vectors, own_head, 1, 0)[0]
    first_exp = jnp.exp(jnp.sum(vectors[0] * vectors[1]))
    second_exp = jnp.exp(jnp.sum(vectors[2] * vectors[3]))
    lambda_value = first_exp - second_exp + lambda_base
    floats = jnp.stack(in_order(1.0, -lambda_value))
    ints = jnp.stack([head_index, core, lengths[0, 0], lengths[0, 0] + lengths[0, 1]])
    gain_own = rolled(
        lax.dynamic_slice_in_dim(head_gain, own_head, 1, 0), core * value_half
    ) * (1.0 - lambda_base)

    third = 3 * qk_width
    heads = [
        jnp.concatenate(
            [
                weight[:, place].reshape(shard, -1)
                for weight in (query_weight, key_weight, value_weight)
            ],
            axis=1,
        )
        for place in range(2)
    ]
    qkv_local = jnp.concatenate(in_order(*heads), axis=1)

    output_local = jnp.concatenate(in_order(output_weight[0], output_weight[1]), axis=0)

    tokens_wide = after(tokens, output_local).astype(jnp.float32)
    attention_scale = lax.rsqrt(jnp.mean(tokens_wide * tokens_wide, axis=-1, keepdims=True) + 1e-06)
    normed_own = (tokens_wide * attention_scale * attention_gain).astype(low)
    output_own = placed(line_gather(output_local))
    ffn_out_grad = valid * cotangent.astype(jnp.float32)
    ffn_out_grad_own = ffn_out_grad.astype(low)
    normed_near = [
        after(
            near,
            *(cosine, sine, cosine_all, sine_all),
            *(ffn_out_grad_own, ints, floats, gain_own, output_own),
        )
        for near in near_rows(normed_own)
    ]
    normed = group_rows(normed_own, normed_near)

    qkv_own = after(fsdp_gather(qkv_local, 0), normed)
    qkv_other = swap(qkv_own, "tensor", 1)
    gate_own = fsdp_gather(jnp.transpose(gate_weight), 1)
    up_own = fsdp_gather(jnp.transpose(up_weight), 1, normed)

    ffn_out_grad_own = after(ffn_out_grad_own, normed)
    ffn_out_grad_near = near_rows(ffn_out_grad_own)
    kept_first, sent_second = project(normed, qkv_own, cosine, sine)
    sent_first, kept_second = project(after(normed, kept_first), qkv_other, cosine, sine)
    ffn_out_grad_near = [after(near, sent_first) for near in ffn_out_grad_near]
    output_other = swap(after(output_own, sent_first), "tensor", 1)
    output_kept = jnp.concatenate([output_own[:value_half], output_other[value_half:]], axis=0)
    output_sent = jnp.concatenate([output_other[:value_half], output_own[value_half:]], axis=0)
    output_all = jnp.concatenate([output_kept, output_sent], axis=0)
    kept, sent, ordered, outs, log_totals = attention_forward(
        ints,
        floats,
        (after(kept_first, *ffn_out_grad_near), kept_second),
        (swap(sent_first, "tensor", 1), swap(sent_second, "tensor", 1)),
        gain_own,
    )
    head_out = jnp.concatenate([kept, swap(sent, "tensor", 1)], axis=1)

    third_out = [
        contract(head_out[start : start + rows // 2], output_all, 1, 0).astype(low)
        for start in (3 * rows, 7 * rows // 2)
    ]
    down_own = fsdp_gather(down_weight, 1, *third_out)
    nearer_out = contract(after(head_out, *third_out)[: 3 * rows], output_all, 1, 0).astype(low)
    attention_out, _ = group_reduce(
        nearer_out,
        rows,
        third_out,
        lambda *arrived: nearer_out[:rows],
    )
    residual = tokens_wide + summed([after(part, gate_own) for part in attention_out])
    ffn_scale = lax.rsqrt(jnp.mean(residual * residual, axis=-1, keepdims=True) + 1e-06)
    ffn_in_own = (residual * ffn_scale * feedforward_gain).astype(low)
    ffn_in_near = near_rows(ffn_in_own)
    ffn_in = group_rows(ffn_in_own, ffn_in_near)
    gate_own, up_own = after(gate_own, ffn_in), after(up_own, ffn_in)
    gate_other, up_other = swap(gate_own, "tensor", 1), swap(up_own, "tensor", 1)
    hidden_own, gate_factor_own, up_factor_own = gate_units(ffn_in, gate_own, up_own)
    hidden_other, gate_factor_other, up_factor_other = gate_units(
        after(ffn_in, hidden_own), gate_other, up_other
    )

    ffn_out_grad_all = group_rows(ffn_out_grad_own, ffn_out_grad_near, hidden_own)

    def weight_grad(own_side, other_side, right_side, *events):
        other = contract(other_side, right_side, 1, 0).astype(low)
        own = contract(after(own_side, other, *events), right_side, 1, 0)
        total = add_low(own, swap(other, "tensor", 1))
        return total, fsdp_reduce(total, 1)

    down_terms, down_grad = weight_grad(hidden_own, hidden_other, ffn_out_grad_all)
    down_own = after(down_own, down_terms)
    down_other = swap(down_own, "tensor", 1)
    gate_grad_own, up_grad_own = gate_grads(
        after(ffn_out_grad_all, down_terms), down_own, gate_factor_own, up_factor_own
    )
    gate_grad_other, up_grad_other = gate_grads(
        ffn_out_grad_all, down_other, gate_factor_other, up_factor_other
    )
    factors = [gate_grad_own, up_grad_own, gate_grad_other, up_grad_other]
    weights = [gate_own, up_own, gate_other, up_other]
    third_grad = sum_over_units(factors, weights, 3, 1, rows, 2)
    gate_other_part = contract(after(gate_grad_other, *third_grad), ffn_in, 1, 0).astype(low)
    (near_grad,) = sum_over_units(
        [after(factors[0], gate_other_part)] + factors[1:], weights, 1, 2, rows
    )
    own_grads, gate_sums = [], []

    def own_grad(*arrived):
        gate_terms = add_low(
            contract(after(gate_grad_own, near_grad, *arrived), ffn_in, 1, 0),
            swap(gate_other_part, "tensor", 1),
        )
        gate_sums.append(fsdp_reduce(gate_terms, 1))
        own_grads.extend(
            sum_over_units(
                [after(factors[0], gate_terms, down_grad, *arrived)] + factors[1:],
                weights,
                0,
                1,
                rows,
            )
        )
        return own_grads[0]

    ffn_in_sum, near_sent = group_reduce(near_grad, 0, third_grad, own_grad)
    gate_weight_grad = gate_sums[0]
    up_terms, up_weight_grad = weight_grad(
        after(up_grad_own, own_grads[0]), after(up_grad_other, own_grads[0], *near_sent), ffn_in
    )
    residual_grad, residual_grad_low, feedforward_gain_part = norm_back(
        [after(part, up_terms) for part in ffn_in_sum],
        residual,
        feedforward_gain,
        ffn_out_grad,
    )
    feedforward_gain_part = feedforward_gain_part[0]

    (ffn_out,) = sum_over_units(
        [after(hidden_own, residual_grad_low), hidden_other], [down_own, down_other], 0, 4, rows
    )
    residual_grad_near = [
        after(near, ffn_out, gate_weight_grad) for near in near_rows(residual_grad_low)
    ]
    attention_out_grad = group_rows(residual_grad_low, residual_grad_near)
    head_grad_sent = contract(attention_out_grad, output_sent, 1, 1).astype(low)
    head_grad_kept = contract(after(attention_out_grad, head_grad_sent), output_kept, 1, 1)
    output_terms = contract(head_out, after(attention_out_grad, head_grad_sent), 0, 0).astype(low)
    output_terms = [
        output_terms[place * value_half : (place + 1) * value_half] for place in range(4)
    ]
    output_sum = add_low(
        jnp.concatenate([output_terms[0], output_terms[3]], axis=0),
        swap(jnp.concatenate([output_terms[2], output_terms[1]], axis=0), "tensor", 1),
    )
    output_grad = fsdp_reduce(output_sum, 1)
    kept_first, kept_second, sent_first, sent_second, head_gain_part, lambda_part = (
        attention_backward(
            ints,
            floats,
            ordered,
            after(head_grad_kept.astype(low), output_sum, up_weight_grad),
            swap(head_grad_sent, "tensor", 1),
            outs,
            log_totals,
            gain_own,
            cosine_all,
            sine_all,
        )
    )

    ffn_arrived = []

    def ffn_own(*arrived):
        ffn_arrived.extend(arrived)
        return ffn_out[:rows]

    ffn_here, ffn_sent = group_reduce(
        ffn_out,
        rows,
        [
            after(ffn_out[start : start + rows // 2], attention_out_grad)
            for start in (3 * rows, 7 * rows // 2)
        ],
        ffn_own,
        (kept_first,),
    )

    received_first = swap(after(sent_first, *ffn_arrived, output_grad), "tensor", 1)
    received_second = swap(sent_second, "tensor", 1)
    others_second = contract(normed, kept_second, 0, 0).astype(low)
    others_first = contract(
        after(normed, others_second, *ffn_sent), received_first, 0, 0
    ).astype(low)
    parts = (kept_first, received_second, received_first, kept_second)
    own_first = add_low(
        contract(after(normed, others_first), kept_first, 0, 0), swap(others_first, "tensor", 1)
    )
    own_second = add_low(
        contract(after(normed, others_first), received_second, 0, 0),
        swap(others_second, "tensor", 1),
    )
    third_gain, *third_terms = project_back(
        (after(kept_first, own_first, own_second, output_grad),) + parts[1:],
        qkv_own,
        qkv_other,
        normed,
        3,
        1,
        rows,
        2,
    )
    qkv_weight_grad = in_order(
        fsdp_reduce(own_first, 0).astype(jnp.float32),
        fsdp_reduce(own_second, 0).astype(jnp.float32),
    )
    nearer_gain, nearer_terms = project_back(
        (after(kept_first, third_gain),) + parts[1:],
        qkv_own,
        qkv_other,
        normed,
        0,
        3,
        rows,
    )
    normed_grad, _ = group_reduce(
        nearer_terms,
        rows,
        [after(terms, *ffn_here) for terms in third_terms],
        lambda *arrived: nearer_terms[:rows],
    )
    output_grad, gate_weight_grad, up_weight_grad, down_grad = (
        after(grad, nearer_gain).astype(jnp.float32)
        for grad in (output_grad, gate_weight_grad, up_weight_grad, down_grad)
    )
    output_grad = jnp.stack(in_order(output_grad[:value_half], output_grad[value_half:]))
    attention_gain_part = (third_gain + nearer_gain)[0]
    ffn_here = [after(part, nearer_gain) for part in ffn_here]
    block_output = (valid * (residual + summed(ffn_here))).astype(low)
    tokens_grad, _, _ = norm_back(normed_grad, tokens, attention_gain, residual_grad)

    lambda_grad = -jnp.sum(lambda_part)
    vector_grads = lambda_grad * jnp.stack(
        [
            first_exp * vectors[1],
            first_exp * vectors[0],
            -second_exp * vectors[3],
            -second_exp * vectors[2],
        ]
    )
    lambda_full = lax.dynamic_update_slice(
        jnp.zeros(lambda_vectors.shape, jnp.float32), vector_grads[None], (own_head, 0, 0)
    )
    gain_full = lax.dynamic_update_slice(
        jnp.zeros(head_gain.shape, jnp.float32),
        rolled(head_gain_part, core * value_half),
        (own_head, 0),
    )
    small = total_over_all(
        jnp.concatenate(
            [
                attention_gain_part / attention_gain,
                feedforward_gain_part,
                lambda_full.reshape(-1),
                gain_full.reshape(-1),
            ]
        )
    )
    lambda_end = 2 * width + lambda_full.size
    return (
        block_output,
        tokens_grad,
        small[:width],
        *(
            jnp.stack(
                [part[:, kind * qk_width : (kind + 1) * qk_width] for part in qkv_weight_grad],
                axis=1,
            ).reshape(weight.shape)
            for kind, weight in enumerate((query_weight, key_weight, value_weight))
        ),
        output_grad.reshape(output_weight.shape),
        small[2 * width : lambda_end].reshape(lambda_full.shape),
        small[lambda_end:].reshape(gain_full.shape),
        small[width : 2 * width],
        jnp.transpose(gate_weight_grad),
        jnp.transpose(up_weight_grad),
        down_grad,
    )


def solution(mesh):
    placed = (
        P(("fsdp", "head", "tensor"), None),
        P("fsdp", None),
        P(),
        P("fsdp", "head", "tensor", None),
        P("fsdp", "head", "tensor", None),
        P("fsdp", "head", "tensor"),
        P("head", "tensor", "fsdp"),
        P(),
        P(),
        P(),
        P("fsdp", ("head", "tensor")),
        P("fsdp", ("head", "tensor")),
        P(("head", "tensor"), "fsdp"),
        P(("fsdp", "head", "tensor"), None),
    )
    return jax.shard_map(
        body,
        mesh=mesh,
        in_specs=placed,
        out_specs=(
            P(("fsdp", "head", "tensor"), None),
            P(("fsdp", "head", "tensor"), None),
            P(),
            P("fsdp", "head", "tensor", None),
            P("fsdp", "head", "tensor", None),
            P("fsdp", "head", "tensor"),
            P("head", "tensor", "fsdp"),
            P(),
            P(),
            P(),
            P("fsdp", ("head", "tensor")),
            P("fsdp", ("head", "tensor")),
            P(("head", "tensor"), "fsdp"),
        ),
        check_vma=False,
    )
```

```python
import functools

import jax
import jax.numpy as jnp
from jax import lax
from jax.experimental import pallas as pl
from jax.experimental.pallas import tpu as pltpu
from jax.sharding import PartitionSpec as P

lambda_base = 0.2
tile = 512
cost_share = 0.02
low = jnp.bfloat16


def contract(left_side, right_side, left_dim, right_dim):
    return lax.dot_general(
        left_side,
        right_side,
        (((left_dim,), (right_dim,)), ((), ())),
        preferred_element_type=jnp.float32,
    )


def after(values, *others):
    if not others:
        return values
    return lax.optimization_barrier((values, *others))[0]


def swap(values, axis, mask):
    size = lax.axis_size(axis)
    return lax.ppermute(values, axis, [(place, place ^ mask) for place in range(size)])


def fsdp_gather(own, axis, *others):
    return lax.all_gather(after(own, *others), "fsdp", axis=axis, tiled=True)


def fsdp_reduce(partial, axis):
    return lax.psum_scatter(partial, "fsdp", scatter_dimension=axis, tiled=True)


def shift(values, step):
    size = lax.axis_size("fsdp")
    return lax.ppermute(values, "fsdp", [(place, (place + step) % size) for place in range(size)])


def line_gather(own):
    size = lax.axis_size("fsdp")
    return [own] + [shift(own, -step) for step in range(1, size)]


def place_kernel(index, *refs):
    shards, out = refs[:-1], refs[-1]
    size, width = len(shards), shards[0].shape[1]
    for place, shard in enumerate(shards):
        to = lax.rem(index[0] + place, size) * width
        out[:, pl.ds(pl.multiple_of(to, width), width)] = shard[...]


def placed(shards):
    size = len(shards)
    rows, width = shards[0].shape
    vmem = pl.BlockSpec(memory_space=pltpu.VMEM)
    return pl.pallas_call(
        place_kernel,
        in_specs=[pl.BlockSpec(memory_space=pltpu.SMEM)] + [vmem] * size,
        out_specs=vmem,
        out_shape=jax.ShapeDtypeStruct((rows, size * width), low),
        cost_estimate=estimate(10**8),
        name="placed",
    )(lax.axis_index("fsdp")[None], *shards)


def add_low(left_side, right_side):
    return (left_side.astype(jnp.float32) + right_side.astype(jnp.float32)).astype(low)


def near_rows(own):
    return swap(own, "head", 1), swap(own, "head", 2)


def group_rows(own, near, *events):
    half = own.shape[0] // 2
    first, second = near
    third_low = swap(second[:half], "head", 1)
    third_high = swap(first[half:], "head", 2)
    far = [after(part, *events) for part in (third_low, third_high)]
    return jnp.concatenate([after(own, *events), first, second, *far], axis=0)


def join_kernel(start, near, to_first, to_second, first, second):
    rows = first.shape[0]
    half = rows // 2
    middle = start + rows
    first[:half] = near[start : start + half]
    first[half:] = add_low(near[start + half : middle], to_second[...])
    second[:half] = add_low(near[middle : middle + half], to_first[...])
    second[half:] = near[middle + half : middle + rows]


def group_reduce(near, start, halves, own_part, hold=()):
    half, width = halves[0].shape
    rows = 2 * half
    to_first = swap(halves[0], "head", 1)
    to_second = swap(halves[1], "head", 2)
    own = own_part(to_first, to_second)
    vmem = pl.BlockSpec(memory_space=pltpu.VMEM)
    first, second = pl.pallas_call(
        functools.partial(join_kernel, start),
        in_specs=[vmem] * 3,
        out_specs=[vmem] * 2,
        out_shape=[jax.ShapeDtypeStruct((rows, width), low)] * 2,
        compiler_params=pltpu.CompilerParams(vmem_limit_bytes=10 * 2**20),
        cost_estimate=estimate(10**9),
        name="join",
    )(after(near, *hold), to_first, to_second)
    from_first = swap(first, "head", 1)
    from_second = swap(second, "head", 2)
    return (own, from_first, from_second), (first, second)


def summed(parts):
    return sum(part.astype(jnp.float32) for part in parts)


def total_over_all(values):
    for axis in ("tensor", "fsdp", "head"):
        mask = 1
        while mask < lax.axis_size(axis):
            values = values + swap(values, axis, mask)
            mask *= 2
    return values


def rolled(values, start):
    twice = jnp.concatenate([values, values], axis=-1)
    return lax.dynamic_slice_in_dim(twice, start, values.shape[-1], values.ndim - 1)


def slot_layout(lengths, slots):
    first_end = lengths[0, 0]
    second_end = first_end + lengths[0, 1]
    segment = (slots >= first_end).astype(jnp.int32) + (slots >= second_end).astype(jnp.int32)
    start = jnp.where(segment == 0, 0, jnp.where(segment == 1, first_end, second_end))
    return segment, slots - start


def store_parts(values, outs):
    size = values.shape[0] // len(outs)
    for place, out in enumerate(outs):
        out[...] = values[place * size : (place + 1) * size].astype(out.dtype)


def kept_block(shape):
    return pl.BlockSpec(shape, lambda i: (0,) * len(shape), pipeline_mode=pl.Buffered(1))


def estimate(flops):
    return pl.CostEstimate(
        flops=int(flops * cost_share), bytes_accessed=2**20, transcendentals=0
    )


def store_block(block, ints, values, kept, sent, columns):
    rows = values.shape[0]
    at = pl.ds(pl.multiple_of(((block >> 1) ^ ints[0]) * rows, rows), rows)

    @pl.when(ints[1] == (block & 1))
    def _():
        kept[at, columns] = values

    @pl.when(ints[1] != (block & 1))
    def _():
        sent[at, columns] = values


def row_starts(slots, first_end, second_end):
    return jnp.where(slots >= second_end, second_end, jnp.where(slots >= first_end, first_end, 0))


def attention_forward_kernel(
    ints,
    floats,
    kept_first,
    kept_second,
    received_first,
    received_second,
    gain,
    head_out_kept,
    head_out_sent,
    ordered,
    outs,
    log_totals,
):
    head_index, core, first_end, second_end = (ints[place] for place in range(4))
    rows = kept_first.shape[0] // 4
    slots = 8 * rows
    width = gain.shape[1]
    e = width // 2
    for parts, other in (
        ((kept_first, kept_second), 0),
        ((received_first, received_second), 1),
    ):
        for j in range(4):
            block = (head_index ^ j) * 2 + (core ^ other)
            at = pl.ds(pl.multiple_of(block * rows, rows), rows)
            for m in range(2):
                for kind in range(3):
                    to = (2 * kind + m) * e
                    ordered[at, to : to + e] = parts[m][
                        j * rows : (j + 1) * rows, kind * e : (kind + 1) * e
                    ]
    for start in range(0, slots, tile):
        stop = start + tile
        row = start + lax.broadcasted_iota(jnp.int32, (tile, 1), 0)
        begin = row_starts(row, first_end, second_end)
        value = ordered[:stop, 4 * e :]
        results = []
        for m in range(2):
            scores = contract(
                ordered[start:stop, m * e : (m + 1) * e],
                ordered[:stop, (2 + m) * e : (3 + m) * e],
                1,
                1,
            )
            column = lax.broadcasted_iota(jnp.int32, (tile, stop), 1)
            scores = jnp.where((column >= begin) & (column <= row), scores, -1e30)
            row_max = jnp.max(scores, axis=1, keepdims=True)
            expanded = jnp.exp(scores - row_max)
            row_total = jnp.sum(expanded, axis=1, keepdims=True)
            result = contract(expanded.astype(low), value, 1, 0) / row_total
            outs[m, start:stop, :] = result
            results.append(result)
            wide = jnp.broadcast_to(row_max + jnp.log(row_total), (tile, 128))
            log_totals[m : m + 1, start:stop] = jnp.transpose(wide)[:1]
        mixed = results[0] * floats[0] + results[1] * floats[1]
        scale = lax.rsqrt(jnp.mean(mixed * mixed, axis=1, keepdims=True) + 1e-05)
        normed = (mixed * scale * gain[...]).astype(low)
        for piece in range(tile // rows):
            store_block(
                start // rows + piece,
                ints,
                normed[piece * rows : (piece + 1) * rows],
                head_out_kept,
                head_out_sent,
                slice(None),
            )


def attention_forward(ints, floats, kept, received, gain):
    rows = kept[0].shape[0] // 4
    slots = 8 * rows
    width = gain.shape[1]
    vmem = pl.BlockSpec(memory_space=pltpu.VMEM)
    smem = pl.BlockSpec(memory_space=pltpu.SMEM)
    return pl.pallas_call(
        attention_forward_kernel,
        in_specs=[smem, smem] + [vmem] * 5,
        out_specs=[vmem] * 5,
        out_shape=[
            jax.ShapeDtypeStruct((slots // 2, width), low),
            jax.ShapeDtypeStruct((slots // 2, width), low),
            jax.ShapeDtypeStruct((slots, 3 * width), low),
            jax.ShapeDtypeStruct((2, slots, width), jnp.float32),
            jax.ShapeDtypeStruct((2, slots), jnp.float32),
        ],
        compiler_params=pltpu.CompilerParams(vmem_limit_bytes=32 * 2**20),
        cost_estimate=estimate(5 * 10**9),
        name="attention_forward",
    )(ints, floats, *kept, *received, gain)


def attention_backward_kernel(
    ints,
    floats,
    ordered,
    grads_kept,
    grads_received,
    outs,
    log_totals,
    gain,
    cosine,
    sine,
    kept_first,
    kept_second,
    sent_first,
    sent_second,
    gain_grad,
    lambda_grad,
    map_grads,
    deltas,
    query_grads,
    key_grads,
    value_grads,
):
    head_index, core, first_end, second_end = (ints[place] for place in range(4))
    rows = grads_kept.shape[0] // 4
    slots = 8 * rows
    width = gain.shape[1]
    e = width // 2
    gain_total = jnp.zeros((1, width), jnp.float32)
    lambda_total = jnp.zeros((1, width), jnp.float32)
    for part, other in ((grads_kept, 0), (grads_received, 1)):
        for j in range(4):
            block = (head_index ^ j) * 2 + (core ^ other)
            at = pl.ds(pl.multiple_of(block * rows, rows), rows)
            grad = part[j * rows : (j + 1) * rows, :].astype(jnp.float32)
            first, second = outs[0, at, :], outs[1, at, :]
            mixed = first * floats[0] + second * floats[1]
            scale = lax.rsqrt(jnp.mean(mixed * mixed, axis=1, keepdims=True) + 1e-05)
            gain_total += jnp.sum(grad * (mixed * scale), axis=0, keepdims=True)
            weighted = grad * gain[...]
            inner = jnp.mean(weighted * mixed, axis=1, keepdims=True)
            mixed_grad = scale * weighted - mixed * (scale * scale * scale * inner)
            lambda_total += jnp.sum(
                mixed_grad * jnp.where(core == 1, first, second), axis=0, keepdims=True
            )
            for m, out in ((0, first), (1, second)):
                map_grad = (mixed_grad * floats[m]).astype(low)
                map_grads[m, at, :] = map_grad
                delta = jnp.sum(map_grad.astype(jnp.float32) * out, axis=1, keepdims=True)
                deltas[m, :, at] = jnp.transpose(jnp.broadcast_to(delta, (rows, 128)))[:8]
    gain_grad[...] = gain_total * (1.0 - lambda_base)
    lambda_grad[...] = lambda_total
    query_grads[...] = jnp.zeros_like(query_grads)

    def pair(key_start, query_start, diagonal):
        at_keys = pl.ds(key_start, tile)
        at_queries = pl.ds(query_start, tile)
        column = query_start + lax.broadcasted_iota(jnp.int32, (1, tile), 1)
        begin = row_starts(column, first_end, second_end)
        row = key_start + lax.broadcasted_iota(jnp.int32, (tile, tile), 0)
        allowed = row >= begin
        if diagonal:
            allowed = allowed & (row <= column)
        value = ordered[at_keys, 4 * e :]
        for m in range(2):
            query = ordered[at_queries, m * e : (m + 1) * e]
            key = ordered[at_keys, (2 + m) * e : (3 + m) * e]
            map_grad = map_grads[m, at_queries, :]
            scores = contract(key, query, 1, 1)
            probability = jnp.where(
                allowed, jnp.exp(scores - log_totals[m : m + 1, at_queries]), 0.0
            )
            prob_grad = contract(value, map_grad, 1, 1)
            score_grad = (probability * (prob_grad - deltas[m, 0:1, at_queries])).astype(low)
            value_term = contract(probability.astype(low), map_grad, 1, 0)
            key_term = contract(score_grad, query, 1, 0)
            query_grads[m, at_queries, :] += contract(score_grad, key, 0, 0)
            if diagonal:
                key_grads[m, at_keys, :] = key_term
                if m == 0:
                    value_grads[at_keys, :] = value_term
                else:
                    value_grads[at_keys, :] += value_term
            else:
                key_grads[m, at_keys, :] += key_term
                value_grads[at_keys, :] += value_term

    for key_start in range(0, slots, tile):
        pair(key_start, key_start, True)

        def step(at, carry, key_start=key_start):
            pair(key_start, pl.multiple_of(at * tile, tile), False)
            return carry

        lax.fori_loop(key_start // tile + 1, slots // tile, step, 0)

    def turn_back(values, at):
        return values * cosine[at, :] - pltpu.roll(values, e // 2, 1) * sine[at, :]

    for block in range(8):
        at = slice(block * rows, (block + 1) * rows)
        for m, kept, sent in ((0, kept_first, sent_first), (1, kept_second, sent_second)):
            query = (turn_back(query_grads[m, at, :], at) * e ** (-0.5)).astype(low)
            key = turn_back(key_grads[m, at, :], at).astype(low)
            value = value_grads[at, m * e : (m + 1) * e].astype(low)
            store_block(
                block, ints, jnp.concatenate([query, key, value], axis=1), kept, sent, slice(None)
            )


def attention_backward(
    ints, floats, ordered, grads_kept, grads_received, outs, log_totals, gain, cosine, sine
):
    slots, width = outs.shape[1:]
    vmem = pl.BlockSpec(memory_space=pltpu.VMEM)
    smem = pl.BlockSpec(memory_space=pltpu.SMEM)
    return pl.pallas_call(
        attention_backward_kernel,
        in_specs=[smem, smem] + [vmem] * 8,
        out_specs=[vmem] * 6,
        out_shape=[jax.ShapeDtypeStruct((slots // 2, 3 * width // 2), low)] * 4
        + [jax.ShapeDtypeStruct((1, width), jnp.float32)] * 2,
        scratch_shapes=[
            pltpu.VMEM((2, slots, width), low),
            pltpu.VMEM((2, 8, slots), jnp.float32),
            pltpu.VMEM((2, slots, width // 2), jnp.float32),
            pltpu.VMEM((2, slots, width // 2), jnp.float32),
            pltpu.VMEM((slots, width), jnp.float32),
        ],
        compiler_params=pltpu.CompilerParams(vmem_limit_bytes=40 * 2**20),
        cost_estimate=estimate(20 * 10**9),
        name="attention_backward",
    )(ints, floats, ordered, grads_kept, grads_received, outs, log_totals, gain, cosine, sine)


def norm_back_kernel(one, two, three, values, gain, added, out, out_low, gain_grad):
    wide = values[...].astype(jnp.float32)
    grad = (
        one[...].astype(jnp.float32) + two[...].astype(jnp.float32) + three[...].astype(jnp.float32)
    )
    scale = lax.rsqrt(jnp.mean(wide * wide, axis=1, keepdims=True) + 1e-06)
    gained = grad * gain[...]
    inner = jnp.mean(gained * wide, axis=1, keepdims=True)
    result = added[...] + scale * gained - wide * (scale * scale * scale * inner)
    out[...] = result
    out_low[...] = result.astype(low)

    @pl.when(pl.program_id(0) == 0)
    def _():
        gain_grad[...] = jnp.zeros_like(gain_grad)

    gain_grad[...] += jnp.sum(grad * (wide * scale), axis=0, keepdims=True)


def norm_back(parts, values, gain, added):
    rows, width = values.shape
    block = rows // 4
    down = pl.BlockSpec((block, width), lambda i: (i, 0))
    once = pl.BlockSpec((1, width), lambda i: (0, 0))
    return pl.pallas_call(
        norm_back_kernel,
        grid=(4,),
        in_specs=[down] * 4 + [once, down],
        out_specs=[down, down, once],
        out_shape=[
            jax.ShapeDtypeStruct((rows, width), jnp.float32),
            jax.ShapeDtypeStruct((rows, width), low),
            jax.ShapeDtypeStruct((1, width), jnp.float32),
        ],
        compiler_params=pltpu.CompilerParams(vmem_limit_bytes=12 * 2**20),
        cost_estimate=estimate(10**9),
        name="norm_back",
    )(*parts, values, gain[None], added)


def project_kernel(inputs, weight, cosine, sine, first, second):
    e = cosine.shape[1]
    product = contract(inputs[...], weight[...], 1, 0)

    def turned(start):
        part = product[:, start : start + e]
        return part * cosine[...] + pltpu.roll(part, e // 2, 1) * sine[...]

    for out, start in ((first, 0), (second, 3 * e)):
        out[:, :e] = (turned(start) * e ** (-0.5)).astype(low)
        out[:, e : 2 * e] = turned(start + e).astype(low)
        out[:, 2 * e :] = product[:, start + 2 * e : start + 3 * e].astype(low)


def project(inputs, weight, cosine, sine):
    slots, width = inputs.shape
    columns = weight.shape[1]
    block = slots // 4
    down = lambda size: pl.BlockSpec((block, size), lambda i: (i, 0))
    return pl.pallas_call(
        project_kernel,
        grid=(4,),
        in_specs=[
            down(width),
            kept_block((width, columns)),
            down(cosine.shape[1]),
            down(cosine.shape[1]),
        ],
        out_specs=[down(columns // 2)] * 2,
        out_shape=[jax.ShapeDtypeStruct((slots, columns // 2), low)] * 2,
        compiler_params=pltpu.CompilerParams(vmem_limit_bytes=14 * 2**20),
        cost_estimate=estimate(2 * slots * width * columns),
        name="project",
    )(inputs, weight, cosine, sine)


def project_back_kernel(one, two, three, four, own, other, normed, gain, *outs):
    half = one.shape[1]
    total = contract(one[...], own[:, :half], 1, 1)
    total += contract(two[...], own[:, half:], 1, 1)
    total += contract(three[...], other[:, :half], 1, 1)
    total += contract(four[...], other[:, half:], 1, 1)
    store_parts(total, outs)
    part = jnp.sum(total * normed[...].astype(jnp.float32), axis=0, keepdims=True)

    @pl.when(pl.program_id(0) == 0)
    def _():
        gain[...] = jnp.zeros_like(gain)

    gain[...] += part


def project_back(grads, own, other, normed, first, count, rows, parts=1):
    width, columns = own.shape
    down = lambda size: pl.BlockSpec((rows, size), lambda i: (first + i, 0))
    whole = kept_block((width, columns))
    return pl.pallas_call(
        project_back_kernel,
        grid=(count,),
        in_specs=[down(columns // 2)] * 4 + [whole, whole, down(width)],
        out_specs=[pl.BlockSpec((1, width), lambda i: (0, 0))]
        + [pl.BlockSpec((rows // parts, width), lambda i: (i, 0))] * parts,
        out_shape=[jax.ShapeDtypeStruct((1, width), jnp.float32)]
        + [jax.ShapeDtypeStruct((count * rows // parts, width), low)] * parts,
        compiler_params=pltpu.CompilerParams(vmem_limit_bytes=22 * 2**20),
        cost_estimate=estimate(4 * count * rows * width * columns),
        name="project_back",
    )(*grads, own, other, normed)


def gate_kernel(inputs, gate, up, hidden, gate_factor, up_factor):
    gate_pre = contract(gate[...], inputs[...], 1, 1)
    upward = contract(up[...], inputs[...], 1, 1)
    sigmoid = 1.0 / (1.0 + jnp.exp(-gate_pre))
    silu = gate_pre * sigmoid
    hidden[...] = (silu * upward).astype(low)
    gate_factor[...] = (upward * (sigmoid * (1.0 + gate_pre * (1.0 - sigmoid)))).astype(low)
    up_factor[...] = silu.astype(low)


def gate_units(inputs, gate, up):
    slots, width = inputs.shape
    units = gate.shape[0]
    block = slots // 4
    whole = kept_block((units, width))
    across = pl.BlockSpec((units, block), lambda i: (0, i))
    return pl.pallas_call(
        gate_kernel,
        grid=(4,),
        in_specs=[pl.BlockSpec((block, width), lambda i: (i, 0)), whole, whole],
        out_specs=[across] * 3,
        out_shape=[jax.ShapeDtypeStruct((units, slots), low)] * 3,
        compiler_params=pltpu.CompilerParams(vmem_limit_bytes=22 * 2**20),
        cost_estimate=estimate(4 * slots * width * units),
        name="gate_units",
    )(inputs, gate, up)


def gate_grad_kernel(grads, down, gate_factor, up_factor, gate_grad, up_grad):
    hidden_grad = contract(down[...], grads[...], 1, 1)
    gate_grad[...] = (hidden_grad * gate_factor[...].astype(jnp.float32)).astype(low)
    up_grad[...] = (hidden_grad * up_factor[...].astype(jnp.float32)).astype(low)


def gate_grads(grads, down, gate_factor, up_factor):
    slots, width = grads.shape
    units = down.shape[0]
    block = slots // 4
    across = pl.BlockSpec((units, block), lambda i: (0, i))
    return pl.pallas_call(
        gate_grad_kernel,
        grid=(4,),
        in_specs=[
            pl.BlockSpec((block, width), lambda i: (i, 0)),
            kept_block((units, width)),
            across,
            across,
        ],
        out_specs=[across] * 2,
        out_shape=[jax.ShapeDtypeStruct((units, slots), low)] * 2,
        compiler_params=pltpu.CompilerParams(vmem_limit_bytes=16 * 2**20),
        cost_estimate=estimate(2 * slots * width * units),
        name="gate_grads",
    )(grads, down, gate_factor, up_factor)


def sum_kernel(terms, *refs):
    total = contract(refs[0][...], refs[terms][...], 0, 0)
    for place in range(1, terms):
        total += contract(refs[place][...], refs[terms + place][...], 0, 0)
    store_parts(total, refs[2 * terms :])


def sum_over_units(factors, weights, first, count, rows, parts=1):
    units, width = weights[0].shape
    terms = len(factors)
    return pl.pallas_call(
        functools.partial(sum_kernel, terms),
        grid=(count,),
        in_specs=[pl.BlockSpec((units, rows), lambda i: (0, first + i))] * terms
        + [kept_block((units, width))] * terms,
        out_specs=[pl.BlockSpec((rows // parts, width), lambda i: (i, 0))] * parts,
        out_shape=[jax.ShapeDtypeStruct((count * rows // parts, width), low)] * parts,
        compiler_params=pltpu.CompilerParams(vmem_limit_bytes=26 * 2**20),
        cost_estimate=estimate(2 * count * rows * width * units * terms),
        name="sum_over_units",
    )(*factors, *weights)


def body(
    tokens,
    lengths,
    attention_gain,
    query_weight,
    key_weight,
    value_weight,
    output_weight,
    lambda_vectors,
    head_gain,
    feedforward_gain,
    gate_weight,
    up_weight,
    down_weight,
    cotangent,
):
    rows, width = tokens.shape
    head_index = lax.axis_index("head")
    core = lax.axis_index("tensor")
    shard = query_weight.shape[0]
    qk_width = query_weight.shape[3]
    value_half = value_weight.shape[2]
    slots = rows * 8

    def in_order(mine, other):
        return jnp.where(core == 0, mine, other), jnp.where(core == 0, other, mine)

    own_slots = (
        (jnp.arange(4, dtype=jnp.int32) ^ head_index)[:, None] * (2 * rows)
        + core * rows
        + jnp.arange(rows, dtype=jnp.int32)[None, :]
    ).reshape(-1)
    segment_own, position_own = slot_layout(lengths, own_slots)
    valid = (segment_own[:rows] < 2).astype(jnp.float32)[:, None]
    half_width = qk_width // 2
    frequency = 10000.0 ** (-jnp.arange(half_width, dtype=jnp.float32) / half_width)

    def turn_tables(positions):
        angles = positions.astype(jnp.float32)[:, None] * frequency[None, :]
        cosine, sine = jnp.cos(angles), jnp.sin(angles)
        return jnp.concatenate([cosine, cosine], axis=1), jnp.concatenate([-sine, sine], axis=1)

    cosine, sine = turn_tables(position_own)
    cosine_all, sine_all = turn_tables(
        slot_layout(lengths, jnp.arange(slots, dtype=jnp.int32))[1]
    )
    own_head = head_index * 2 + core
    vectors = lax.dynamic_slice_in_dim(lambda_vectors, own_head, 1, 0)[0]
    first_exp = jnp.exp(jnp.sum(vectors[0] * vectors[1]))
    second_exp = jnp.exp(jnp.sum(vectors[2] * vectors[3]))
    lambda_value = first_exp - second_exp + lambda_base
    floats = jnp.stack(in_order(1.0, -lambda_value))
    ints = jnp.stack([head_index, core, lengths[0, 0], lengths[0, 0] + lengths[0, 1]])
    gain_own = rolled(
        lax.dynamic_slice_in_dim(head_gain, own_head, 1, 0), core * value_half
    ) * (1.0 - lambda_base)

    third = 3 * qk_width
    heads = [
        jnp.concatenate(
            [
                weight[:, place].reshape(shard, -1)
                for weight in (query_weight, key_weight, value_weight)
            ],
            axis=1,
        )
        for place in range(2)
    ]
    qkv_local = jnp.concatenate(in_order(*heads), axis=1)

    output_local = jnp.concatenate(in_order(output_weight[0], output_weight[1]), axis=0)

    tokens_wide = after(tokens, output_local).astype(jnp.float32)
    attention_scale = lax.rsqrt(jnp.mean(tokens_wide * tokens_wide, axis=-1, keepdims=True) + 1e-06)
    normed_own = (tokens_wide * attention_scale * attention_gain).astype(low)
    output_own = placed(line_gather(output_local))
    ffn_out_grad = valid * cotangent.astype(jnp.float32)
    ffn_out_grad_own = ffn_out_grad.astype(low)
    normed_near = [
        after(
            near,
            *(cosine, sine, cosine_all, sine_all),
            *(ffn_out_grad_own, ints, floats, gain_own, output_own),
        )
        for near in near_rows(normed_own)
    ]
    normed = group_rows(normed_own, normed_near)

    qkv_own = after(fsdp_gather(qkv_local, 0), normed)
    qkv_other = swap(qkv_own, "tensor", 1)
    gate_own = fsdp_gather(jnp.transpose(gate_weight), 1)
    up_own = fsdp_gather(jnp.transpose(up_weight), 1, normed)

    ffn_out_grad_own = after(ffn_out_grad_own, normed)
    ffn_out_grad_near = near_rows(ffn_out_grad_own)
    kept_first, sent_second = project(normed, qkv_own, cosine, sine)
    sent_first, kept_second = project(after(normed, kept_first), qkv_other, cosine, sine)
    output_other = swap(after(output_own, sent_first), "tensor", 1)
    output_kept = jnp.concatenate([output_own[:value_half], output_other[value_half:]], axis=0)
    output_sent = jnp.concatenate([output_other[:value_half], output_own[value_half:]], axis=0)
    output_all = jnp.concatenate([output_kept, output_sent], axis=0)
    kept, sent, ordered, outs, log_totals = attention_forward(
        ints,
        floats,
        (kept_first, kept_second),
        (swap(sent_first, "tensor", 1), swap(sent_second, "tensor", 1)),
        gain_own,
    )
    sent = after(sent, *ffn_out_grad_near)
    head_out = jnp.concatenate([kept, swap(sent, "tensor", 1)], axis=1)

    third_out = [
        contract(head_out[start : start + rows // 2], output_all, 1, 0).astype(low)
        for start in (3 * rows, 7 * rows // 2)
    ]
    down_own = fsdp_gather(down_weight, 1, *third_out)
    nearer_out = contract(after(head_out, *third_out)[: 3 * rows], output_all, 1, 0).astype(low)
    attention_out, _ = group_reduce(
        nearer_out,
        rows,
        third_out,
        lambda *arrived: nearer_out[:rows],
    )
    residual = tokens_wide + summed([after(part, gate_own) for part in attention_out])
    ffn_scale = lax.rsqrt(jnp.mean(residual * residual, axis=-1, keepdims=True) + 1e-06)
    ffn_in_own = (residual * ffn_scale * feedforward_gain).astype(low)
    ffn_in_near = near_rows(ffn_in_own)
    ffn_in = group_rows(ffn_in_own, ffn_in_near)
    gate_own, up_own = after(gate_own, ffn_in), after(up_own, ffn_in)
    gate_other, up_other = swap(gate_own, "tensor", 1), swap(up_own, "tensor", 1)
    hidden_own, gate_factor_own, up_factor_own = gate_units(ffn_in, gate_own, up_own)
    hidden_other, gate_factor_other, up_factor_other = gate_units(
        after(ffn_in, hidden_own), gate_other, up_other
    )

    ffn_out_grad_near = [after(near, hidden_own) for near in ffn_out_grad_near]
    ffn_out_grad_all = group_rows(ffn_out_grad_own, ffn_out_grad_near, hidden_own)

    def weight_grad(own_side, other_side, right_side, *events):
        other = contract(other_side, right_side, 1, 0).astype(low)
        own = contract(after(own_side, other, *events), right_side, 1, 0)
        total = add_low(own, swap(other, "tensor", 1))
        return total, fsdp_reduce(total, 1)

    down_terms, down_grad = weight_grad(hidden_own, hidden_other, ffn_out_grad_all)
    down_own = after(down_own, down_terms)
    down_other = swap(down_own, "tensor", 1)
    gate_grad_own, up_grad_own = gate_grads(
        after(ffn_out_grad_all, down_terms), down_own, gate_factor_own, up_factor_own
    )
    gate_grad_other, up_grad_other = gate_grads(
        ffn_out_grad_all, down_other, gate_factor_other, up_factor_other
    )
    factors = [gate_grad_own, up_grad_own, gate_grad_other, up_grad_other]
    weights = [gate_own, up_own, gate_other, up_other]
    third_grad = sum_over_units(factors, weights, 3, 1, rows, 2)
    gate_other_part = contract(after(gate_grad_other, *third_grad), ffn_in, 1, 0).astype(low)
    (near_grad,) = sum_over_units(
        [after(factors[0], gate_other_part)] + factors[1:], weights, 1, 2, rows
    )
    own_grads, gate_sums = [], []

    def own_grad(*arrived):
        gate_terms = add_low(
            contract(after(gate_grad_own, near_grad, *arrived), ffn_in, 1, 0),
            swap(gate_other_part, "tensor", 1),
        )
        gate_sums.append(fsdp_reduce(gate_terms, 1))
        own_grads.extend(
            sum_over_units(
                [after(factors[0], gate_terms, down_grad, *arrived)] + factors[1:],
                weights,
                0,
                1,
                rows,
            )
        )
        return own_grads[0]

    ffn_in_sum, near_sent = group_reduce(near_grad, 0, third_grad, own_grad)
    gate_weight_grad = gate_sums[0]
    up_terms, up_weight_grad = weight_grad(
        after(up_grad_own, own_grads[0]), after(up_grad_other, own_grads[0], *near_sent), ffn_in
    )
    residual_grad, residual_grad_low, feedforward_gain_part = norm_back(
        [after(part, up_terms) for part in ffn_in_sum],
        residual,
        feedforward_gain,
        ffn_out_grad,
    )
    feedforward_gain_part = feedforward_gain_part[0]

    (ffn_out,) = sum_over_units(
        [after(hidden_own, residual_grad_low), hidden_other], [down_own, down_other], 0, 4, rows
    )
    residual_grad_near = [
        after(near, ffn_out, gate_weight_grad) for near in near_rows(residual_grad_low)
    ]
    attention_out_grad = group_rows(residual_grad_low, residual_grad_near)
    head_grad_sent = contract(attention_out_grad, output_sent, 1, 1).astype(low)
    head_grad_kept = contract(after(attention_out_grad, head_grad_sent), output_kept, 1, 1)
    output_terms = contract(head_out, after(attention_out_grad, head_grad_sent), 0, 0).astype(low)
    output_terms = [
        output_terms[place * value_half : (place + 1) * value_half] for place in range(4)
    ]
    output_sum = add_low(
        jnp.concatenate([output_terms[0], output_terms[3]], axis=0),
        swap(jnp.concatenate([output_terms[2], output_terms[1]], axis=0), "tensor", 1),
    )
    output_grad = fsdp_reduce(output_sum, 1)
    kept_first, kept_second, sent_first, sent_second, head_gain_part, lambda_part = (
        attention_backward(
            ints,
            floats,
            ordered,
            after(head_grad_kept.astype(low), output_sum, up_weight_grad),
            swap(head_grad_sent, "tensor", 1),
            outs,
            log_totals,
            gain_own,
            cosine_all,
            sine_all,
        )
    )

    ffn_arrived = []

    def ffn_own(*arrived):
        ffn_arrived.extend(arrived)
        return ffn_out[:rows]

    ffn_here, ffn_sent = group_reduce(
        ffn_out,
        rows,
        [
            after(ffn_out[start : start + rows // 2], attention_out_grad)
            for start in (3 * rows, 7 * rows // 2)
        ],
        ffn_own,
        (kept_first,),
    )

    received_first = swap(after(sent_first, *ffn_arrived, output_grad), "tensor", 1)
    received_second = swap(sent_second, "tensor", 1)
    others_second = contract(normed, kept_second, 0, 0).astype(low)
    others_first = contract(
        after(normed, others_second, *ffn_sent), received_first, 0, 0
    ).astype(low)
    parts = (kept_first, received_second, received_first, kept_second)
    own_first = add_low(
        contract(after(normed, others_first), kept_first, 0, 0), swap(others_first, "tensor", 1)
    )
    own_second = add_low(
        contract(after(normed, others_first), received_second, 0, 0),
        swap(others_second, "tensor", 1),
    )
    third_gain, *third_terms = project_back(
        (after(kept_first, own_first, own_second, output_grad),) + parts[1:],
        qkv_own,
        qkv_other,
        normed,
        3,
        1,
        rows,
        2,
    )
    qkv_weight_grad = in_order(
        fsdp_reduce(own_first, 0).astype(jnp.float32),
        fsdp_reduce(own_second, 0).astype(jnp.float32),
    )
    nearer_gain, nearer_terms = project_back(
        (after(kept_first, third_gain),) + parts[1:],
        qkv_own,
        qkv_other,
        normed,
        0,
        3,
        rows,
    )
    normed_grad, _ = group_reduce(
        nearer_terms,
        rows,
        [after(terms, *ffn_here) for terms in third_terms],
        lambda *arrived: nearer_terms[:rows],
    )
    output_grad, gate_weight_grad, up_weight_grad, down_grad = (
        after(grad, nearer_gain).astype(jnp.float32)
        for grad in (output_grad, gate_weight_grad, up_weight_grad, down_grad)
    )
    output_grad = jnp.stack(in_order(output_grad[:value_half], output_grad[value_half:]))
    attention_gain_part = (third_gain + nearer_gain)[0]
    ffn_here = [after(part, nearer_gain) for part in ffn_here]
    block_output = (valid * (residual + summed(ffn_here))).astype(low)
    tokens_grad, _, _ = norm_back(normed_grad, tokens, attention_gain, residual_grad)

    lambda_grad = -jnp.sum(lambda_part)
    vector_grads = lambda_grad * jnp.stack(
        [
            first_exp * vectors[1],
            first_exp * vectors[0],
            -second_exp * vectors[3],
            -second_exp * vectors[2],
        ]
    )
    lambda_full = lax.dynamic_update_slice(
        jnp.zeros(lambda_vectors.shape, jnp.float32), vector_grads[None], (own_head, 0, 0)
    )
    gain_full = lax.dynamic_update_slice(
        jnp.zeros(head_gain.shape, jnp.float32),
        rolled(head_gain_part, core * value_half),
        (own_head, 0),
    )
    small = total_over_all(
        jnp.concatenate(
            [
                attention_gain_part / attention_gain,
                feedforward_gain_part,
                lambda_full.reshape(-1),
                gain_full.reshape(-1),
            ]
        )
    )
    lambda_end = 2 * width + lambda_full.size
    return (
        block_output,
        tokens_grad,
        small[:width],
        *(
            jnp.stack(
                [part[:, kind * qk_width : (kind + 1) * qk_width] for part in qkv_weight_grad],
                axis=1,
            ).reshape(weight.shape)
            for kind, weight in enumerate((query_weight, key_weight, value_weight))
        ),
        output_grad.reshape(output_weight.shape),
        small[2 * width : lambda_end].reshape(lambda_full.shape),
        small[lambda_end:].reshape(gain_full.shape),
        small[width : 2 * width],
        jnp.transpose(gate_weight_grad),
        jnp.transpose(up_weight_grad),
        down_grad,
    )


def solution(mesh):
    placed = (
        P(("fsdp", "head", "tensor"), None),
        P("fsdp", None),
        P(),
        P("fsdp", "head", "tensor", None),
        P("fsdp", "head", "tensor", None),
        P("fsdp", "head", "tensor"),
        P("head", "tensor", "fsdp"),
        P(),
        P(),
        P(),
        P("fsdp", ("head", "tensor")),
        P("fsdp", ("head", "tensor")),
        P(("head", "tensor"), "fsdp"),
        P(("fsdp", "head", "tensor"), None),
    )
    return jax.shard_map(
        body,
        mesh=mesh,
        in_specs=placed,
        out_specs=(
            P(("fsdp", "head", "tensor"), None),
            P(("fsdp", "head", "tensor"), None),
            P(),
            P("fsdp", "head", "tensor", None),
            P("fsdp", "head", "tensor", None),
            P("fsdp", "head", "tensor"),
            P("head", "tensor", "fsdp"),
            P(),
            P(),
            P(),
            P("fsdp", ("head", "tensor")),
            P("fsdp", ("head", "tensor")),
            P(("head", "tensor"), "fsdp"),
        ),
        check_vma=False,
    )
```
